128 devices in a mesh: scan: 32 (over x, z, core), tile: 4 (over y).
Axes of the slice: x: 4, y: 4, z: 4, core: 2. Of those that a mesh axis runs over, the one named last changes fastest.
Arguments:
- object_slab: float32 [2, 3072, 24576], P(None, 'tile', 'scan'), may hold values from -6 to 6
- probe_field: float32 [2, 512, 512], replicated, may hold values from -3 to 3
- intensities: bfloat16 [32, 4, 6, 512, 512], P('scan', 'tile'), may hold values from 0 to 2
- offsets: int32 [32, 4, 6, 2], P('scan', 'tile'), may hold values from 0 to 767
- live_count: int32 [32, 4], P(None, 'tile'), may hold values from 1 to 6, as said below
Outputs:
- object_grad: float32 [2, 3072, 24576], P(None, 'tile', 'scan')
The draws below stay inside these ranges and needn't reach their ends.
Inputs may be any that keep to these rules, and one draw needn't show every extreme that they name: The first live_count slots of a group hold its measured positions; some group has all 6 slots live.
All inputs are finite; a program needn't handle non-finite values.
Results may differ from the reference program's by a relative error of at most 0.014.
Values may be sent and summed in bfloat16 or wider, within the bound.
No kernel may reach another device: no remote copies, remote signals or barrier semaphores. Data moves between devices by JAX's collectives and lax.ppermute only.
A program may use at most 128 MiB of HBM per device.

```python
import math
import jax
import jax.numpy as jnp
from jax import lax

W = 512
TILE = 768
SLOTS = 6
OBJ_Y = 3072
OBJ_X = 24576
N_SCAN = 32
N_TILE = 4


def draw_live_count(key, part):
    key_side, key_high, key_low, key_full = jax.random.split(key, 4)
    shape = (N_SCAN // 2, N_TILE)
    busy_left = jax.random.randint(key_side, shape, 0, 2)
    high = SLOTS - jax.random.randint(key_high, shape, 0, 2)
    low = 1 + jax.random.randint(key_low, shape, 0, max(SLOTS // 4, 1))
    left = jnp.where(busy_left == 1, high, low)
    right = jnp.where(busy_left == 1, low, high)
    counts = jnp.concatenate([left, right], axis=0)
    full_at = jax.random.randint(key_full, (), 0, N_SCAN * N_TILE)
    flat_ids = jnp.arange(N_SCAN * N_TILE, dtype=jnp.int32).reshape((N_SCAN, N_TILE))
    counts = jnp.where(flat_ids == full_at, SLOTS, counts)
    return counts.astype(jnp.int32)


def with_ends(drawn, stream_key, least, largest):
    shape = drawn.shape
    spot = [jax.random.randint(jax.random.fold_in(stream_key, axis), (), 0, shape[axis]) for axis in range(len(shape))]
    drawn = drawn.at[tuple(spot)].set(least)
    longest = shape.index(max(shape))
    spot[longest] = (spot[longest] + 1) % shape[longest]
    return drawn.at[tuple(spot)].set(largest)


def shard_levels(own_key, extent, cuts, low, high):
    def one(position, shards_of):
        draws = jax.random.uniform(jax.random.fold_in(jax.random.fold_in(own_key, 6), position), (shards_of,), jnp.float32, low / len(cuts), high / len(cuts))
        return jnp.repeat(jnp.exp(draws), extent[position] // shards_of).reshape((-1,) + (1,) * (len(extent) - position - 1))

    gain = one(*cuts[0])
    for cut in cuts[1:]:
        gain = gain * one(*cut)
    return gain


def normal_values(own_key, extent, width, most, pieces=(), held_as=jnp.bfloat16):
    result = width * jax.random.normal(own_key, extent, jnp.float32)
    if pieces:
        result = result * shard_levels(own_key, extent, pieces, -0.22, 0.18)
    return jnp.clip(result, -most, most).astype(held_as)


def setup_inputs(seed: int = 0) -> dict:
    arg_keys = jax.random.split(jax.random.key(seed), 6)
    return {
        "object_slab": normal_values(arg_keys[0], (2, OBJ_Y, OBJ_X), 1.0, 6.0, ((1, 4), (2, 32)), jnp.float32),
        "probe_field": normal_values(arg_keys[1], (2, W, W), 0.5, 3.0, (), jnp.float32),
        "intensities": jnp.clip(2.0 * jax.random.uniform(arg_keys[2], (N_SCAN, N_TILE, SLOTS, W, W), jnp.float32) ** shard_levels(arg_keys[2], (N_SCAN, N_TILE, SLOTS, W, W), ((0, 32), (1, 4)), -0.2, 0.2), 0.0, 2.0).astype(jnp.bfloat16),
        "offsets": with_ends(jax.random.randint(arg_keys[3], (N_SCAN, N_TILE, SLOTS, 2), 0, TILE), jax.random.fold_in(arg_keys[3], 1), 0, TILE - 1).astype(jnp.int32),
        "live_count": draw_live_count(jax.random.fold_in(arg_keys[5], 71), 0),
    }


def fourier_tables(side_len):
    across = jnp.arange(side_len, dtype=jnp.int32)
    phase = (across[:, None] * across[None, :] % side_len).astype(jnp.float32) * (2.0 * math.pi / side_len)
    factor = 1.0 / math.sqrt(side_len)
    return ((jnp.cos(phase) * factor).astype(jnp.bfloat16), (-jnp.sin(phase) * factor).astype(jnp.bfloat16))

def left_apply(table_re, table_im, part_re, part_im):
    side_len = part_re.shape[-1]
    joined = jnp.concatenate([part_re, part_im], axis=-1).astype(jnp.float32)
    with_re = jnp.einsum('ij,bjk->bik', table_re.astype(jnp.float32), joined)
    with_im = jnp.einsum('ij,bjk->bik', table_im.astype(jnp.float32), joined)
    return (with_re[..., :side_len] - with_im[..., side_len:], with_re[..., side_len:] + with_im[..., :side_len])

def right_apply(part_re, part_im, table_re, table_im):
    side_len = part_re.shape[-1]
    joined = jnp.concatenate([part_re, part_im], axis=-2).astype(jnp.float32)
    with_re = jnp.einsum('bij,jk->bik', joined, table_re.astype(jnp.float32))
    with_im = jnp.einsum('bij,jk->bik', joined, table_im.astype(jnp.float32))
    return (with_re[:, :side_len] - with_im[:, side_len:], with_im[:, :side_len] + with_re[:, side_len:])

def transform(exit_waves, measured, tables):
    table_re, table_im = tables
    conj_im = -table_im
    half_re, half_im = left_apply(table_re, table_im, exit_waves[:, 0], exit_waves[:, 1])
    half_re = half_re.astype(jnp.bfloat16)
    half_im = half_im.astype(jnp.bfloat16)
    far_re, far_im = right_apply(half_re, half_im, table_re, table_im)
    misfit = far_re * far_re + far_im * far_im - measured.astype(jnp.float32)
    mis_re = (misfit * far_re).astype(jnp.bfloat16)
    mis_im = (misfit * far_im).astype(jnp.bfloat16)
    back_re, back_im = left_apply(table_re, conj_im, mis_re, mis_im)
    back_re = back_re.astype(jnp.bfloat16)
    back_im = back_im.astype(jnp.bfloat16)
    grad_re, grad_im = right_apply(back_re, back_im, table_re, conj_im)
    return jnp.stack([grad_re, grad_im], axis=1).astype(jnp.bfloat16)

def exit_wave(probe_field, patches):
    probe_re = probe_field[0]
    probe_im = probe_field[1]
    real_part = probe_re * patches[:, 0] - probe_im * patches[:, 1]
    imag_part = probe_re * patches[:, 1] + probe_im * patches[:, 0]
    return jnp.stack([real_part, imag_part], axis=1).astype(jnp.bfloat16)

def object_gradient(probe_field, wave_grads):
    probe_re = probe_field[0]
    probe_im = probe_field[1]
    grad_re = wave_grads[:, 0].astype(jnp.float32)
    grad_im = wave_grads[:, 1].astype(jnp.float32)
    real_part = probe_re * grad_re + probe_im * grad_im
    imag_part = probe_re * grad_im - probe_im * grad_re
    return jnp.stack([real_part, imag_part], axis=1)

def reference(object_slab, probe_field, intensities, offsets, live_count):
    side_len = probe_field.shape[-1]
    grid_rows = object_slab.shape[1]
    grid_cols = object_slab.shape[2]
    padded = jnp.pad(object_slab, ((0, 0), (0, side_len), (0, side_len)))
    groups = N_SCAN * N_TILE
    flat_measured = intensities.reshape(groups, SLOTS, side_len, side_len)
    flat_shifts = offsets.reshape(groups, SLOTS, 2)
    flat_live = live_count.reshape(groups)
    group_ids = jnp.arange(groups, dtype=jnp.int32)
    scan_ids = group_ids // N_TILE
    tile_ids = group_ids % N_TILE
    zero_index = jnp.zeros((), jnp.int32)
    tables = fourier_tables(side_len)

    def one_group(gradient_sum, inputs):
        measured, shifts, live_total, scan_id, tile_id = inputs
        row_start = (tile_id * TILE + shifts[:, 0]).astype(jnp.int32)
        col_start = (scan_id * TILE + shifts[:, 1]).astype(jnp.int32)

        def cut_patch(row_at, col_at):
            return lax.dynamic_slice(padded, (zero_index, row_at, col_at), (2, side_len, side_len))
        patches = jax.vmap(cut_patch)(row_start, col_start)
        exit_waves = exit_wave(probe_field, patches)
        wave_grads = transform(exit_waves, measured, tables)
        live_mask = (jnp.arange(SLOTS, dtype=jnp.int32) < live_total).astype(jnp.float32)
        patch_grad = object_gradient(probe_field, wave_grads) * live_mask[:, None, None, None]

        def add_one(slot_index, running):
            corner = (zero_index, row_start[slot_index], col_start[slot_index])
            current = lax.dynamic_slice(running, corner, (2, side_len, side_len))
            return lax.dynamic_update_slice(running, current + patch_grad[slot_index], corner)
        return (lax.fori_loop(0, SLOTS, add_one, gradient_sum), None)
    gradient_sum = jnp.zeros(padded.shape, jnp.float32)
    gradient_sum, unused = lax.scan(one_group, gradient_sum, (flat_measured, flat_shifts, flat_live, scan_ids, tile_ids))
    return gradient_sum[:, :grid_rows, :grid_cols]
```

```python
import functools

import jax
import jax.numpy as jnp
import ml_dtypes
import numpy as np
from jax import lax
from jax.experimental import pallas as pl
from jax.experimental.pallas import tpu as pltpu
from jax.sharding import PartitionSpec as P

W = 512
Q = W // 4
T = 768
E = T + W
NB = E // Q
TB = T // Q
R = 16
f32, bf16 = jnp.float32, jnp.bfloat16


def shifted(value, axis, by):
    n = lax.axis_size(axis)
    return lax.ppermute(value, axis, [(i, i + by) for i in range(n) if 0 <= i + by < n])


def tables():
    k = np.arange(W, dtype=np.int64)
    phase = (k[:, None] * k[None, :] % W).astype(np.float64) * (2.0 * np.pi / W)
    factor = 1.0 / np.sqrt(W)
    re = (np.cos(phase) * factor).astype(np.float32)[:, :Q]
    im = (-np.sin(phase) * factor).astype(np.float32)[:, :Q]
    left = np.stack(
        [
            np.block([[re[j::4], -im[j::4]], [im[j::4], re[j::4]]])
            for j in range(4)
        ]
    ).astype(ml_dtypes.bfloat16)
    pick = np.zeros((W, W), np.float32)
    for j in range(4):
        pick[j * Q + np.arange(Q), 4 * np.arange(Q) + j] = 1.0
    return left, left.transpose(0, 2, 1).copy(), pick.astype(ml_dtypes.bfloat16)


def split4(re, im):
    t0r, t0i, t1r, t1i = re[0] + re[2], im[0] + im[2], re[0] - re[2], im[0] - im[2]
    t2r, t2i, t3r, t3i = re[1] + re[3], im[1] + im[3], re[1] - re[3], im[1] - im[3]
    return (
        (t0r + t2r, t1r + t3i, t0r - t2r, t1r - t3i),
        (t0i + t2i, t1i - t3r, t0i - t2i, t1i + t3r),
    )


def join4(re, im):
    s0r, s0i, s1r, s1i = re[0] + re[2], im[0] + im[2], re[0] - re[2], im[0] - im[2]
    s2r, s2i, s3r, s3i = re[1] + re[3], im[1] + im[3], re[1] - re[3], im[1] - im[3]
    return (
        (s0r + s2r, s1r - s3i, s0r - s2r, s1r + s3i),
        (s0i + s2i, s1i + s3r, s0i - s2i, s1i - s3r),
    )


def lanes(b):
    return pl.ds(b * Q, Q)


def sort_kernel(pick_ref, pick_t_ref, in_ref, out_ref):
    rows = jnp.dot(pick_ref[...], in_ref[0], preferred_element_type=f32).astype(bf16)
    out_ref[0] = jnp.dot(rows, pick_t_ref[...], preferred_element_type=f32).astype(bf16)


def sort_intensities(measured, pick):
    slots = measured.shape[0]
    whole = pl.BlockSpec((W, W), lambda s: (0, 0))
    each = pl.BlockSpec((1, W, W), lambda s: (s, 0, 0))
    return pl.pallas_call(
        sort_kernel,
        grid=(slots,),
        in_specs=[whole, whole, each],
        out_specs=each,
        out_shape=jax.ShapeDtypeStruct(measured.shape, bf16),
        cost_estimate=pl.CostEstimate(
            flops=slots * 4 * W**3, bytes_accessed=slots * 4 * W * W, transcendentals=0
        ),
        compiler_params=pltpu.CompilerParams(vmem_limit_bytes=16 * 2**20),
    )(jnp.asarray(pick), jnp.asarray(pick.T.copy()), measured)


def main_kernel(
    live_ref,
    shift_ref,
    slab_ref,
    right_ref,
    below_ref,
    corner_ref,
    probe_ref,
    meas_ref,
    ga_ref,
    gb_ref,
    local_ref,
    spill_right_ref,
    spill_below_ref,
    spill_corner_ref,
    ext,
    grown,
    half16,
    full32,
    mid,
    out,
    in_sem,
    out_sem,
):
    def slab_copy(p, b):
        return pltpu.make_async_copy(
            slab_ref.at[p, :, lanes(b)], ext.at[p, b, pl.ds(0, T), :], in_sem.at[p, b]
        )

    def local_copy(p, b):
        return pltpu.make_async_copy(
            grown.at[p, b, pl.ds(0, T), :], local_ref.at[p, :, lanes(b)], out_sem.at[p, b]
        )

    for p in range(2):
        for b in range(TB):
            slab_copy(p, b).start()

    def clear(i, carry):
        rows = pl.ds(pl.multiple_of(i * R, R), R)
        for p in range(2):
            for b in range(NB):
                grown[p, b, rows, :] = jnp.zeros((R, Q), f32)
        return carry

    lax.fori_loop(0, E // R, clear, 0)

    def fill_right(i, carry):
        rows = pl.ds(pl.multiple_of(i * R, R), R)
        for p in range(2):
            for b in range(4):
                ext[p, TB + b, rows, :] = right_ref[p, rows, lanes(b)].astype(f32)
        return carry

    lax.fori_loop(0, T // R, fill_right, 0)

    def fill_below(i, carry):
        rows = pl.ds(pl.multiple_of(i * R, R), R)
        there = pl.ds(pl.multiple_of(T + i * R, R), R)
        for p in range(2):
            for b in range(TB):
                ext[p, b, there, :] = below_ref[p, rows, lanes(b)].astype(f32)
            for b in range(4):
                ext[p, TB + b, there, :] = corner_ref[p, rows, lanes(b)].astype(f32)
        return carry

    lax.fori_loop(0, W // R, fill_below, 0)

    for p in range(2):
        for b in range(TB):
            slab_copy(p, b).wait()

    lane = lax.broadcasted_iota(jnp.int32, (R, Q), 1)

    def one_slot(slot, carry):
        row0 = shift_ref[slot, 0]
        col0 = shift_ref[slot, 1]
        block0 = col0 // Q
        by = col0 % Q
        inner = lane < Q - by
        outer = lane < by

        def cut(i, c):
            for b in range(4):
                re, im = [], []
                for q in range(4):
                    rows = pl.ds(row0 + q * Q + i * R, R)
                    here = pl.ds(pl.multiple_of(q * Q + i * R, R), R)
                    part = []
                    for p in range(2):
                        one = pltpu.roll(ext[p, block0 + b, rows, :], Q - by, 1)
                        two = pltpu.roll(ext[p, block0 + b + 1, rows, :], Q - by, 1)
                        part.append(jnp.where(inner, one, two))
                    pr, pi = probe_ref[0, here, lanes(b)], probe_ref[1, here, lanes(b)]
                    re.append(pr * part[0] - pi * part[1])
                    im.append(pr * part[1] + pi * part[0])
                re, im = split4(re, im)
                top = pl.ds(pl.multiple_of(i * R, R), R)
                low = pl.ds(pl.multiple_of(Q + i * R, R), R)
                for j in range(4):
                    half16[j, top, lanes(b)] = re[j].astype(bf16)
                    half16[j, low, lanes(b)] = im[j].astype(bf16)
            return c

        lax.fori_loop(0, Q // R, cut, 0)
        for j in range(4):
            full32[j] = jnp.dot(ga_ref[j], half16[j], preferred_element_type=f32)

        def across(i, c):
            top = pl.ds(pl.multiple_of(i * R, R), R)
            low = pl.ds(pl.multiple_of(Q + i * R, R), R)
            for j in range(4):
                re = [full32[j, top, lanes(q)] for q in range(4)]
                im = [full32[j, low, lanes(q)] for q in range(4)]
                re, im = split4(re, im)
                there = pl.ds(pl.multiple_of(j * Q + i * R, R), R)
                for l in range(4):
                    mid[l, there, lanes(0)] = re[l].astype(bf16)
                    mid[l, there, lanes(1)] = im[l].astype(bf16)
            return c

        lax.fori_loop(0, Q // R, across, 0)
        for l in range(4):
            far = jnp.dot(mid[l], gb_ref[l], preferred_element_type=f32)
            re, im = far[:, :Q], far[:, Q:]
            gap = re * re + im * im - meas_ref[slot, :, lanes(l)].astype(f32)
            misfit = jnp.concatenate([gap * re, gap * im], axis=1).astype(bf16)
            out[l] = jnp.dot(misfit, ga_ref[l], preferred_element_type=f32)

        def back(i, c):
            top = pl.ds(pl.multiple_of(i * R, R), R)
            low = pl.ds(pl.multiple_of(Q + i * R, R), R)
            for j in range(4):
                here = pl.ds(pl.multiple_of(j * Q + i * R, R), R)
                re = [out[l, here, lanes(0)] for l in range(4)]
                im = [out[l, here, lanes(1)] for l in range(4)]
                re, im = join4(re, im)
                for q in range(4):
                    half16[j, top, lanes(q)] = re[q].astype(bf16)
                    half16[j, low, lanes(q)] = im[q].astype(bf16)
            return c

        lax.fori_loop(0, Q // R, back, 0)
        for j in range(4):
            full32[j] = jnp.dot(gb_ref[j], half16[j], preferred_element_type=f32)

        def add(i, c):
            top = pl.ds(pl.multiple_of(i * R, R), R)
            low = pl.ds(pl.multiple_of(Q + i * R, R), R)
            last = [[None, None] for q in range(4)]
            for b in range(5):
                if b < 4:
                    re = [full32[j, top, lanes(b)] for j in range(4)]
                    im = [full32[j, low, lanes(b)] for j in range(4)]
                    re, im = join4(re, im)
                for q in range(4):
                    rows = pl.ds(row0 + q * Q + i * R, R)
                    here = pl.ds(pl.multiple_of(q * Q + i * R, R), R)
                    if b < 4:
                        pr, pi = probe_ref[0, here, lanes(b)], probe_ref[1, here, lanes(b)]
                        both = (pr * re[q] + pi * im[q], pr * im[q] - pi * re[q])
                        both = [pltpu.roll(v, by, 1) for v in both]
                    else:
                        both = [jnp.zeros((R, Q), f32)] * 2
                    for p in range(2):
                        before = last[q][p]
                        if before is None:
                            before = jnp.zeros((R, Q), f32)
                        grown[p, block0 + b, rows, :] += jnp.where(outer, before, both[p])
                        last[q][p] = both[p]
            return c

        lax.fori_loop(0, Q // R, add, 0)
        return carry

    lax.fori_loop(0, live_ref[0], one_slot, 0)

    for p in range(2):
        for b in range(TB):
            local_copy(p, b).start()

    def drain_right(i, carry):
        rows = pl.ds(pl.multiple_of(i * R, R), R)
        for p in range(2):
            for b in range(4):
                spill_right_ref[p, rows, lanes(b)] = grown[p, TB + b, rows, :].astype(bf16)
        return carry

    lax.fori_loop(0, T // R, drain_right, 0)

    def drain_below(i, carry):
        rows = pl.ds(pl.multiple_of(i * R, R), R)
        here = pl.ds(pl.multiple_of(T + i * R, R), R)
        for p in range(2):
            for b in range(TB):
                spill_below_ref[p, rows, lanes(b)] = grown[p, b, here, :].astype(bf16)
            for b in range(4):
                spill_corner_ref[p, rows, lanes(b)] = grown[p, TB + b, here, :].astype(bf16)
        return carry

    lax.fori_loop(0, W // R, drain_below, 0)
    for p in range(2):
        for b in range(TB):
            local_copy(p, b).wait()


def solve(live, shifts, slab, right, below, corner, probe, measured, left, left_t):
    vmem = pl.BlockSpec(memory_space=pltpu.VMEM)
    smem = pl.BlockSpec(memory_space=pltpu.SMEM)
    anywhere = pl.BlockSpec(memory_space=pl.ANY)
    return pl.pallas_call(
        main_kernel,
        in_specs=[smem, smem, anywhere] + [vmem] * 7,
        out_specs=[anywhere, vmem, vmem, vmem],
        out_shape=[
            jax.ShapeDtypeStruct((2, T, T), f32),
            jax.ShapeDtypeStruct((2, T, W), bf16),
            jax.ShapeDtypeStruct((2, W, T), bf16),
            jax.ShapeDtypeStruct((2, W, W), bf16),
        ],
        scratch_shapes=[
            pltpu.VMEM((2, NB, E, Q), f32),
            pltpu.VMEM((2, NB, E, Q), f32),
            pltpu.VMEM((4, 2 * Q, W), bf16),
            pltpu.VMEM((4, 2 * Q, W), f32),
            pltpu.VMEM((4, W, 2 * Q), bf16),
            pltpu.VMEM((4, W, 2 * Q), f32),
            pltpu.SemaphoreType.DMA((2, TB)),
            pltpu.SemaphoreType.DMA((2, TB)),
        ],
        cost_estimate=pl.CostEstimate(
            flops=6 * 2 * W**3, bytes_accessed=20 * 2**20, transcendentals=0
        ),
        compiler_params=pltpu.CompilerParams(vmem_limit_bytes=56 * 2**20),
    )(live, shifts, slab, right, below, corner, probe, measured, left, left_t)


def finish_kernel(local_ref, right_ref, below_ref, out_ref):
    out_ref[...] = local_ref[...]
    out_ref[:, :, :W] += right_ref[...].astype(f32)

    @pl.when(pl.program_id(0) < W // Q)
    def _():
        out_ref[...] += below_ref[...].astype(f32)


def finish(local, right, below):
    return pl.pallas_call(
        finish_kernel,
        grid=(TB,),
        in_specs=[
            pl.BlockSpec((2, Q, T), lambda i: (0, i, 0)),
            pl.BlockSpec((2, Q, W), lambda i: (0, i, 0)),
            pl.BlockSpec((2, Q, T), lambda i: (0, jnp.minimum(i, W // Q - 1), 0)),
        ],
        out_specs=pl.BlockSpec((2, Q, T), lambda i: (0, i, 0)),
        out_shape=jax.ShapeDtypeStruct((2, T, T), f32),
        compiler_params=pltpu.CompilerParams(vmem_limit_bytes=24 * 2**20),
    )(local, right, below)


def shards(slab, probe, intensities, offsets, live_count):
    left, left_t, pick = tables()
    send_below = slab[:, :W, :].astype(bf16)
    send_right = slab[:, :, :W].astype(bf16)
    below = shifted(send_below, "tile", -1)
    right = shifted(send_right, "scan", -1)
    corner = shifted(below[:, :, :W], "scan", -1)
    measured = sort_intensities(intensities[0, 0], pick)
    live = lax.dynamic_slice(live_count[:, 0], (lax.axis_index("scan"),), (1,))
    local, to_right, to_below, to_corner = solve(
        live, offsets[0, 0], slab, right, below, corner, probe, measured,
        jnp.asarray(left), jnp.asarray(left_t),
    )
    from_left = shifted(to_right, "scan", 1)
    from_corner = shifted(to_corner, "scan", 1)
    far_half = shifted(to_below[:, :, W:], "tile", 1)
    near = (to_below[:, :, :W].astype(f32) + from_corner.astype(f32)).astype(bf16)
    near_half = shifted(near, "tile", 1)
    return finish(local, from_left, jnp.concatenate([near_half, far_half], axis=2))


def solution(mesh):
    placed = (
        P(None, "tile", "scan"),
        P(),
        P("scan", "tile", None, None, None),
        P("scan", "tile", None, None),
        P(None, "tile"),
    )
    return jax.shard_map(
        shards, mesh=mesh, in_specs=placed, out_specs=P(None, "tile", "scan"), check_vma=False
    )
```

```python
import functools

import jax
import jax.numpy as jnp
import ml_dtypes
import numpy as np
from jax import lax
from jax.experimental import pallas as pl
from jax.experimental.pallas import tpu as pltpu
from jax.sharding import PartitionSpec as P

W = 512
Q = W // 4
T = 768
E = T + W
NB = E // Q
TB = T // Q
VMEM_MAIN = 48 * 2**20
R = 16
f32, bf16 = jnp.float32, jnp.bfloat16


def shifted(value, axis, by):
    n = lax.axis_size(axis)
    return lax.ppermute(value, axis, [(i, i + by) for i in range(n) if 0 <= i + by < n])


def tables():
    k = np.arange(W, dtype=np.int64)
    phase = (k[:, None] * k[None, :] % W).astype(np.float64) * (2.0 * np.pi / W)
    factor = 1.0 / np.sqrt(W)
    re = (np.cos(phase) * factor).astype(np.float32)[:, :Q]
    im = (-np.sin(phase) * factor).astype(np.float32)[:, :Q]
    left = np.stack(
        [
            np.block([[re[j::4], -im[j::4]], [im[j::4], re[j::4]]])
            for j in range(4)
        ]
    ).astype(ml_dtypes.bfloat16)
    pick = np.zeros((W, W), np.float32)
    for j in range(4):
        pick[j * Q + np.arange(Q), 4 * np.arange(Q) + j] = 1.0
    return left, left.transpose(0, 2, 1).copy(), pick.astype(ml_dtypes.bfloat16)


def split4(re, im):
    t0r, t0i, t1r, t1i = re[0] + re[2], im[0] + im[2], re[0] - re[2], im[0] - im[2]
    t2r, t2i, t3r, t3i = re[1] + re[3], im[1] + im[3], re[1] - re[3], im[1] - im[3]
    return (
        (t0r + t2r, t1r + t3i, t0r - t2r, t1r - t3i),
        (t0i + t2i, t1i - t3r, t0i - t2i, t1i + t3r),
    )


def join4(re, im):
    s0r, s0i, s1r, s1i = re[0] + re[2], im[0] + im[2], re[0] - re[2], im[0] - im[2]
    s2r, s2i, s3r, s3i = re[1] + re[3], im[1] + im[3], re[1] - re[3], im[1] - im[3]
    return (
        (s0r + s2r, s1r - s3i, s0r - s2r, s1r + s3i),
        (s0i + s2i, s1i + s3r, s0i - s2i, s1i - s3r),
    )


def lanes(b):
    return pl.ds(b * Q, Q)


def sort_kernel(pick_ref, pick_t_ref, in_ref, out_ref):
    rows = jnp.dot(pick_ref[...], in_ref[0], preferred_element_type=f32).astype(bf16)
    out_ref[0] = jnp.dot(rows, pick_t_ref[...], preferred_element_type=f32).astype(bf16)


def sort_intensities(measured, pick):
    slots = measured.shape[0]
    whole = pl.BlockSpec((W, W), lambda s: (0, 0))
    each = pl.BlockSpec((1, W, W), lambda s: (s, 0, 0))
    return pl.pallas_call(
        sort_kernel,
        grid=(slots,),
        in_specs=[whole, whole, each],
        out_specs=each,
        out_shape=jax.ShapeDtypeStruct(measured.shape, bf16),
        cost_estimate=pl.CostEstimate(
            flops=slots * 4 * W**3, bytes_accessed=slots * 4 * W * W, transcendentals=0
        ),
        compiler_params=pltpu.CompilerParams(vmem_limit_bytes=16 * 2**20),
    )(jnp.asarray(pick), jnp.asarray(pick.T.copy()), measured)


def main_kernel(
    live_ref,
    shift_ref,
    slab_ref,
    right_ref,
    below0_ref,
    below1_ref,
    below2_ref,
    corner0_ref,
    corner1_ref,
    probe_ref,
    meas_ref,
    ga_ref,
    gb_ref,
    local_ref,
    spill_right_ref,
    spill_near_ref,
    spill_far_ref,
    spill_corner_ref,
    ext,
    grown,
    half16,
    full32,
    mid,
    out,
    in_sem,
    out_sem,
):
    below_refs = (below0_ref, below1_ref, below2_ref)
    corner_refs = (corner0_ref, corner1_ref)

    def slab_copy(p, b):
        return pltpu.make_async_copy(
            slab_ref.at[p, :, lanes(b)], ext.at[p, b, pl.ds(0, T), :], in_sem.at[p, b]
        )

    def local_copy(p, b):
        return pltpu.make_async_copy(
            grown.at[p, b, pl.ds(0, T), :], local_ref.at[p, :, lanes(b)], out_sem.at[p, b]
        )

    for p in range(2):
        for b in range(TB):
            slab_copy(p, b).start()

    def clear(i, carry):
        rows = pl.ds(pl.multiple_of(i * R, R), R)
        for p in range(2):
            for b in range(NB):
                grown[p, b, rows, :] = jnp.zeros((R, Q), f32)
        return carry

    lax.fori_loop(0, E // R, clear, 0)

    def fill_right(i, carry):
        rows = pl.ds(pl.multiple_of(i * R, R), R)
        for p in range(2):
            for b in range(4):
                ext[p, TB + b, rows, :] = right_ref[p, rows, lanes(b)].astype(f32)
        return carry

    lax.fori_loop(0, T // R, fill_right, 0)

    def fill_below(i, carry):
        rows = pl.ds(pl.multiple_of(i * R, R), R)
        there = pl.ds(pl.multiple_of(T + i * R, R), R)
        for p in range(2):
            for b in range(2):
                for piece in range(3):
                    ext[p, 2 * piece + b, there, :] = below_refs[piece][p, rows, lanes(b)].astype(f32)
                for piece in range(2):
                    ext[p, TB + 2 * piece + b, there, :] = corner_refs[piece][
                        p, rows, lanes(b)
                    ].astype(f32)
        return carry

    lax.fori_loop(0, W // R, fill_below, 0)

    for p in range(2):
        for b in range(TB):
            slab_copy(p, b).wait()

    lane = lax.broadcasted_iota(jnp.int32, (R, Q), 1)

    def one_slot(slot, carry):
        row0 = shift_ref[0, slot]
        col0 = shift_ref[1, slot]
        block0 = col0 // Q
        by = col0 % Q
        inner = lane < Q - by
        outer = lane < by

        def cut(i, c):
            for b in range(4):
                re, im = [], []
                for q in range(4):
                    rows = pl.ds(row0 + q * Q + i * R, R)
                    here = pl.ds(pl.multiple_of(q * Q + i * R, R), R)
                    part = []
                    for p in range(2):
                        one = pltpu.roll(ext[p, block0 + b, rows, :], Q - by, 1)
                        two = pltpu.roll(ext[p, block0 + b + 1, rows, :], Q - by, 1)
                        part.append(jnp.where(inner, one, two))
                    pr, pi = probe_ref[0, here, lanes(b)], probe_ref[1, here, lanes(b)]
                    re.append(pr * part[0] - pi * part[1])
                    im.append(pr * part[1] + pi * part[0])
                re, im = split4(re, im)
                top = pl.ds(pl.multiple_of(i * R, R), R)
                low = pl.ds(pl.multiple_of(Q + i * R, R), R)
                for j in range(4):
                    half16[j, top, lanes(b)] = re[j].astype(bf16)
                    half16[j, low, lanes(b)] = im[j].astype(bf16)
            return c

        lax.fori_loop(0, Q // R, cut, 0)
        for j in range(4):
            full32[j] = jnp.dot(ga_ref[j], half16[j], preferred_element_type=f32)

        def across(i, c):
            top = pl.ds(pl.multiple_of(i * R, R), R)
            low = pl.ds(pl.multiple_of(Q + i * R, R), R)
            for j in range(4):
                re = [full32[j, top, lanes(q)] for q in range(4)]
                im = [full32[j, low, lanes(q)] for q in range(4)]
                re, im = split4(re, im)
                there = pl.ds(pl.multiple_of(j * Q + i * R, R), R)
                for l in range(4):
                    mid[l, there, lanes(0)] = re[l].astype(bf16)
                    mid[l, there, lanes(1)] = im[l].astype(bf16)
            return c

        lax.fori_loop(0, Q // R, across, 0)
        for l in range(4):
            far = jnp.dot(mid[l], gb_ref[l], preferred_element_type=f32)
            re, im = far[:, :Q], far[:, Q:]
            gap = re * re + im * im - meas_ref[slot, :, lanes(l)].astype(f32)
            misfit = jnp.concatenate([gap * re, gap * im], axis=1).astype(bf16)
            out[l] = jnp.dot(misfit, ga_ref[l], preferred_element_type=f32)

        def back(i, c):
            top = pl.ds(pl.multiple_of(i * R, R), R)
            low = pl.ds(pl.multiple_of(Q + i * R, R), R)
            for j in range(4):
                here = pl.ds(pl.multiple_of(j * Q + i * R, R), R)
                re = [out[l, here, lanes(0)] for l in range(4)]
                im = [out[l, here, lanes(1)] for l in range(4)]
                re, im = join4(re, im)
                for q in range(4):
                    half16[j, top, lanes(q)] = re[q].astype(bf16)
                    half16[j, low, lanes(q)] = im[q].astype(bf16)
            return c

        lax.fori_loop(0, Q // R, back, 0)
        for j in range(4):
            full32[j] = jnp.dot(gb_ref[j], half16[j], preferred_element_type=f32)

        def add(i, c):
            top = pl.ds(pl.multiple_of(i * R, R), R)
            low = pl.ds(pl.multiple_of(Q + i * R, R), R)
            last = [[None, None] for q in range(4)]
            for b in range(5):
                if b < 4:
                    re = [full32[j, top, lanes(b)] for j in range(4)]
                    im = [full32[j, low, lanes(b)] for j in range(4)]
                    re, im = join4(re, im)
                for q in range(4):
                    rows = pl.ds(row0 + q * Q + i * R, R)
                    here = pl.ds(pl.multiple_of(q * Q + i * R, R), R)
                    if b < 4:
                        pr, pi = probe_ref[0, here, lanes(b)], probe_ref[1, here, lanes(b)]
                        both = (pr * re[q] + pi * im[q], pr * im[q] - pi * re[q])
                        both = [pltpu.roll(v, by, 1) for v in both]
                    else:
                        both = [jnp.zeros((R, Q), f32)] * 2
                    for p in range(2):
                        before = last[q][p]
                        if before is None:
                            before = jnp.zeros((R, Q), f32)
                        grown[p, block0 + b, rows, :] += jnp.where(outer, before, both[p])
                        last[q][p] = both[p]
            return c

        lax.fori_loop(0, Q // R, add, 0)
        return carry

    lax.fori_loop(0, live_ref[0], one_slot, 0)

    for p in range(2):
        for b in range(TB):
            local_copy(p, b).start()

    def drain_below(i, carry):
        rows = pl.ds(pl.multiple_of(i * R, R), R)
        here = pl.ds(pl.multiple_of(T + i * R, R), R)
        for p in range(2):
            for b in range(4):
                spill_near_ref[p, rows, lanes(b)] = grown[p, b, here, :].astype(bf16)
                spill_corner_ref[p, rows, lanes(b)] = grown[p, TB + b, here, :].astype(bf16)
            for b in range(2):
                spill_far_ref[p, rows, lanes(b)] = grown[p, 4 + b, here, :].astype(bf16)
        return carry

    lax.fori_loop(0, W // R, drain_below, 0)

    def drain_right(i, carry):
        rows = pl.ds(pl.multiple_of(i * R, R), R)
        for p in range(2):
            for b in range(4):
                spill_right_ref[p, rows, lanes(b)] = grown[p, TB + b, rows, :].astype(bf16)
        return carry

    lax.fori_loop(0, T // R, drain_right, 0)
    for p in range(2):
        for b in range(TB):
            local_copy(p, b).wait()


def solve(live, shifts, slab, right, below, corner, probe, measured, left, left_t):
    vmem = pl.BlockSpec(memory_space=pltpu.VMEM)
    smem = pl.BlockSpec(memory_space=pltpu.SMEM)
    anywhere = pl.BlockSpec(memory_space=pl.ANY)
    return pl.pallas_call(
        main_kernel,
        in_specs=[smem, smem, anywhere] + [vmem] * 10,
        out_specs=[anywhere] + [vmem] * 4,
        out_shape=[
            jax.ShapeDtypeStruct((2, T, T), f32),
            jax.ShapeDtypeStruct((2, T, W), bf16),
            jax.ShapeDtypeStruct((2, W, W), bf16),
            jax.ShapeDtypeStruct((2, W, T - W), bf16),
            jax.ShapeDtypeStruct((2, W, W), bf16),
        ],
        scratch_shapes=[
            pltpu.VMEM((2, NB, E, Q), f32),
            pltpu.VMEM((2, NB, E, Q), f32),
            pltpu.VMEM((4, 2 * Q, W), bf16),
            pltpu.VMEM((4, 2 * Q, W), f32),
            pltpu.VMEM((4, W, 2 * Q), bf16),
            pltpu.VMEM((4, W, 2 * Q), f32),
            pltpu.SemaphoreType.DMA((2, TB)),
            pltpu.SemaphoreType.DMA((2, TB)),
        ],
        cost_estimate=pl.CostEstimate(
            flops=6 * 4 * W**3, bytes_accessed=20 * 2**20, transcendentals=0
        ),
        compiler_params=pltpu.CompilerParams(vmem_limit_bytes=VMEM_MAIN),
    )(live, shifts, slab, right, *below, *corner, probe, measured, left, left_t)


def add_right_kernel(local_ref, right_ref, out_ref):
    out_ref[...] = local_ref[...]
    out_ref[:, :, :W] += right_ref[...].astype(f32)


def add_right(local, right):
    return pl.pallas_call(
        add_right_kernel,
        grid=(TB,),
        in_specs=[
            pl.BlockSpec((2, Q, T), lambda i: (0, i, 0)),
            pl.BlockSpec((2, Q, W), lambda i: (0, i, 0)),
        ],
        out_specs=pl.BlockSpec((2, Q, T), lambda i: (0, i, 0)),
        out_shape=jax.ShapeDtypeStruct((2, T, T), f32),
        input_output_aliases={0: 0},
        compiler_params=pltpu.CompilerParams(vmem_limit_bytes=16 * 2**20),
    )(local, right)


def add_below_kernel(local_ref, near_ref, far_ref, out_ref):
    out_ref[:, :, :W] = local_ref[:, :, :W] + near_ref[...].astype(f32)
    out_ref[:, :, W:] = local_ref[:, :, W:] + far_ref[...].astype(f32)


def add_below(local, near, far):
    return pl.pallas_call(
        add_below_kernel,
        grid=(W // Q,),
        in_specs=[
            pl.BlockSpec((2, Q, T), lambda i: (0, i, 0)),
            pl.BlockSpec((2, Q, W), lambda i: (0, i, 0)),
            pl.BlockSpec((2, Q, T - W), lambda i: (0, i, 0)),
        ],
        out_specs=pl.BlockSpec((2, Q, T), lambda i: (0, i, 0)),
        out_shape=jax.ShapeDtypeStruct((2, T, T), f32),
        input_output_aliases={0: 0},
        compiler_params=pltpu.CompilerParams(vmem_limit_bytes=16 * 2**20),
    )(local, near, far)


def shards(slab, probe, intensities, offsets, live_count):
    left, left_t, pick = tables()
    cols = [slice(piece * 2 * Q, (piece + 1) * 2 * Q) for piece in range(3)]
    below0 = shifted(slab[:, :W, cols[0]].astype(bf16), "tile", -1)
    below1 = shifted(slab[:, :W, cols[1]].astype(bf16), "tile", -1)
    below2 = shifted(slab[:, :W, cols[2]].astype(bf16), "tile", -1)
    right = shifted(slab[:, :, :W].astype(bf16), "scan", -1)
    measured = sort_intensities(intensities[0, 0], pick)
    live = lax.dynamic_slice(live_count[:, 0], (lax.axis_index("scan"),), (1,))
    shifts = offsets[0, 0].T
    below0, measured, live, shifts = lax.optimization_barrier((below0, measured, live, shifts))
    corner0 = shifted(below0, "scan", -1)
    corner1 = shifted(below1, "scan", -1)
    local, to_right, near, far, to_corner = solve(
        live, shifts, slab, right, (below0, below1, below2), (corner0, corner1), probe, measured,
        jnp.asarray(left), jnp.asarray(left_t),
    )
    far = shifted(far, "tile", 1)
    from_corner = shifted(to_corner, "scan", 1)
    near = (near.astype(f32) + from_corner.astype(f32)).astype(bf16)
    near, to_right, far = lax.optimization_barrier((near, to_right, far))
    near = shifted(near, "tile", 1)
    from_left = shifted(to_right, "scan", 1)
    local = add_right(local, from_left)
    return add_below(local, near, far)


def solution(mesh):
    placed = (
        P(None, "tile", "scan"),
        P(),
        P("scan", "tile", None, None, None),
        P("scan", "tile", None, None),
        P(None, "tile"),
    )
    return jax.shard_map(
        shards, mesh=mesh, in_specs=placed, out_specs=P(None, "tile", "scan"), check_vma=False
    )
```

```python
import functools

import jax
import jax.numpy as jnp
import ml_dtypes
import numpy as np
from jax import lax
from jax.experimental import pallas as pl
from jax.experimental.pallas import tpu as pltpu
from jax.sharding import PartitionSpec as P

W = 512
Q = W // 4
T = 768
E = T + W
NB = E // Q
TB = T // Q
CUTS = (0, 208, 384, 512)
F = T - W
R = 16
f32, bf16 = jnp.float32, jnp.bfloat16


def shifted(value, axis, by):
    n = lax.axis_size(axis)
    return lax.ppermute(value, axis, [(i, i + by) for i in range(n) if 0 <= i + by < n])


def tables():
    k = np.arange(W, dtype=np.int64)
    phase = (k[:, None] * k[None, :] % W).astype(np.float64) * (2.0 * np.pi / W)
    factor = 1.0 / np.sqrt(W)
    re = (np.cos(phase) * factor).astype(np.float32)[:, :Q]
    im = (-np.sin(phase) * factor).astype(np.float32)[:, :Q]
    left = np.stack(
        [
            np.block([[re[j::4], -im[j::4]], [im[j::4], re[j::4]]])
            for j in range(4)
        ]
    ).astype(ml_dtypes.bfloat16)
    pick = np.zeros((W, W), np.float32)
    for j in range(4):
        pick[j * Q + np.arange(Q), 4 * np.arange(Q) + j] = 1.0
    return left, left.transpose(0, 2, 1).copy(), pick.astype(ml_dtypes.bfloat16)


def split4(re, im):
    t0r, t0i, t1r, t1i = re[0] + re[2], im[0] + im[2], re[0] - re[2], im[0] - im[2]
    t2r, t2i, t3r, t3i = re[1] + re[3], im[1] + im[3], re[1] - re[3], im[1] - im[3]
    return (
        (t0r + t2r, t1r + t3i, t0r - t2r, t1r - t3i),
        (t0i + t2i, t1i - t3r, t0i - t2i, t1i + t3r),
    )


def join4(re, im):
    s0r, s0i, s1r, s1i = re[0] + re[2], im[0] + im[2], re[0] - re[2], im[0] - im[2]
    s2r, s2i, s3r, s3i = re[1] + re[3], im[1] + im[3], re[1] - re[3], im[1] - im[3]
    return (
        (s0r + s2r, s1r - s3i, s0r - s2r, s1r + s3i),
        (s0i + s2i, s1i + s3r, s0i - s2i, s1i - s3r),
    )


def lanes(b):
    return pl.ds(b * Q, Q)


def each_rows(count, body):
    def step(i, carry):
        body(pl.multiple_of(i * R, R))
        return carry

    lax.fori_loop(0, count // R, step, 0)


VMEM = pl.BlockSpec(memory_space=pltpu.VMEM)
SMEM = pl.BlockSpec(memory_space=pltpu.SMEM)
ANY = pl.BlockSpec(memory_space=pl.ANY)
TILES = jax.ShapeDtypeStruct((2, NB, E, Q), f32)


def params(mib):
    return pltpu.CompilerParams(vmem_limit_bytes=mib * 2**20)


def cost():
    return pl.CostEstimate(flops=1024, bytes_accessed=1024, transcendentals=0)


def pack_kernel(slab_ref, *refs):
    count = len(CUTS) - 1
    below, right_ref, buf, sem = refs[:count], *refs[count:]
    cuts = (*CUTS, T)

    def copy(c):
        rows = pl.ds(cuts[c], cuts[c + 1] - cuts[c])
        return pltpu.make_async_copy(slab_ref.at[:, rows, :], buf.at[:, rows, :], sem.at[c])

    for c in range(count + 1):
        copy(c).start()
    for c in range(count + 1):
        copy(c).wait()

        def convert(row):
            here = pl.ds(pl.multiple_of(cuts[c] + row, R), R)
            for p in range(2):
                part = buf[p, here, :].astype(bf16)
                right_ref[p, here, :] = part[:, :W]
                if c < count:
                    below[c][p, pl.ds(row, R), :] = part

        each_rows(cuts[c + 1] - cuts[c], convert)


def pack(slab):
    rows = [high - low for low, high in zip(CUTS[:-1], CUTS[1:])]
    shapes = [(2, r, T) for r in rows] + [(2, T, W)]
    made = pl.pallas_call(
        pack_kernel,
        in_specs=[ANY],
        out_specs=[VMEM] * len(shapes),
        out_shape=[jax.ShapeDtypeStruct(shape, bf16) for shape in shapes],
        scratch_shapes=[pltpu.VMEM((2, T, T), f32), pltpu.SemaphoreType.DMA((len(CUTS),))],
        cost_estimate=cost(),
        compiler_params=params(24),
    )(slab)
    return made[:-1], made[-1]


def sort_kernel(pick_ref, pick_t_ref, in_ref, out_ref):
    rows = jnp.dot(pick_ref[...], in_ref[0], preferred_element_type=f32).astype(bf16)
    out_ref[0] = jnp.dot(rows, pick_t_ref[...], preferred_element_type=f32).astype(bf16)


def sort_intensities(measured, pick):
    whole = pl.BlockSpec((W, W), lambda s: (0, 0))
    each = pl.BlockSpec((1, W, W), lambda s: (s, 0, 0))
    return pl.pallas_call(
        sort_kernel,
        grid=(measured.shape[0],),
        in_specs=[whole, whole, each],
        out_specs=each,
        out_shape=jax.ShapeDtypeStruct(measured.shape, bf16),
        cost_estimate=cost(),
        compiler_params=params(16),
    )(jnp.asarray(pick), jnp.asarray(pick.T.copy()), measured)


def slots_kernel(
    chunk,
    meta_ref,
    below_ref,
    corner_ref,
    probe_ref,
    meas_ref,
    ga_ref,
    gb_ref,
    first_ref,
    second_ref,
    ext,
    grown,
    half16,
    full32,
    mid,
    out,
    sem,
):
    def copy(p, b):
        return pltpu.make_async_copy(
            first_ref.at[p, :, lanes(b)], ext.at[p, b, pl.ds(0, T), :], sem.at[p, b]
        )

    def clear(row):
        for p in range(2):
            for b in range(NB):
                grown[p, b, pl.ds(row, R), :] = jnp.zeros((R, Q), f32)

    def fill_right(row):
        for p in range(2):
            for b in range(4):
                ext[p, TB + b, pl.ds(row, R), :] = second_ref[p, pl.ds(row, R), lanes(b)].astype(f32)

    if chunk == 0:
        for p in range(2):
            for b in range(TB):
                copy(p, b).start()
        each_rows(E, clear)
        each_rows(T, fill_right)

    def fill(row):
        rows = pl.ds(row, R)
        there = pl.ds(pl.multiple_of(T + CUTS[chunk] + row, R), R)
        for p in range(2):
            for b in range(TB):
                ext[p, b, there, :] = below_ref[p, rows, lanes(b)].astype(f32)
            for b in range(4):
                ext[p, TB + b, there, :] = corner_ref[p, rows, lanes(b)].astype(f32)

    each_rows(CUTS[chunk + 1] - CUTS[chunk], fill)
    if chunk == 0:
        for p in range(2):
            for b in range(TB):
                copy(p, b).wait()

    lane = lax.broadcasted_iota(jnp.int32, (R, Q), 1)

    def one_slot(slot, carry):
        row0 = meta_ref[0, slot]
        col0 = meta_ref[1, slot]
        block0 = col0 // Q
        by = col0 % Q
        inner = lane < Q - by
        outer = lane < by

        def cut(i, c):
            for b in range(4):
                re, im = [], []
                for q in range(4):
                    rows = pl.ds(row0 + q * Q + i * R, R)
                    here = pl.ds(pl.multiple_of(q * Q + i * R, R), R)
                    part = []
                    for p in range(2):
                        one = pltpu.roll(ext[p, block0 + b, rows, :], Q - by, 1)
                        two = pltpu.roll(ext[p, block0 + b + 1, rows, :], Q - by, 1)
                        part.append(jnp.where(inner, one, two))
                    pr, pi = probe_ref[0, here, lanes(b)], probe_ref[1, here, lanes(b)]
                    re.append(pr * part[0] - pi * part[1])
                    im.append(pr * part[1] + pi * part[0])
                re, im = split4(re, im)
                top = pl.ds(pl.multiple_of(i * R, R), R)
                low = pl.ds(pl.multiple_of(Q + i * R, R), R)
                for j in range(4):
                    half16[j, top, lanes(b)] = re[j].astype(bf16)
                    half16[j, low, lanes(b)] = im[j].astype(bf16)
            return c

        lax.fori_loop(0, Q // R, cut, 0)
        for j in range(4):
            full32[j] = jnp.dot(ga_ref[j], half16[j], preferred_element_type=f32)

        def across(i, c):
            top = pl.ds(pl.multiple_of(i * R, R), R)
            low = pl.ds(pl.multiple_of(Q + i * R, R), R)
            for j in range(4):
                re = [full32[j, top, lanes(q)] for q in range(4)]
                im = [full32[j, low, lanes(q)] for q in range(4)]
                re, im = split4(re, im)
                there = pl.ds(pl.multiple_of(j * Q + i * R, R), R)
                for l in range(4):
                    mid[l, there, lanes(0)] = re[l].astype(bf16)
                    mid[l, there, lanes(1)] = im[l].astype(bf16)
            return c

        lax.fori_loop(0, Q // R, across, 0)
        for l in range(4):
            far = jnp.dot(mid[l], gb_ref[l], preferred_element_type=f32)
            re, im = far[:, :Q], far[:, Q:]
            gap = re * re + im * im - meas_ref[slot, :, lanes(l)].astype(f32)
            misfit = jnp.concatenate([gap * re, gap * im], axis=1).astype(bf16)
            out[l] = jnp.dot(misfit, ga_ref[l], preferred_element_type=f32)

        def back(i, c):
            top = pl.ds(pl.multiple_of(i * R, R), R)
            low = pl.ds(pl.multiple_of(Q + i * R, R), R)
            for j in range(4):
                here = pl.ds(pl.multiple_of(j * Q + i * R, R), R)
                re = [out[l, here, lanes(0)] for l in range(4)]
                im = [out[l, here, lanes(1)] for l in range(4)]
                re, im = join4(re, im)
                for q in range(4):
                    half16[j, top, lanes(q)] = re[q].astype(bf16)
                    half16[j, low, lanes(q)] = im[q].astype(bf16)
            return c

        lax.fori_loop(0, Q // R, back, 0)
        for j in range(4):
            full32[j] = jnp.dot(gb_ref[j], half16[j], preferred_element_type=f32)

        def add(i, c):
            top = pl.ds(pl.multiple_of(i * R, R), R)
            low = pl.ds(pl.multiple_of(Q + i * R, R), R)
            last = [[None, None] for q in range(4)]
            for b in range(5):
                if b < 4:
                    re = [full32[j, top, lanes(b)] for j in range(4)]
                    im = [full32[j, low, lanes(b)] for j in range(4)]
                    re, im = join4(re, im)
                for q in range(4):
                    rows = pl.ds(row0 + q * Q + i * R, R)
                    here = pl.ds(pl.multiple_of(q * Q + i * R, R), R)
                    if b < 4:
                        pr, pi = probe_ref[0, here, lanes(b)], probe_ref[1, here, lanes(b)]
                        both = (pr * re[q] + pi * im[q], pr * im[q] - pi * re[q])
                        both = [pltpu.roll(v, by, 1) for v in both]
                    else:
                        both = [jnp.zeros((R, Q), f32)] * 2
                    for p in range(2):
                        before = last[q][p]
                        if before is None:
                            before = jnp.zeros((R, Q), f32)
                        grown[p, block0 + b, rows, :] += jnp.where(outer, before, both[p])
                        last[q][p] = both[p]
            return c

        lax.fori_loop(0, Q // R, add, 0)
        return carry

    def maybe(slot, carry):
        @pl.when(meta_ref[2, slot] == chunk)
        def _():
            one_slot(slot, 0)

        return carry

    lax.fori_loop(0, meta_ref.shape[1], maybe, 0)


def solve(chunk, meta, below, corner, probe, measured, left, left_t, first, second):
    return pl.pallas_call(
        functools.partial(slots_kernel, chunk),
        in_specs=[SMEM] + [VMEM] * 6 + [ANY if chunk == 0 else VMEM, VMEM],
        out_specs=[VMEM, VMEM],
        out_shape=[TILES, TILES],
        input_output_aliases={7: 0, 8: 1} if chunk else {},
        scratch_shapes=[
            pltpu.VMEM((4, 2 * Q, W), bf16),
            pltpu.VMEM((4, 2 * Q, W), f32),
            pltpu.VMEM((4, W, 2 * Q), bf16),
            pltpu.VMEM((4, W, 2 * Q), f32),
            pltpu.SemaphoreType.DMA((2, TB)),
        ],
        cost_estimate=cost(),
        compiler_params=params(12),
    )(meta, below, corner, probe, measured, left, left_t, first, second)


def drain_kernel(grown, near_ref, far_ref, corner_ref, right_ref):
    def below(row):
        rows = pl.ds(row, R)
        here = pl.ds(pl.multiple_of(T + row, R), R)
        for p in range(2):
            for b in range(4):
                near_ref[p, rows, lanes(b)] = grown[p, b, here, :].astype(bf16)
                corner_ref[p, rows, lanes(b)] = grown[p, TB + b, here, :].astype(bf16)
            for b in range(2):
                far_ref[p, rows, lanes(b)] = grown[p, 4 + b, here, :].astype(bf16)

    def right(row):
        rows = pl.ds(row, R)
        for p in range(2):
            for b in range(4):
                right_ref[p, rows, lanes(b)] = grown[p, TB + b, rows, :].astype(bf16)

    each_rows(W, below)
    each_rows(T, right)


def drain(grown):
    return pl.pallas_call(
        drain_kernel,
        in_specs=[VMEM],
        out_specs=[VMEM] * 4,
        out_shape=[
            jax.ShapeDtypeStruct((2, W, W), bf16),
            jax.ShapeDtypeStruct((2, W, F), bf16),
            jax.ShapeDtypeStruct((2, W, W), bf16),
            jax.ShapeDtypeStruct((2, T, W), bf16),
        ],
        cost_estimate=cost(),
        compiler_params=params(4),
    )(grown)


def write_copy(tile, whole_ref, sem, p, b, first, count):
    rows = pl.ds(first, count)
    return pltpu.make_async_copy(
        tile.at[p, b, rows, :], whole_ref.at[p, rows, lanes(b)], sem.at[p, b]
    )


def side_kernel(right_ref, far_ref, grown_in, grown, whole_ref, sem):
    def done(p, b):
        if b < 4:
            return write_copy(grown, whole_ref, sem, p, b, W, T - W)
        return write_copy(grown, whole_ref, sem, p, b, 0, T)

    def far(row):
        rows = pl.ds(row, R)
        for p in range(2):
            for b in range(2):
                grown[p, 4 + b, rows, :] += far_ref[p, rows, lanes(b)].astype(f32)

    each_rows(W, far)
    for p in range(2):
        for b in range(4, TB):
            done(p, b).start()

    def right(row):
        rows = pl.ds(row, R)
        for p in range(2):
            for b in range(4):
                grown[p, b, rows, :] += right_ref[p, rows, lanes(b)].astype(f32)

    each_rows(T, right)
    for p in range(2):
        for b in range(4):
            done(p, b).start()
    for p in range(2):
        for b in range(TB):
            done(p, b).wait()


def add_side(right, far, grown):
    return pl.pallas_call(
        side_kernel,
        in_specs=[VMEM] * 3,
        out_specs=[VMEM, ANY],
        out_shape=[TILES, jax.ShapeDtypeStruct((2, T, T), f32)],
        input_output_aliases={2: 0},
        scratch_shapes=[pltpu.SemaphoreType.DMA((2, TB))],
        cost_estimate=cost(),
        compiler_params=params(4),
    )(right, far, grown)


def last_kernel(near_ref, grown_in, whole_in, grown, whole_ref, sem):
    for b in range(4):
        for p in range(2):

            def add(row):
                rows = pl.ds(row, R)
                grown[p, b, rows, :] += near_ref[p, rows, lanes(b)].astype(f32)

            each_rows(W, add)
            write_copy(grown, whole_ref, sem, p, b, 0, W).start()
    for b in range(4):
        for p in range(2):
            write_copy(grown, whole_ref, sem, p, b, 0, W).wait()


def add_near(near, grown, whole):
    return pl.pallas_call(
        last_kernel,
        in_specs=[VMEM, VMEM, ANY],
        out_specs=[VMEM, ANY],
        out_shape=[TILES, jax.ShapeDtypeStruct((2, T, T), f32)],
        input_output_aliases={1: 0, 2: 1},
        scratch_shapes=[pltpu.SemaphoreType.DMA((2, 4))],
        cost_estimate=cost(),
        compiler_params=params(4),
    )(near, grown, whole)[1]


def shards(slab, probe, intensities, offsets, live_count):
    left, left_t, pick = tables()
    left, left_t = jnp.asarray(left), jnp.asarray(left_t)
    chunks = range(len(CUTS) - 1)
    send_below, send_right = pack(slab)
    below = [shifted(part, "tile", -1) for part in send_below]
    right = shifted(send_right, "scan", -1)
    live = lax.dynamic_slice(live_count[:, 0], (lax.axis_index("scan"),), (1,))
    shifts = offsets[0, 0].T
    reach = shifts[0] + (W - T)
    stage = sum((reach > CUTS[c + 1]).astype(jnp.int32) for c in chunks)
    stage = jnp.where(jnp.arange(shifts.shape[1], dtype=jnp.int32) < live, stage, len(CUTS))
    meta = jnp.concatenate([shifts, stage[None]], axis=0)
    measured = sort_intensities(intensities[0, 0], pick)
    below[0], measured, meta = lax.optimization_barrier((below[0], measured, meta))
    corner = [shifted(part[:, :, :W], "scan", -1) for part in below]
    ext, grown = slab, right
    for c in chunks:
        ext, grown = solve(
            c, meta, below[c], corner[c], probe, measured, left, left_t, ext, grown
        )
    to_near, to_far, to_corner, to_right = drain(grown)
    to_far = shifted(to_far, "tile", 1)
    from_corner = shifted(to_corner, "scan", 1)
    to_near = (to_near.astype(f32) + from_corner.astype(f32)).astype(bf16)
    to_near, to_far = lax.optimization_barrier((to_near, to_far))
    to_near = shifted(to_near, "tile", 1)
    from_left = shifted(to_right, "scan", 1)
    grown, whole = add_side(from_left, to_far, grown)
    return add_near(to_near, grown, whole)


def solution(mesh):
    placed = (
        P(None, "tile", "scan"),
        P(),
        P("scan", "tile", None, None, None),
        P("scan", "tile", None, None),
        P(None, "tile"),
    )
    return jax.shard_map(
        shards, mesh=mesh, in_specs=placed, out_specs=P(None, "tile", "scan"), check_vma=False
    )
```

```python
import functools

import jax
import jax.numpy as jnp
import ml_dtypes
import numpy as np
from jax import lax
from jax.experimental import pallas as pl
from jax.experimental.pallas import tpu as pltpu
from jax.sharding import PartitionSpec as P

W = 512
Q = W // 4
T = 768
E = T + W
NB = E // Q
TB = T // Q
CUTS = (0, 208, 384, 512)
F = T - W
R = 16
f32, bf16 = jnp.float32, jnp.bfloat16


def shifted(value, axis, by):
    n = lax.axis_size(axis)
    return lax.ppermute(value, axis, [(i, i + by) for i in range(n) if 0 <= i + by < n])


def tables():
    k = np.arange(W, dtype=np.int64)
    phase = (k[:, None] * k[None, :] % W).astype(np.float64) * (2.0 * np.pi / W)
    factor = 1.0 / np.sqrt(W)
    re = (np.cos(phase) * factor).astype(np.float32)[:, :Q]
    im = (-np.sin(phase) * factor).astype(np.float32)[:, :Q]
    left = np.stack(
        [
            np.block([[re[j::4], -im[j::4]], [im[j::4], re[j::4]]])
            for j in range(4)
        ]
    ).astype(ml_dtypes.bfloat16)
    pick = np.zeros((W, W), np.float32)
    for j in range(4):
        pick[j * Q + np.arange(Q), 4 * np.arange(Q) + j] = 1.0
    return left, left.transpose(0, 2, 1).copy(), pick.astype(ml_dtypes.bfloat16)


def split4(re, im):
    t0r, t0i, t1r, t1i = re[0] + re[2], im[0] + im[2], re[0] - re[2], im[0] - im[2]
    t2r, t2i, t3r, t3i = re[1] + re[3], im[1] + im[3], re[1] - re[3], im[1] - im[3]
    return (
        (t0r + t2r, t1r + t3i, t0r - t2r, t1r - t3i),
        (t0i + t2i, t1i - t3r, t0i - t2i, t1i + t3r),
    )


def join4(re, im):
    s0r, s0i, s1r, s1i = re[0] + re[2], im[0] + im[2], re[0] - re[2], im[0] - im[2]
    s2r, s2i, s3r, s3i = re[1] + re[3], im[1] + im[3], re[1] - re[3], im[1] - im[3]
    return (
        (s0r + s2r, s1r - s3i, s0r - s2r, s1r + s3i),
        (s0i + s2i, s1i + s3r, s0i - s2i, s1i - s3r),
    )


def lanes(b):
    return pl.ds(b * Q, Q)


def each_rows(count, body):
    def step(i, carry):
        body(pl.multiple_of(i * R, R))
        return carry

    lax.fori_loop(0, count // R, step, 0)


VMEM = pl.BlockSpec(memory_space=pltpu.VMEM)
SMEM = pl.BlockSpec(memory_space=pltpu.SMEM)
ANY = pl.BlockSpec(memory_space=pl.ANY)
TILES = jax.ShapeDtypeStruct((2, NB, E, Q), f32)


def params(mib):
    return pltpu.CompilerParams(vmem_limit_bytes=mib * 2**20)


def cost():
    return pl.CostEstimate(flops=1024, bytes_accessed=1024, transcendentals=0)


def pack_kernel(slab_ref, *refs):
    count = len(CUTS) - 1
    below, right_ref, buf, sem = refs[:count], *refs[count:]
    cuts = (*CUTS, T)

    def copy(c):
        rows = pl.ds(cuts[c], cuts[c + 1] - cuts[c])
        return pltpu.make_async_copy(slab_ref.at[:, rows, :], buf.at[:, rows, :], sem.at[c])

    for c in range(count + 1):
        copy(c).start()
    for c in range(count + 1):
        copy(c).wait()

        def convert(row):
            here = pl.ds(pl.multiple_of(cuts[c] + row, R), R)
            for p in range(2):
                part = buf[p, here, :].astype(bf16)
                right_ref[p, here, :] = part[:, :W]
                if c < count:
                    below[c][p, pl.ds(row, R), :] = part

        each_rows(cuts[c + 1] - cuts[c], convert)


def pack(slab):
    rows = [high - low for low, high in zip(CUTS[:-1], CUTS[1:])]
    shapes = [(2, r, T) for r in rows] + [(2, T, W)]
    made = pl.pallas_call(
        pack_kernel,
        in_specs=[ANY],
        out_specs=[VMEM] * len(shapes),
        out_shape=[jax.ShapeDtypeStruct(shape, bf16) for shape in shapes],
        scratch_shapes=[pltpu.VMEM((2, T, T), f32), pltpu.SemaphoreType.DMA((len(CUTS),))],
        cost_estimate=cost(),
        compiler_params=params(52),
    )(slab)
    return list(made[:-1]), made[-1]


def sort_kernel(pick_ref, pick_t_ref, in_ref, *refs):
    out_ref = refs[-1]
    rows = jnp.dot(pick_ref[...], in_ref[0], preferred_element_type=f32).astype(bf16)
    out_ref[0] = jnp.dot(rows, pick_t_ref[...], preferred_element_type=f32).astype(bf16)


def sort_intensities(measured, pick, *later):
    whole = pl.BlockSpec((W, W), lambda s: (0, 0))
    each = pl.BlockSpec((1, W, W), lambda s: (s, 0, 0))
    return pl.pallas_call(
        sort_kernel,
        grid=(measured.shape[0],),
        in_specs=[whole, whole, each] + [VMEM] * len(later),
        out_specs=each,
        out_shape=jax.ShapeDtypeStruct(measured.shape, bf16),
        cost_estimate=pl.CostEstimate(
            flops=24 * W**3, bytes_accessed=24 * W * W, transcendentals=0
        ),
        compiler_params=params(16),
    )(jnp.asarray(pick), jnp.asarray(pick.T.copy()), measured, *later)


def slots_kernel(
    chunk,
    meta_ref,
    below_ref,
    corner_ref,
    probe_ref,
    meas_ref,
    ga_ref,
    gb_ref,
    first_ref,
    second_ref,
    ext,
    grown,
    half16,
    full32,
    mid,
    out,
    sem,
):
    def copy(p, b):
        return pltpu.make_async_copy(
            first_ref.at[p, :, lanes(b)], ext.at[p, b, pl.ds(0, T), :], sem.at[p, b]
        )

    def clear(row):
        for p in range(2):
            for b in range(NB):
                grown[p, b, pl.ds(row, R), :] = jnp.zeros((R, Q), f32)

    def fill_right(row):
        for p in range(2):
            for b in range(4):
                ext[p, TB + b, pl.ds(row, R), :] = second_ref[p, pl.ds(row, R), lanes(b)].astype(f32)

    if chunk == 0:
        for p in range(2):
            for b in range(TB):
                copy(p, b).start()
        each_rows(E, clear)
        each_rows(T, fill_right)

    def fill(row):
        rows = pl.ds(row, R)
        there = pl.ds(pl.multiple_of(T + CUTS[chunk] + row, R), R)
        for p in range(2):
            for b in range(TB):
                ext[p, b, there, :] = below_ref[p, rows, lanes(b)].astype(f32)
            for b in range(4):
                ext[p, TB + b, there, :] = corner_ref[p, rows, lanes(b)].astype(f32)

    each_rows(CUTS[chunk + 1] - CUTS[chunk], fill)
    if chunk == 0:
        for p in range(2):
            for b in range(TB):
                copy(p, b).wait()

    lane = lax.broadcasted_iota(jnp.int32, (R, Q), 1)

    def one_slot(slot, carry):
        row0 = meta_ref[0, slot]
        col0 = meta_ref[1, slot]
        block0 = col0 // Q
        by = col0 % Q
        inner = lane < Q - by
        outer = lane < by

        def cut(i, c):
            for b in range(4):
                re, im = [], []
                for q in range(4):
                    rows = pl.ds(row0 + q * Q + i * R, R)
                    here = pl.ds(pl.multiple_of(q * Q + i * R, R), R)
                    part = []
                    for p in range(2):
                        one = pltpu.roll(ext[p, block0 + b, rows, :], Q - by, 1)
                        two = pltpu.roll(ext[p, block0 + b + 1, rows, :], Q - by, 1)
                        part.append(jnp.where(inner, one, two))
                    pr, pi = probe_ref[0, here, lanes(b)], probe_ref[1, here, lanes(b)]
                    re.append(pr * part[0] - pi * part[1])
                    im.append(pr * part[1] + pi * part[0])
                re, im = split4(re, im)
                top = pl.ds(pl.multiple_of(i * R, R), R)
                low = pl.ds(pl.multiple_of(Q + i * R, R), R)
                for j in range(4):
                    half16[j, top, lanes(b)] = re[j].astype(bf16)
                    half16[j, low, lanes(b)] = im[j].astype(bf16)
            return c

        lax.fori_loop(0, Q // R, cut, 0)
        for j in range(4):
            full32[j] = jnp.dot(ga_ref[j], half16[j], preferred_element_type=f32)

        def across(i, c):
            top = pl.ds(pl.multiple_of(i * R, R), R)
            low = pl.ds(pl.multiple_of(Q + i * R, R), R)
            for j in range(4):
                re = [full32[j, top, lanes(q)] for q in range(4)]
                im = [full32[j, low, lanes(q)] for q in range(4)]
                re, im = split4(re, im)
                there = pl.ds(pl.multiple_of(j * Q + i * R, R), R)
                for l in range(4):
                    mid[l, there, lanes(0)] = re[l].astype(bf16)
                    mid[l, there, lanes(1)] = im[l].astype(bf16)
            return c

        lax.fori_loop(0, Q // R, across, 0)
        for l in range(4):
            far = jnp.dot(mid[l], gb_ref[l], preferred_element_type=f32)
            re, im = far[:, :Q], far[:, Q:]
            gap = re * re + im * im - meas_ref[slot, :, lanes(l)].astype(f32)
            misfit = jnp.concatenate([gap * re, gap * im], axis=1).astype(bf16)
            out[l] = jnp.dot(misfit, ga_ref[l], preferred_element_type=f32)

        def back(i, c):
            top = pl.ds(pl.multiple_of(i * R, R), R)
            low = pl.ds(pl.multiple_of(Q + i * R, R), R)
            for j in range(4):
                here = pl.ds(pl.multiple_of(j * Q + i * R, R), R)
                re = [out[l, here, lanes(0)] for l in range(4)]
                im = [out[l, here, lanes(1)] for l in range(4)]
                re, im = join4(re, im)
                for q in range(4):
                    half16[j, top, lanes(q)] = re[q].astype(bf16)
                    half16[j, low, lanes(q)] = im[q].astype(bf16)
            return c

        lax.fori_loop(0, Q // R, back, 0)
        for j in range(4):
            full32[j] = jnp.dot(gb_ref[j], half16[j], preferred_element_type=f32)

        def add(i, c):
            top = pl.ds(pl.multiple_of(i * R, R), R)
            low = pl.ds(pl.multiple_of(Q + i * R, R), R)
            last = [[None, None] for q in range(4)]
            for b in range(5):
                if b < 4:
                    re = [full32[j, top, lanes(b)] for j in range(4)]
                    im = [full32[j, low, lanes(b)] for j in range(4)]
                    re, im = join4(re, im)
                for q in range(4):
                    rows = pl.ds(row0 + q * Q + i * R, R)
                    here = pl.ds(pl.multiple_of(q * Q + i * R, R), R)
                    if b < 4:
                        pr, pi = probe_ref[0, here, lanes(b)], probe_ref[1, here, lanes(b)]
                        both = (pr * re[q] + pi * im[q], pr * im[q] - pi * re[q])
                        both = [pltpu.roll(v, by, 1) for v in both]
                    else:
                        both = [jnp.zeros((R, Q), f32)] * 2
                    for p in range(2):
                        before = last[q][p]
                        if before is None:
                            before = jnp.zeros((R, Q), f32)
                        grown[p, block0 + b, rows, :] += jnp.where(outer, before, both[p])
                        last[q][p] = both[p]
            return c

        lax.fori_loop(0, Q // R, add, 0)
        return carry

    def maybe(slot, carry):
        @pl.when(meta_ref[2, slot] == chunk)
        def _():
            one_slot(slot, 0)

        return carry

    lax.fori_loop(0, meta_ref.shape[1], maybe, 0)


def solve(chunk, meta, below, corner, probe, measured, left, left_t, first, second):
    return pl.pallas_call(
        functools.partial(slots_kernel, chunk),
        in_specs=[SMEM] + [VMEM] * 6 + [ANY if chunk == 0 else VMEM, VMEM],
        out_specs=[VMEM, VMEM],
        out_shape=[TILES, TILES],
        input_output_aliases={7: 0, 8: 1} if chunk else {},
        scratch_shapes=[
            pltpu.VMEM((4, 2 * Q, W), bf16),
            pltpu.VMEM((4, 2 * Q, W), f32),
            pltpu.VMEM((4, W, 2 * Q), bf16),
            pltpu.VMEM((4, W, 2 * Q), f32),
            pltpu.SemaphoreType.DMA((2, TB)),
        ],
        cost_estimate=cost(),
        compiler_params=params(12),
    )(meta, below, corner, probe, measured, left, left_t, first, second)


def drain_kernel(grown, near0_ref, near1_ref, far_ref, corner0_ref, corner1_ref, right_ref):
    def below(row):
        rows = pl.ds(row, R)
        here = pl.ds(pl.multiple_of(T + row, R), R)
        for p in range(2):
            for b in range(2):
                near0_ref[p, rows, lanes(b)] = grown[p, b, here, :].astype(bf16)
                near1_ref[p, rows, lanes(b)] = grown[p, 2 + b, here, :].astype(bf16)
                far_ref[p, rows, lanes(b)] = grown[p, 4 + b, here, :].astype(bf16)
                corner0_ref[p, rows, lanes(b)] = grown[p, TB + b, here, :].astype(bf16)
                corner1_ref[p, rows, lanes(b)] = grown[p, TB + 2 + b, here, :].astype(bf16)

    def right(row):
        rows = pl.ds(row, R)
        for p in range(2):
            for b in range(4):
                right_ref[p, rows, lanes(b)] = grown[p, TB + b, rows, :].astype(bf16)

    each_rows(W, below)
    each_rows(T, right)


def drain(grown):
    return pl.pallas_call(
        drain_kernel,
        in_specs=[VMEM],
        out_specs=[VMEM] * 6,
        out_shape=[jax.ShapeDtypeStruct((2, W, 2 * Q), bf16)] * 5
        + [jax.ShapeDtypeStruct((2, T, W), bf16)],
        cost_estimate=cost(),
        compiler_params=params(4),
    )(grown)


def write_copy(tile, whole_ref, sem, p, b, first, count):
    rows = pl.ds(first, count)
    return pltpu.make_async_copy(
        tile.at[p, b, rows, :], whole_ref.at[p, rows, lanes(b)], sem.at[p, b]
    )


def side_kernel(right_ref, far_ref, grown_in, grown, whole_ref, sem):
    def done(p, b):
        if b < 4:
            return write_copy(grown, whole_ref, sem, p, b, W, T - W)
        return write_copy(grown, whole_ref, sem, p, b, 0, T)

    def far(row):
        rows = pl.ds(row, R)
        for p in range(2):
            for b in range(2):
                grown[p, 4 + b, rows, :] += far_ref[p, rows, lanes(b)].astype(f32)

    each_rows(W, far)
    for p in range(2):
        for b in range(4, TB):
            done(p, b).start()

    def right(row):
        rows = pl.ds(row, R)
        for p in range(2):
            for b in range(4):
                grown[p, b, rows, :] += right_ref[p, rows, lanes(b)].astype(f32)

    each_rows(T, right)
    for p in range(2):
        for b in range(4):
            done(p, b).start()
    for p in range(2):
        for b in range(TB):
            done(p, b).wait()


def add_side(right, far, grown):
    return pl.pallas_call(
        side_kernel,
        in_specs=[VMEM] * 3,
        out_specs=[VMEM, ANY],
        out_shape=[TILES, jax.ShapeDtypeStruct((2, T, T), f32)],
        input_output_aliases={2: 0},
        scratch_shapes=[pltpu.SemaphoreType.DMA((2, TB))],
        cost_estimate=cost(),
        compiler_params=params(4),
    )(right, far, grown)


def last_kernel(near0_ref, near1_ref, grown_in, whole_in, grown, whole_ref, sem):
    for b in range(4):
        near_ref = near1_ref if b >= 2 else near0_ref
        for p in range(2):

            def add(row):
                rows = pl.ds(row, R)
                grown[p, b, rows, :] += near_ref[p, rows, lanes(b % 2)].astype(f32)

            each_rows(W, add)
            write_copy(grown, whole_ref, sem, p, b, 0, W).start()
    for b in range(4):
        for p in range(2):
            write_copy(grown, whole_ref, sem, p, b, 0, W).wait()


def add_near(near0, near1, grown, whole):
    return pl.pallas_call(
        last_kernel,
        in_specs=[VMEM, VMEM, VMEM, ANY],
        out_specs=[VMEM, ANY],
        out_shape=[TILES, jax.ShapeDtypeStruct((2, T, T), f32)],
        input_output_aliases={2: 0, 3: 1},
        scratch_shapes=[pltpu.SemaphoreType.DMA((2, 4))],
        cost_estimate=cost(),
        compiler_params=params(4),
    )(near0, near1, grown, whole)[1]


def shards(slab, probe, intensities, offsets, live_count):
    left, left_t, pick = tables()
    left, left_t = jnp.asarray(left), jnp.asarray(left_t)
    chunks = range(len(CUTS) - 1)
    send_below, send_right = pack(slab)
    right = shifted(send_right, "scan", -1)
    measured = sort_intensities(intensities[0, 0], pick, probe, left, left_t)
    live = lax.dynamic_slice(live_count[:, 0], (lax.axis_index("scan"),), (1,))
    shifts = offsets[0, 0].T
    reach = shifts[0] + (W - T)
    stage = sum((reach > CUTS[c + 1]).astype(jnp.int32) for c in chunks)
    stage = jnp.where(jnp.arange(shifts.shape[1], dtype=jnp.int32) < live, stage, len(CUTS))
    meta = jnp.concatenate([shifts, stage[None]], axis=0)
    send_below[1], meta = lax.optimization_barrier((send_below[1], meta))
    below = [shifted(part, "tile", -1) for part in send_below]
    below[0], measured = lax.optimization_barrier((below[0], measured))
    corner = [shifted(part[:, :, :W], "scan", -1) for part in below[:-1]]
    ext, grown = slab, right
    for c in chunks:
        ext, grown = solve(
            c, meta, below[c], corner[c], probe, measured, left, left_t, ext, grown
        )
        if c == 0:
            below[-1], ext, grown = lax.optimization_barrier((below[-1], ext, grown))
            corner.append(shifted(below[-1][:, :, :W], "scan", -1))
    near0, near1, far, corner0, corner1, to_right = drain(grown)
    corner1 = shifted(corner1, "scan", 1)
    far = shifted(far, "tile", 1)
    corner0 = shifted(corner0, "scan", 1)
    near1 = (near1.astype(f32) + corner1.astype(f32)).astype(bf16)
    corner0, near1 = lax.optimization_barrier((corner0, near1))
    near0 = (near0.astype(f32) + corner0.astype(f32)).astype(bf16)
    near1 = shifted(near1, "tile", 1)
    near0, far, to_right = lax.optimization_barrier((near0, far, to_right))
    near0 = shifted(near0, "tile", 1)
    from_left = shifted(to_right, "scan", 1)
    grown, whole = add_side(from_left, far, grown)
    return add_near(near0, near1, grown, whole)


def solution(mesh):
    placed = (
        P(None, "tile", "scan"),
        P(),
        P("scan", "tile", None, None, None),
        P("scan", "tile", None, None),
        P(None, "tile"),
    )
    return jax.shard_map(
        shards, mesh=mesh, in_specs=placed, out_specs=P(None, "tile", "scan"), check_vma=False
    )
```

```python
import functools

import jax
import jax.numpy as jnp
import ml_dtypes
import numpy as np
from jax import lax
from jax.experimental import pallas as pl
from jax.experimental.pallas import tpu as pltpu
from jax.sharding import PartitionSpec as P

W = 512
Q = W // 4
T = 768
E = T + W
NB = E // Q
TB = T // Q
F = T - W
SOLVE_MIB = 24
R = 16
f32, bf16 = jnp.float32, jnp.bfloat16


def shifted(value, axis, by):
    n = lax.axis_size(axis)
    return lax.ppermute(value, axis, [(i, i + by) for i in range(n) if 0 <= i + by < n])


def tables():
    k = np.arange(W, dtype=np.int64)
    phase = (k[:, None] * k[None, :] % W).astype(np.float64) * (2.0 * np.pi / W)
    factor = 1.0 / np.sqrt(W)
    re = (np.cos(phase) * factor).astype(np.float32)[:, :Q]
    im = (-np.sin(phase) * factor).astype(np.float32)[:, :Q]
    left = np.stack(
        [
            np.block([[re[j::4], -im[j::4]], [im[j::4], re[j::4]]])
            for j in range(4)
        ]
    ).astype(ml_dtypes.bfloat16)
    pick = np.zeros((W, W), np.float32)
    for j in range(4):
        pick[j * Q + np.arange(Q), 4 * np.arange(Q) + j] = 1.0
    return left, left.transpose(0, 2, 1).copy(), pick.astype(ml_dtypes.bfloat16)


def split4(re, im):
    t0r, t0i, t1r, t1i = re[0] + re[2], im[0] + im[2], re[0] - re[2], im[0] - im[2]
    t2r, t2i, t3r, t3i = re[1] + re[3], im[1] + im[3], re[1] - re[3], im[1] - im[3]
    return (
        (t0r + t2r, t1r + t3i, t0r - t2r, t1r - t3i),
        (t0i + t2i, t1i - t3r, t0i - t2i, t1i + t3r),
    )


def join4(re, im):
    s0r, s0i, s1r, s1i = re[0] + re[2], im[0] + im[2], re[0] - re[2], im[0] - im[2]
    s2r, s2i, s3r, s3i = re[1] + re[3], im[1] + im[3], re[1] - re[3], im[1] - im[3]
    return (
        (s0r + s2r, s1r - s3i, s0r - s2r, s1r + s3i),
        (s0i + s2i, s1i + s3r, s0i - s2i, s1i - s3r),
    )


def lanes(b):
    return pl.ds(b * Q, Q)


def each_rows(count, body):
    def step(i, carry):
        body(pl.multiple_of(i * R, R))
        return carry

    lax.fori_loop(0, count // R, step, 0)


VMEM = pl.BlockSpec(memory_space=pltpu.VMEM)
SMEM = pl.BlockSpec(memory_space=pltpu.SMEM)
ANY = pl.BlockSpec(memory_space=pl.ANY)
TILES = jax.ShapeDtypeStruct((2, NB, E, Q), f32)


def params(mib):
    return pltpu.CompilerParams(vmem_limit_bytes=mib * 2**20)


def cost():
    return pl.CostEstimate(flops=1024, bytes_accessed=1024, transcendentals=0)


def pack_kernel(slab_ref, near_ref, far_ref, right_ref, buf, sem):
    step = T // 6

    def copy(c):
        rows = pl.ds(c * step, step)
        return pltpu.make_async_copy(slab_ref.at[:, rows, :], buf.at[:, rows, :], sem.at[c])

    for c in range(6):
        copy(c).start()
    for c in range(6):
        copy(c).wait()

        def convert(row):
            here = pl.ds(pl.multiple_of(c * step + row, R), R)
            for p in range(2):
                part = buf[p, here, :].astype(bf16)
                right_ref[p, here, :] = part[:, :W]
                if (c + 1) * step <= W:
                    near_ref[p, here, :] = part[:, :W]
                    far_ref[p, here, :] = part[:, W:]

        each_rows(step, convert)


def pack(slab):
    return pl.pallas_call(
        pack_kernel,
        in_specs=[ANY],
        out_specs=[VMEM] * 3,
        out_shape=[
            jax.ShapeDtypeStruct((2, W, W), bf16),
            jax.ShapeDtypeStruct((2, W, F), bf16),
            jax.ShapeDtypeStruct((2, T, W), bf16),
        ],
        scratch_shapes=[pltpu.VMEM((2, T, T), f32), pltpu.SemaphoreType.DMA((6,))],
        cost_estimate=cost(),
        compiler_params=params(52),
    )(slab)


def sort_kernel(pick_ref, pick_t_ref, in_ref, *refs):
    out_ref = refs[-1]
    rows = jnp.dot(pick_ref[...], in_ref[0], preferred_element_type=f32).astype(bf16)
    out_ref[0] = jnp.dot(rows, pick_t_ref[...], preferred_element_type=f32).astype(bf16)


def sort_intensities(measured, pick, *later):
    whole = pl.BlockSpec((W, W), lambda s: (0, 0))
    each = pl.BlockSpec((1, W, W), lambda s: (s, 0, 0))
    return pl.pallas_call(
        sort_kernel,
        grid=(measured.shape[0],),
        in_specs=[whole, whole, each] + [VMEM] * len(later),
        out_specs=each,
        out_shape=jax.ShapeDtypeStruct(measured.shape, bf16),
        cost_estimate=pl.CostEstimate(
            flops=24 * W**3, bytes_accessed=24 * W * W, transcendentals=0
        ),
        compiler_params=params(16),
    )(jnp.asarray(pick), jnp.asarray(pick.T.copy()), measured, *later)


def slots_kernel(
    live_ref,
    meta_ref,
    slab_ref,
    right_ref,
    near_ref,
    far_ref,
    corner_ref,
    probe_ref,
    meas_ref,
    ga_ref,
    gb_ref,
    grown,
    ext,
    half16,
    full32,
    mid,
    out,
    sem,
):
    def copy(p, b):
        return pltpu.make_async_copy(
            slab_ref.at[p, :, lanes(b)], ext.at[p, b, pl.ds(0, T), :], sem.at[p, b]
        )

    for p in range(2):
        for b in range(TB):
            copy(p, b).start()

    def clear(row):
        for p in range(2):
            for b in range(NB):
                grown[p, b, pl.ds(row, R), :] = jnp.zeros((R, Q), f32)

    def fill_right(row):
        rows = pl.ds(row, R)
        for p in range(2):
            for b in range(4):
                ext[p, TB + b, rows, :] = right_ref[p, rows, lanes(b)].astype(f32)

    def fill_below(row):
        rows = pl.ds(row, R)
        there = pl.ds(pl.multiple_of(T + row, R), R)
        for p in range(2):
            for b in range(4):
                ext[p, b, there, :] = near_ref[p, rows, lanes(b)].astype(f32)
                ext[p, TB + b, there, :] = corner_ref[p, rows, lanes(b)].astype(f32)
            for b in range(2):
                ext[p, 4 + b, there, :] = far_ref[p, rows, lanes(b)].astype(f32)

    each_rows(E, clear)
    each_rows(T, fill_right)
    each_rows(W, fill_below)
    for p in range(2):
        for b in range(TB):
            copy(p, b).wait()

    lane = lax.broadcasted_iota(jnp.int32, (R, Q), 1)

    def one_slot(slot, carry):
        row0 = meta_ref[0, slot]
        col0 = meta_ref[1, slot]
        block0 = col0 // Q
        by = col0 % Q
        inner = lane < Q - by
        outer = lane < by

        def cut(i, c):
            def rolled(q, p, b):
                rows = pl.ds(row0 + q * Q + i * R, R)
                return pltpu.roll(ext[p, block0 + b, rows, :], Q - by, 1)

            last = [[rolled(q, p, 0) for p in range(2)] for q in range(4)]
            for b in range(4):
                re, im = [], []
                for q in range(4):
                    here = pl.ds(pl.multiple_of(q * Q + i * R, R), R)
                    part = []
                    for p in range(2):
                        after = rolled(q, p, b + 1)
                        part.append(jnp.where(inner, last[q][p], after))
                        last[q][p] = after
                    pr, pi = probe_ref[0, here, lanes(b)], probe_ref[1, here, lanes(b)]
                    re.append(pr * part[0] - pi * part[1])
                    im.append(pr * part[1] + pi * part[0])
                re, im = split4(re, im)
                top = pl.ds(pl.multiple_of(i * R, R), R)
                low = pl.ds(pl.multiple_of(Q + i * R, R), R)
                for j in range(4):
                    half16[j, top, lanes(b)] = re[j].astype(bf16)
                    half16[j, low, lanes(b)] = im[j].astype(bf16)
            return c

        lax.fori_loop(0, Q // R, cut, 0, unroll=4)
        for j in range(4):
            full32[j] = jnp.dot(ga_ref[j], half16[j], preferred_element_type=f32)
            for i in range(Q // R):
                top, low = pl.ds(i * R, R), pl.ds(Q + i * R, R)
                re = [full32[j, top, lanes(q)] for q in range(4)]
                im = [full32[j, low, lanes(q)] for q in range(4)]
                re, im = split4(re, im)
                there = pl.ds(j * Q + i * R, R)
                for l in range(4):
                    mid[l, there, lanes(0)] = re[l].astype(bf16)
                    mid[l, there, lanes(1)] = im[l].astype(bf16)

        for l in range(4):
            far = jnp.dot(mid[l], gb_ref[l], preferred_element_type=f32)
            re, im = far[:, :Q], far[:, Q:]
            gap = re * re + im * im - meas_ref[slot, :, lanes(l)].astype(f32)
            misfit = jnp.concatenate([gap * re, gap * im], axis=1).astype(bf16)
            out[l] = jnp.dot(misfit, ga_ref[l], preferred_element_type=f32)

        for j in range(4):
            for i in range(Q // R):
                top, low = pl.ds(i * R, R), pl.ds(Q + i * R, R)
                here = pl.ds(j * Q + i * R, R)
                re = [out[l, here, lanes(0)] for l in range(4)]
                im = [out[l, here, lanes(1)] for l in range(4)]
                re, im = join4(re, im)
                for q in range(4):
                    half16[j, top, lanes(q)] = re[q].astype(bf16)
                    half16[j, low, lanes(q)] = im[q].astype(bf16)
            full32[j] = jnp.dot(gb_ref[j], half16[j], preferred_element_type=f32)

        def add(i, c):
            top = pl.ds(pl.multiple_of(i * R, R), R)
            low = pl.ds(pl.multiple_of(Q + i * R, R), R)
            last = [[None, None] for q in range(4)]
            for b in range(5):
                if b < 4:
                    re = [full32[j, top, lanes(b)] for j in range(4)]
                    im = [full32[j, low, lanes(b)] for j in range(4)]
                    re, im = join4(re, im)
                for q in range(4):
                    rows = pl.ds(row0 + q * Q + i * R, R)
                    here = pl.ds(pl.multiple_of(q * Q + i * R, R), R)
                    if b < 4:
                        pr, pi = probe_ref[0, here, lanes(b)], probe_ref[1, here, lanes(b)]
                        both = (pr * re[q] + pi * im[q], pr * im[q] - pi * re[q])
                        both = [pltpu.roll(v, by, 1) for v in both]
                    else:
                        both = [jnp.zeros((R, Q), f32)] * 2
                    for p in range(2):
                        before = last[q][p]
                        if before is None:
                            before = jnp.zeros((R, Q), f32)
                        grown[p, block0 + b, rows, :] += jnp.where(outer, before, both[p])
                        last[q][p] = both[p]
            return c

        lax.fori_loop(0, Q // R, add, 0, unroll=4)
        return carry

    lax.fori_loop(0, live_ref[0], one_slot, 0)


def solve(live, meta, slab, right, near, far, corner, probe, measured, left, left_t):
    return pl.pallas_call(
        slots_kernel,
        in_specs=[SMEM, SMEM, ANY] + [VMEM] * 8,
        out_specs=VMEM,
        out_shape=TILES,
        scratch_shapes=[
            pltpu.VMEM((2, NB, E, Q), f32),
            pltpu.VMEM((4, 2 * Q, W), bf16),
            pltpu.VMEM((4, 2 * Q, W), f32),
            pltpu.VMEM((4, W, 2 * Q), bf16),
            pltpu.VMEM((4, W, 2 * Q), f32),
            pltpu.SemaphoreType.DMA((2, TB)),
        ],
        cost_estimate=cost(),
        compiler_params=params(SOLVE_MIB),
    )(live, meta, slab, right, near, far, corner, probe, measured, left, left_t)


def drain_kernel(grown, to_near_ref, to_far_ref, to_corner_ref, to_right_ref):
    def drain_below(row):
        rows = pl.ds(row, R)
        here = pl.ds(pl.multiple_of(T + row, R), R)
        for p in range(2):
            for b in range(4):
                to_near_ref[p, rows, lanes(b)] = grown[p, b, here, :].astype(bf16)
                to_corner_ref[p, rows, lanes(b)] = grown[p, TB + b, here, :].astype(bf16)
            for b in range(2):
                to_far_ref[p, rows, lanes(b)] = grown[p, 4 + b, here, :].astype(bf16)

    def drain_right(row):
        rows = pl.ds(row, R)
        for p in range(2):
            for b in range(4):
                to_right_ref[p, rows, lanes(b)] = grown[p, TB + b, rows, :].astype(bf16)

    each_rows(W, drain_below)
    each_rows(T, drain_right)


def drain(grown):
    return pl.pallas_call(
        drain_kernel,
        in_specs=[VMEM],
        out_specs=[VMEM] * 4,
        out_shape=[
            jax.ShapeDtypeStruct((2, W, W), bf16),
            jax.ShapeDtypeStruct((2, W, F), bf16),
            jax.ShapeDtypeStruct((2, W, W), bf16),
            jax.ShapeDtypeStruct((2, T, W), bf16),
        ],
        cost_estimate=cost(),
        compiler_params=params(4),
    )(grown)


def write_copy(tile, whole_ref, sem, p, b, first, count):
    rows = pl.ds(first, count)
    return pltpu.make_async_copy(
        tile.at[p, b, rows, :], whole_ref.at[p, rows, lanes(b)], sem.at[p, b]
    )


def side_kernel(right_ref, far_ref, grown_in, grown, whole_ref, sem):
    def done(p, b):
        if b < 4:
            return write_copy(grown, whole_ref, sem, p, b, W, T - W)
        return write_copy(grown, whole_ref, sem, p, b, 0, T)

    def far(row):
        rows = pl.ds(row, R)
        for p in range(2):
            for b in range(2):
                grown[p, 4 + b, rows, :] += far_ref[p, rows, lanes(b)].astype(f32)

    each_rows(W, far)
    for p in range(2):
        for b in range(4, TB):
            done(p, b).start()

    def right(row):
        rows = pl.ds(row, R)
        for p in range(2):
            for b in range(4):
                grown[p, b, rows, :] += right_ref[p, rows, lanes(b)].astype(f32)

    each_rows(T, right)
    for p in range(2):
        for b in range(4):
            done(p, b).start()
    for p in range(2):
        for b in range(TB):
            done(p, b).wait()


def add_side(right, far, grown):
    return pl.pallas_call(
        side_kernel,
        in_specs=[VMEM] * 3,
        out_specs=[VMEM, ANY],
        out_shape=[TILES, jax.ShapeDtypeStruct((2, T, T), f32)],
        input_output_aliases={2: 0},
        scratch_shapes=[pltpu.SemaphoreType.DMA((2, TB))],
        cost_estimate=cost(),
        compiler_params=params(4),
    )(right, far, grown)


def last_kernel(near_ref, grown_in, whole_in, grown, whole_ref, sem):
    for b in range(4):
        for p in range(2):

            def add(row):
                rows = pl.ds(row, R)
                grown[p, b, rows, :] += near_ref[p, rows, lanes(b)].astype(f32)

            each_rows(W, add)
            write_copy(grown, whole_ref, sem, p, b, 0, W).start()
    for b in range(4):
        for p in range(2):
            write_copy(grown, whole_ref, sem, p, b, 0, W).wait()


def add_near(near, grown, whole):
    return pl.pallas_call(
        last_kernel,
        in_specs=[VMEM, VMEM, ANY],
        out_specs=[VMEM, ANY],
        out_shape=[TILES, jax.ShapeDtypeStruct((2, T, T), f32)],
        input_output_aliases={1: 0, 2: 1},
        scratch_shapes=[pltpu.SemaphoreType.DMA((2, 4))],
        cost_estimate=cost(),
        compiler_params=params(4),
    )(near, grown, whole)[1]


def shards(slab, probe, intensities, offsets, live_count):
    left, left_t, pick = tables()
    left, left_t = jnp.asarray(left), jnp.asarray(left_t)
    near, far, right = pack(slab)
    near = shifted(near, "tile", -1)
    far = shifted(far, "tile", -1)
    right = shifted(right, "scan", -1)
    measured = sort_intensities(intensities[0, 0], pick, probe, left, left_t)
    live = lax.dynamic_slice(live_count[:, 0], (lax.axis_index("scan"),), (1,))
    shifts = offsets[0, 0].T
    near, measured, live, shifts = lax.optimization_barrier((near, measured, live, shifts))
    corner = shifted(near, "scan", -1)
    grown = solve(
        live, shifts, slab, right, near, far, corner, probe, measured, left, left_t
    )
    near, far, corner, right = drain(grown)
    far = shifted(far, "tile", 1)
    corner = shifted(corner, "scan", 1)
    near = (near.astype(f32) + corner.astype(f32)).astype(bf16)
    near = shifted(near, "tile", 1)
    far, right = lax.optimization_barrier((far, right))
    right = shifted(right, "scan", 1)
    grown, whole = add_side(right, far, grown)
    return add_near(near, grown, whole)


def solution(mesh):
    placed = (
        P(None, "tile", "scan"),
        P(),
        P("scan", "tile", None, None, None),
        P("scan", "tile", None, None),
        P(None, "tile"),
    )
    return jax.shard_map(
        shards, mesh=mesh, in_specs=placed, out_specs=P(None, "tile", "scan"), check_vma=False
    )
```

```python
import functools

import jax
import jax.numpy as jnp
import ml_dtypes
import numpy as np
from jax import lax
from jax.experimental import pallas as pl
from jax.experimental.pallas import tpu as pltpu
from jax.sharding import PartitionSpec as P

W = 512
Q = W // 4
T = 768
E = T + W
NB = E // Q
TB = T // Q
F = T - W
SOLVE_MIB = 24
PACK_MIB = 52
R = 16
f32, bf16 = jnp.float32, jnp.bfloat16


def shifted(value, axis, by):
    n = lax.axis_size(axis)
    return lax.ppermute(value, axis, [(i, i + by) for i in range(n) if 0 <= i + by < n])


def tables():
    k = np.arange(W, dtype=np.int64)
    phase = (k[:, None] * k[None, :] % W).astype(np.float64) * (2.0 * np.pi / W)
    factor = 1.0 / np.sqrt(W)
    re = (np.cos(phase) * factor).astype(np.float32)[:, :Q]
    im = (-np.sin(phase) * factor).astype(np.float32)[:, :Q]
    left = np.stack(
        [
            np.block([[re[j::4], -im[j::4]], [im[j::4], re[j::4]]])
            for j in range(4)
        ]
    ).astype(ml_dtypes.bfloat16)
    pick = np.zeros((W, W), np.float32)
    for j in range(4):
        pick[j * Q + np.arange(Q), 4 * np.arange(Q) + j] = 1.0
    return left, left.transpose(0, 2, 1).copy(), pick.astype(ml_dtypes.bfloat16)


def split4(re, im):
    t0r, t0i, t1r, t1i = re[0] + re[2], im[0] + im[2], re[0] - re[2], im[0] - im[2]
    t2r, t2i, t3r, t3i = re[1] + re[3], im[1] + im[3], re[1] - re[3], im[1] - im[3]
    return (
        (t0r + t2r, t1r + t3i, t0r - t2r, t1r - t3i),
        (t0i + t2i, t1i - t3r, t0i - t2i, t1i + t3r),
    )


def join4(re, im):
    s0r, s0i, s1r, s1i = re[0] + re[2], im[0] + im[2], re[0] - re[2], im[0] - im[2]
    s2r, s2i, s3r, s3i = re[1] + re[3], im[1] + im[3], re[1] - re[3], im[1] - im[3]
    return (
        (s0r + s2r, s1r - s3i, s0r - s2r, s1r + s3i),
        (s0i + s2i, s1i + s3r, s0i - s2i, s1i - s3r),
    )


def lanes(b):
    return pl.ds(b * Q, Q)


def each_rows(count, body):
    def step(i, carry):
        body(pl.multiple_of(i * R, R))
        return carry

    lax.fori_loop(0, count // R, step, 0)


VMEM = pl.BlockSpec(memory_space=pltpu.VMEM)
SMEM = pl.BlockSpec(memory_space=pltpu.SMEM)
ANY = pl.BlockSpec(memory_space=pl.ANY)
TILES = jax.ShapeDtypeStruct((2, NB, E, Q), f32)


def params(mib):
    return pltpu.CompilerParams(vmem_limit_bytes=mib * 2**20)


def cost():
    return pl.CostEstimate(flops=1024, bytes_accessed=1024, transcendentals=0)


def pack_kernel(slab_ref, *refs):
    outs, halves, (buf, sem, out_sem) = refs[:4], refs[4:8], refs[8:]
    pieces = 6
    step = T // pieces

    def copy(c):
        rows = pl.ds(c * step, step)
        return pltpu.make_async_copy(slab_ref.at[:, rows, :], buf.at[:, rows, :], sem.at[c])

    def copies_out(c):
        rows = pl.ds(c * step, step)
        return [
            pltpu.make_async_copy(half.at[:, rows, :], o.at[:, rows, :], out_sem.at[c, k])
            for k, (half, o) in enumerate(zip(halves, outs))
            if (c + 1) * step <= o.shape[1]
        ]

    for c in range(pieces):
        copy(c).start()
    for c in range(pieces):
        copy(c).wait()
        for p in range(2):
            for row in range(c * step, (c + 1) * step, 2 * R):
                here = pl.ds(row, 2 * R)
                part = buf[p, here, :].astype(bf16)
                if row < W:
                    halves[0][p, here, :] = part[:, : 2 * Q]
                    halves[1][p, here, :] = part[:, 2 * Q : W]
                    halves[2][p, here, :] = part[:, W:]
                halves[3][p, here, :] = part[:, :W]
        for one in copies_out(c):
            one.start()
    for c in range(pieces):
        for one in copies_out(c):
            one.wait()


def pack(slab):
    shapes = [(2, W, 2 * Q)] * 3 + [(2, T, W)]
    return pl.pallas_call(
        pack_kernel,
        in_specs=[ANY],
        out_specs=[ANY] * 4,
        out_shape=[jax.ShapeDtypeStruct(shape, bf16) for shape in shapes],
        scratch_shapes=[pltpu.VMEM(shape, bf16) for shape in shapes]
        + [
            pltpu.VMEM((2, T, T), f32),
            pltpu.SemaphoreType.DMA((6,)),
            pltpu.SemaphoreType.DMA((6, 4)),
        ],
        cost_estimate=cost(),
        compiler_params=params(PACK_MIB),
    )(slab)


def sort_kernel(pick_ref, pick_t_ref, in_ref, *refs):
    out_ref = refs[-1]
    rows = jnp.dot(pick_ref[...], in_ref[0], preferred_element_type=f32).astype(bf16)
    out_ref[0] = jnp.dot(rows, pick_t_ref[...], preferred_element_type=f32).astype(bf16)


def sort_intensities(measured, pick, *later):
    whole = pl.BlockSpec((W, W), lambda s: (0, 0))
    each = pl.BlockSpec((1, W, W), lambda s: (s, 0, 0))
    return pl.pallas_call(
        sort_kernel,
        grid=(measured.shape[0],),
        in_specs=[whole, whole, each] + [VMEM] * len(later),
        out_specs=each,
        out_shape=jax.ShapeDtypeStruct(measured.shape, bf16),
        cost_estimate=pl.CostEstimate(
            flops=24 * W**3, bytes_accessed=24 * W * W, transcendentals=0
        ),
        compiler_params=params(16),
    )(jnp.asarray(pick), jnp.asarray(pick.T.copy()), measured, *later)


def slots_kernel(
    live_ref,
    meta_ref,
    slab_ref,
    right_ref,
    near0_ref,
    near1_ref,
    far_ref,
    corner0_ref,
    corner1_ref,
    probe_ref,
    meas_ref,
    ga_ref,
    gb_ref,
    grown,
    ext,
    half16,
    full32,
    mid,
    out,
    sem,
):
    def copy(p, b):
        return pltpu.make_async_copy(
            slab_ref.at[p, :, lanes(b)], ext.at[p, b, pl.ds(0, T), :], sem.at[p, b]
        )

    for p in range(2):
        for b in range(TB):
            copy(p, b).start()

    def clear(row):
        for p in range(2):
            for b in range(NB):
                grown[p, b, pl.ds(row, R), :] = jnp.zeros((R, Q), f32)

    def fill_right(row):
        rows = pl.ds(row, R)
        for p in range(2):
            for b in range(4):
                ext[p, TB + b, rows, :] = right_ref[p, rows, lanes(b)].astype(f32)

    def fill_below(row):
        rows = pl.ds(row, R)
        there = pl.ds(pl.multiple_of(T + row, R), R)
        for p in range(2):
            for b in range(2):
                ext[p, b, there, :] = near0_ref[p, rows, lanes(b)].astype(f32)
                ext[p, 2 + b, there, :] = near1_ref[p, rows, lanes(b)].astype(f32)
                ext[p, 4 + b, there, :] = far_ref[p, rows, lanes(b)].astype(f32)
                ext[p, TB + b, there, :] = corner0_ref[p, rows, lanes(b)].astype(f32)
                ext[p, TB + 2 + b, there, :] = corner1_ref[p, rows, lanes(b)].astype(f32)

    each_rows(E, clear)
    each_rows(T, fill_right)
    each_rows(W, fill_below)
    for p in range(2):
        for b in range(TB):
            copy(p, b).wait()

    lane = lax.broadcasted_iota(jnp.int32, (R, Q), 1)

    def one_slot(slot, carry):
        row0 = meta_ref[0, slot]
        col0 = meta_ref[1, slot]
        block0 = col0 // Q
        by = col0 % Q
        inner = lane < Q - by
        outer = lane < by

        def cut(i, c):
            def rolled(q, p, b):
                rows = pl.ds(row0 + q * Q + i * R, R)
                return pltpu.roll(ext[p, block0 + b, rows, :], Q - by, 1)

            last = [[rolled(q, p, 0) for p in range(2)] for q in range(4)]
            for b in range(4):
                re, im = [], []
                for q in range(4):
                    here = pl.ds(pl.multiple_of(q * Q + i * R, R), R)
                    part = []
                    for p in range(2):
                        after = rolled(q, p, b + 1)
                        part.append(jnp.where(inner, last[q][p], after))
                        last[q][p] = after
                    pr, pi = probe_ref[0, here, lanes(b)], probe_ref[1, here, lanes(b)]
                    re.append(pr * part[0] - pi * part[1])
                    im.append(pr * part[1] + pi * part[0])
                re, im = split4(re, im)
                top = pl.ds(pl.multiple_of(i * R, R), R)
                low = pl.ds(pl.multiple_of(Q + i * R, R), R)
                for j in range(4):
                    half16[j, top, lanes(b)] = re[j].astype(bf16)
                    half16[j, low, lanes(b)] = im[j].astype(bf16)
            return c

        lax.fori_loop(0, Q // R, cut, 0, unroll=4)
        for j in range(4):
            full32[j] = jnp.dot(ga_ref[j], half16[j], preferred_element_type=f32)
            for i in range(Q // R):
                top, low = pl.ds(i * R, R), pl.ds(Q + i * R, R)
                re = [full32[j, top, lanes(q)] for q in range(4)]
                im = [full32[j, low, lanes(q)] for q in range(4)]
                re, im = split4(re, im)
                there = pl.ds(j * Q + i * R, R)
                for l in range(4):
                    mid[l, there, lanes(0)] = re[l].astype(bf16)
                    mid[l, there, lanes(1)] = im[l].astype(bf16)

        for l in range(4):
            far = jnp.dot(mid[l], gb_ref[l], preferred_element_type=f32)
            re, im = far[:, :Q], far[:, Q:]
            gap = re * re + im * im - meas_ref[slot, :, lanes(l)].astype(f32)
            misfit = jnp.concatenate([gap * re, gap * im], axis=1).astype(bf16)
            out[l] = jnp.dot(misfit, ga_ref[l], preferred_element_type=f32)

        for j in range(4):
            for i in range(Q // R):
                top, low = pl.ds(i * R, R), pl.ds(Q + i * R, R)
                here = pl.ds(j * Q + i * R, R)
                re = [out[l, here, lanes(0)] for l in range(4)]
                im = [out[l, here, lanes(1)] for l in range(4)]
                re, im = join4(re, im)
                for q in range(4):
                    half16[j, top, lanes(q)] = re[q].astype(bf16)
                    half16[j, low, lanes(q)] = im[q].astype(bf16)
            full32[j] = jnp.dot(gb_ref[j], half16[j], preferred_element_type=f32)

        def add(i, c):
            top = pl.ds(pl.multiple_of(i * R, R), R)
            low = pl.ds(pl.multiple_of(Q + i * R, R), R)
            last = [[None, None] for q in range(4)]
            for b in range(5):
                if b < 4:
                    re = [full32[j, top, lanes(b)] for j in range(4)]
                    im = [full32[j, low, lanes(b)] for j in range(4)]
                    re, im = join4(re, im)
                for q in range(4):
                    rows = pl.ds(row0 + q * Q + i * R, R)
                    here = pl.ds(pl.multiple_of(q * Q + i * R, R), R)
                    if b < 4:
                        pr, pi = probe_ref[0, here, lanes(b)], probe_ref[1, here, lanes(b)]
                        both = (pr * re[q] + pi * im[q], pr * im[q] - pi * re[q])
                        both = [pltpu.roll(v, by, 1) for v in both]
                    else:
                        both = [jnp.zeros((R, Q), f32)] * 2
                    for p in range(2):
                        before = last[q][p]
                        if before is None:
                            before = jnp.zeros((R, Q), f32)
                        grown[p, block0 + b, rows, :] += jnp.where(outer, before, both[p])
                        last[q][p] = both[p]
            return c

        lax.fori_loop(0, Q // R, add, 0, unroll=4)
        return carry

    lax.fori_loop(0, live_ref[0], one_slot, 0)


def solve(live, meta, slab, right, below, corner, probe, measured, left, left_t):
    return pl.pallas_call(
        slots_kernel,
        in_specs=[SMEM, SMEM, ANY] + [VMEM] * 10,
        out_specs=VMEM,
        out_shape=TILES,
        scratch_shapes=[
            pltpu.VMEM((2, NB, E, Q), f32),
            pltpu.VMEM((4, 2 * Q, W), bf16),
            pltpu.VMEM((4, 2 * Q, W), f32),
            pltpu.VMEM((4, W, 2 * Q), bf16),
            pltpu.VMEM((4, W, 2 * Q), f32),
            pltpu.SemaphoreType.DMA((2, TB)),
        ],
        cost_estimate=cost(),
        compiler_params=params(SOLVE_MIB),
    )(live, meta, slab, right, *below, *corner, probe, measured, left, left_t)


def drain_kernel(grown, to_near_ref, to_far_ref, to_corner_ref, to_right_ref):
    def drain_below(row):
        rows = pl.ds(row, R)
        here = pl.ds(pl.multiple_of(T + row, R), R)
        for p in range(2):
            for b in range(4):
                to_near_ref[p, rows, lanes(b)] = grown[p, b, here, :].astype(bf16)
                to_corner_ref[p, rows, lanes(b)] = grown[p, TB + b, here, :].astype(bf16)
            for b in range(2):
                to_far_ref[p, rows, lanes(b)] = grown[p, 4 + b, here, :].astype(bf16)

    def drain_right(row):
        rows = pl.ds(row, R)
        for p in range(2):
            for b in range(4):
                to_right_ref[p, rows, lanes(b)] = grown[p, TB + b, rows, :].astype(bf16)

    each_rows(W, drain_below)
    each_rows(T, drain_right)


def drain(grown):
    return pl.pallas_call(
        drain_kernel,
        in_specs=[VMEM],
        out_specs=[VMEM] * 4,
        out_shape=[
            jax.ShapeDtypeStruct((2, W, W), bf16),
            jax.ShapeDtypeStruct((2, W, F), bf16),
            jax.ShapeDtypeStruct((2, W, W), bf16),
            jax.ShapeDtypeStruct((2, T, W), bf16),
        ],
        cost_estimate=cost(),
        compiler_params=params(4),
    )(grown)


def write_copy(tile, whole_ref, sem, p, b, first, count):
    rows = pl.ds(first, count)
    return pltpu.make_async_copy(
        tile.at[p, b, rows, :], whole_ref.at[p, rows, lanes(b)], sem.at[p, b]
    )


def side_kernel(right_ref, far_ref, grown_in, grown, whole_ref, sem):
    def done(p, b):
        if b < 4:
            return write_copy(grown, whole_ref, sem, p, b, W, T - W)
        return write_copy(grown, whole_ref, sem, p, b, 0, T)

    def far(row):
        rows = pl.ds(row, R)
        for p in range(2):
            for b in range(2):
                grown[p, 4 + b, rows, :] += far_ref[p, rows, lanes(b)].astype(f32)

    each_rows(W, far)
    for p in range(2):
        for b in range(4, TB):
            done(p, b).start()

    def right(row):
        rows = pl.ds(row, R)
        for p in range(2):
            for b in range(4):
                grown[p, b, rows, :] += right_ref[p, rows, lanes(b)].astype(f32)

    each_rows(T, right)
    for p in range(2):
        for b in range(4):
            done(p, b).start()
    for p in range(2):
        for b in range(TB):
            done(p, b).wait()


def add_side(right, far, grown):
    return pl.pallas_call(
        side_kernel,
        in_specs=[VMEM] * 3,
        out_specs=[VMEM, ANY],
        out_shape=[TILES, jax.ShapeDtypeStruct((2, T, T), f32)],
        input_output_aliases={2: 0},
        scratch_shapes=[pltpu.SemaphoreType.DMA((2, TB))],
        cost_estimate=cost(),
        compiler_params=params(4),
    )(right, far, grown)


def last_kernel(near_ref, grown_in, whole_in, grown, whole_ref, sem):
    for b in range(4):
        for p in range(2):

            def add(row):
                rows = pl.ds(row, R)
                grown[p, b, rows, :] += near_ref[p, rows, lanes(b)].astype(f32)

            each_rows(W, add)
            write_copy(grown, whole_ref, sem, p, b, 0, W).start()
    for b in range(4):
        for p in range(2):
            write_copy(grown, whole_ref, sem, p, b, 0, W).wait()


def add_near(near, grown, whole):
    return pl.pallas_call(
        last_kernel,
        in_specs=[VMEM, VMEM, ANY],
        out_specs=[VMEM, ANY],
        out_shape=[TILES, jax.ShapeDtypeStruct((2, T, T), f32)],
        input_output_aliases={1: 0, 2: 1},
        scratch_shapes=[pltpu.SemaphoreType.DMA((2, 4))],
        cost_estimate=cost(),
        compiler_params=params(4),
    )(near, grown, whole)[1]


def shards(slab, probe, intensities, offsets, live_count):
    left, left_t, pick = tables()
    left, left_t = jnp.asarray(left), jnp.asarray(left_t)
    near0, near1, far, right = pack(slab)
    near0 = shifted(near0, "tile", -1)
    near1 = shifted(near1, "tile", -1)
    far = shifted(far, "tile", -1)
    right = shifted(right, "scan", -1)
    measured = sort_intensities(intensities[0, 0], pick, probe, left, left_t)
    live = lax.dynamic_slice(live_count[:, 0], (lax.axis_index("scan"),), (1,))
    shifts = offsets[0, 0].T
    near0, measured, live, shifts = lax.optimization_barrier((near0, measured, live, shifts))
    corner0 = shifted(near0, "scan", -1)
    corner1 = shifted(near1, "scan", -1)
    grown = solve(
        live, shifts, slab, right, (near0, near1, far), (corner0, corner1), probe, measured,
        left, left_t,
    )
    near, far, corner, right = drain(grown)
    far = shifted(far, "tile", 1)
    corner = shifted(corner, "scan", 1)
    near = (near.astype(f32) + corner.astype(f32)).astype(bf16)
    near, far = lax.optimization_barrier((near, far))
    near = shifted(near, "tile", 1)
    right = shifted(right, "scan", 1)
    grown, whole = add_side(right, far, grown)
    return add_near(near, grown, whole)


def solution(mesh):
    placed = (
        P(None, "tile", "scan"),
        P(),
        P("scan", "tile", None, None, None),
        P("scan", "tile", None, None),
        P(None, "tile"),
    )
    return jax.shard_map(
        shards, mesh=mesh, in_specs=placed, out_specs=P(None, "tile", "scan"), check_vma=False
    )
```

```python
import functools

import jax
import jax.numpy as jnp
import ml_dtypes
import numpy as np
from jax import lax
from jax.experimental import pallas as pl
from jax.experimental.pallas import tpu as pltpu
from jax.sharding import PartitionSpec as P

W = 512
Q = W // 4
T = 768
E = T + W
NB = E // Q
TB = T // Q
F = T - W
SOLVE_MIB = 24
RP = 2
PACK_MIB = 52
R = 16
f32, bf16 = jnp.float32, jnp.bfloat16


def shifted(value, axis, by):
    n = lax.axis_size(axis)
    return lax.ppermute(value, axis, [(i, i + by) for i in range(n) if 0 <= i + by < n])


def tables():
    k = np.arange(W, dtype=np.int64)
    phase = (k[:, None] * k[None, :] % W).astype(np.float64) * (2.0 * np.pi / W)
    factor = 1.0 / np.sqrt(W)
    re = (np.cos(phase) * factor).astype(np.float32)[:, :Q]
    im = (-np.sin(phase) * factor).astype(np.float32)[:, :Q]
    left = np.stack(
        [
            np.block([[re[j::4], -im[j::4]], [im[j::4], re[j::4]]])
            for j in range(4)
        ]
    ).astype(ml_dtypes.bfloat16)
    pick = np.zeros((W, W), np.float32)
    for j in range(4):
        pick[j * Q + np.arange(Q), 4 * np.arange(Q) + j] = 1.0
    return left, left.transpose(0, 2, 1).copy(), pick.astype(ml_dtypes.bfloat16)


def split4(re, im):
    t0r, t0i, t1r, t1i = re[0] + re[2], im[0] + im[2], re[0] - re[2], im[0] - im[2]
    t2r, t2i, t3r, t3i = re[1] + re[3], im[1] + im[3], re[1] - re[3], im[1] - im[3]
    return (
        (t0r + t2r, t1r + t3i, t0r - t2r, t1r - t3i),
        (t0i + t2i, t1i - t3r, t0i - t2i, t1i + t3r),
    )


def join4(re, im):
    s0r, s0i, s1r, s1i = re[0] + re[2], im[0] + im[2], re[0] - re[2], im[0] - im[2]
    s2r, s2i, s3r, s3i = re[1] + re[3], im[1] + im[3], re[1] - re[3], im[1] - im[3]
    return (
        (s0r + s2r, s1r - s3i, s0r - s2r, s1r + s3i),
        (s0i + s2i, s1i + s3r, s0i - s2i, s1i - s3r),
    )


def lanes(b):
    return pl.ds(b * Q, Q)


def each_rows(count, body):
    def step(i, carry):
        body(pl.multiple_of(i * R, R))
        return carry

    lax.fori_loop(0, count // R, step, 0)


VMEM = pl.BlockSpec(memory_space=pltpu.VMEM)
SMEM = pl.BlockSpec(memory_space=pltpu.SMEM)
ANY = pl.BlockSpec(memory_space=pl.ANY)
TILES = jax.ShapeDtypeStruct((2, NB, E, Q), f32)


def params(mib):
    return pltpu.CompilerParams(vmem_limit_bytes=mib * 2**20)


def cost():
    return pl.CostEstimate(flops=1024, bytes_accessed=1024, transcendentals=0)


def pack_kernel(slab_ref, *refs):
    outs, halves, (buf, sem, out_sem) = refs[:4], refs[4:8], refs[8:]
    pieces = 6
    step = T // pieces

    def copy(c):
        rows = pl.ds(c * step, step)
        return pltpu.make_async_copy(slab_ref.at[:, rows, :], buf.at[:, rows, :], sem.at[c])

    def copies_out(c):
        rows = pl.ds(c * step, step)
        return [
            pltpu.make_async_copy(half.at[:, rows, :], o.at[:, rows, :], out_sem.at[c, k])
            for k, (half, o) in enumerate(zip(halves, outs))
            if (c + 1) * step <= o.shape[1]
        ]

    for c in range(pieces):
        copy(c).start()
    for c in range(pieces):
        copy(c).wait()
        for p in range(2):
            for row in range(c * step, (c + 1) * step, 2 * R):
                here = pl.ds(row, 2 * R)
                part = buf[p, here, :].astype(bf16)
                if row < W:
                    halves[0][p, here, :] = part[:, : 2 * Q]
                    halves[1][p, here, :] = part[:, 2 * Q : W]
                    halves[2][p, here, :] = part[:, W:]
                halves[3][p, here, :] = part[:, :W]
        for one in copies_out(c):
            one.start()
    for c in range(pieces):
        for one in copies_out(c):
            one.wait()


def pack(slab):
    shapes = [(2, W, 2 * Q)] * 3 + [(2, T, W)]
    return pl.pallas_call(
        pack_kernel,
        in_specs=[ANY],
        out_specs=[ANY] * 4,
        out_shape=[jax.ShapeDtypeStruct(shape, bf16) for shape in shapes],
        scratch_shapes=[pltpu.VMEM(shape, bf16) for shape in shapes]
        + [
            pltpu.VMEM((2, T, T), f32),
            pltpu.SemaphoreType.DMA((6,)),
            pltpu.SemaphoreType.DMA((6, 4)),
        ],
        cost_estimate=cost(),
        compiler_params=params(PACK_MIB),
    )(slab)


def sort_kernel(pick_ref, pick_t_ref, in_ref, *refs):
    out_ref = refs[-1]
    rows = jnp.dot(pick_ref[...], in_ref[0], preferred_element_type=f32).astype(bf16)
    out_ref[0] = jnp.dot(rows, pick_t_ref[...], preferred_element_type=f32).astype(bf16)


def sort_intensities(measured, pick, *later):
    whole = pl.BlockSpec((W, W), lambda s: (0, 0))
    each = pl.BlockSpec((1, W, W), lambda s: (s, 0, 0))
    return pl.pallas_call(
        sort_kernel,
        grid=(measured.shape[0],),
        in_specs=[whole, whole, each] + [VMEM] * len(later),
        out_specs=each,
        out_shape=jax.ShapeDtypeStruct(measured.shape, bf16),
        cost_estimate=pl.CostEstimate(
            flops=24 * W**3, bytes_accessed=24 * W * W, transcendentals=0
        ),
        compiler_params=params(16),
    )(jnp.asarray(pick), jnp.asarray(pick.T.copy()), measured, *later)


def slots_kernel(
    live_ref,
    meta_ref,
    slab_ref,
    right_ref,
    near0_ref,
    near1_ref,
    far_ref,
    corner0_ref,
    corner1_ref,
    probe_ref,
    meas_ref,
    ga_ref,
    gb_ref,
    grown,
    ext,
    half16,
    full32,
    mid,
    out,
    sem,
):
    def copy(p, b):
        return pltpu.make_async_copy(
            slab_ref.at[p, :, lanes(b)], ext.at[p, b, pl.ds(0, T), :], sem.at[p, b]
        )

    for p in range(2):
        for b in range(TB):
            copy(p, b).start()

    def clear(row):
        for p in range(2):
            for b in range(NB):
                grown[p, b, pl.ds(row, R), :] = jnp.zeros((R, Q), f32)

    def fill_right(row):
        rows = pl.ds(row, R)
        for p in range(2):
            for b in range(4):
                ext[p, TB + b, rows, :] = right_ref[p, rows, lanes(b)].astype(f32)

    def fill_below(row):
        rows = pl.ds(row, R)
        there = pl.ds(pl.multiple_of(T + row, R), R)
        for p in range(2):
            for b in range(2):
                ext[p, b, there, :] = near0_ref[p, rows, lanes(b)].astype(f32)
                ext[p, 2 + b, there, :] = near1_ref[p, rows, lanes(b)].astype(f32)
                ext[p, 4 + b, there, :] = far_ref[p, rows, lanes(b)].astype(f32)
                ext[p, TB + b, there, :] = corner0_ref[p, rows, lanes(b)].astype(f32)
                ext[p, TB + 2 + b, there, :] = corner1_ref[p, rows, lanes(b)].astype(f32)

    each_rows(E, clear)
    each_rows(T, fill_right)
    each_rows(W, fill_below)
    for p in range(2):
        for b in range(TB):
            copy(p, b).wait()

    lane = lax.broadcasted_iota(jnp.int32, (R, Q), 1)

    def one_slot(slot, carry):
        row0 = meta_ref[0, slot]
        col0 = meta_ref[1, slot]
        block0 = col0 // Q
        by = col0 % Q
        inner = lane < Q - by
        outer = lane < by

        def cut(i, c):
            def rolled(q, p, b):
                rows = pl.ds(row0 + q * Q + i * R, R)
                return pltpu.roll(ext[p, block0 + b, rows, :], Q - by, 1)

            last = [[rolled(q, p, 0) for p in range(2)] for q in range(4)]
            for b in range(4):
                re, im = [], []
                for q in range(4):
                    here = pl.ds(pl.multiple_of(q * Q + i * R, R), R)
                    part = []
                    for p in range(2):
                        after = rolled(q, p, b + 1)
                        part.append(jnp.where(inner, last[q][p], after))
                        last[q][p] = after
                    pr, pi = probe_ref[0, here, lanes(b)], probe_ref[1, here, lanes(b)]
                    re.append(pr * part[0] - pi * part[1])
                    im.append(pr * part[1] + pi * part[0])
                re, im = split4(re, im)
                top = pl.ds(pl.multiple_of(i * R, R), R)
                low = pl.ds(pl.multiple_of(Q + i * R, R), R)
                for j in range(4):
                    half16[j, top, lanes(b)] = re[j].astype(bf16)
                    half16[j, low, lanes(b)] = im[j].astype(bf16)
            return c

        lax.fori_loop(0, Q // R, cut, 0, unroll=4)
        for j in range(4):
            full32[j] = jnp.dot(ga_ref[j], half16[j], preferred_element_type=f32)
            for i in range(Q // R):
                top, low = pl.ds(i * R, R), pl.ds(Q + i * R, R)
                re = [full32[j, top, lanes(q)] for q in range(4)]
                im = [full32[j, low, lanes(q)] for q in range(4)]
                re, im = split4(re, im)
                there = pl.ds(j * Q + i * R, R)
                for l in range(4):
                    mid[l, there, lanes(0)] = re[l].astype(bf16)
                    mid[l, there, lanes(1)] = im[l].astype(bf16)

        for l in range(4):
            far = jnp.dot(mid[l], gb_ref[l], preferred_element_type=f32)
            re, im = far[:, :Q], far[:, Q:]
            gap = re * re + im * im - meas_ref[slot, :, lanes(l)].astype(f32)
            misfit = jnp.concatenate([gap * re, gap * im], axis=1).astype(bf16)
            out[l] = jnp.dot(misfit, ga_ref[l], preferred_element_type=f32)

        for j in range(4):
            for i in range(Q // R):
                top, low = pl.ds(i * R, R), pl.ds(Q + i * R, R)
                here = pl.ds(j * Q + i * R, R)
                re = [out[l, here, lanes(0)] for l in range(4)]
                im = [out[l, here, lanes(1)] for l in range(4)]
                re, im = join4(re, im)
                for q in range(4):
                    half16[j, top, lanes(q)] = re[q].astype(bf16)
                    half16[j, low, lanes(q)] = im[q].astype(bf16)
            full32[j] = jnp.dot(gb_ref[j], half16[j], preferred_element_type=f32)

        def add(i, c):
            top = pl.ds(pl.multiple_of(i * R, R), R)
            low = pl.ds(pl.multiple_of(Q + i * R, R), R)
            last = [[None, None] for q in range(4)]
            for b in range(5):
                if b < 4:
                    re = [full32[j, top, lanes(b)] for j in range(4)]
                    im = [full32[j, low, lanes(b)] for j in range(4)]
                    re, im = join4(re, im)
                for q in range(4):
                    rows = pl.ds(row0 + q * Q + i * R, R)
                    here = pl.ds(pl.multiple_of(q * Q + i * R, R), R)
                    if b < 4:
                        pr, pi = probe_ref[0, here, lanes(b)], probe_ref[1, here, lanes(b)]
                        both = (pr * re[q] + pi * im[q], pr * im[q] - pi * re[q])
                        both = [pltpu.roll(v, by, 1) for v in both]
                    else:
                        both = [jnp.zeros((R, Q), f32)] * 2
                    for p in range(2):
                        before = last[q][p]
                        if before is None:
                            before = jnp.zeros((R, Q), f32)
                        grown[p, block0 + b, rows, :] += jnp.where(outer, before, both[p])
                        last[q][p] = both[p]
            return c

        lax.fori_loop(0, Q // R, add, 0, unroll=4)
        return carry

    lax.fori_loop(0, live_ref[0], one_slot, 0)


def solve(live, meta, slab, right, below, corner, probe, measured, left, left_t):
    return pl.pallas_call(
        slots_kernel,
        in_specs=[SMEM, SMEM, ANY] + [VMEM] * 10,
        out_specs=VMEM,
        out_shape=TILES,
        scratch_shapes=[
            pltpu.VMEM((2, NB, E, Q), f32),
            pltpu.VMEM((4, 2 * Q, W), bf16),
            pltpu.VMEM((4, 2 * Q, W), f32),
            pltpu.VMEM((4, W, 2 * Q), bf16),
            pltpu.VMEM((4, W, 2 * Q), f32),
            pltpu.SemaphoreType.DMA((2, TB)),
        ],
        cost_estimate=cost(),
        compiler_params=params(SOLVE_MIB),
    )(live, meta, slab, right, *below, *corner, probe, measured, left, left_t)


def drain_kernel(grown, near0_ref, near1_ref, far_ref, corner0_ref, corner1_ref, *right_refs):
    def below(row):
        rows = pl.ds(row, R)
        here = pl.ds(pl.multiple_of(T + row, R), R)
        for p in range(2):
            for b in range(2):
                near0_ref[p, rows, lanes(b)] = grown[p, b, here, :].astype(bf16)
                near1_ref[p, rows, lanes(b)] = grown[p, 2 + b, here, :].astype(bf16)
                far_ref[p, rows, lanes(b)] = grown[p, 4 + b, here, :].astype(bf16)
                corner0_ref[p, rows, lanes(b)] = grown[p, TB + b, here, :].astype(bf16)
                corner1_ref[p, rows, lanes(b)] = grown[p, TB + 2 + b, here, :].astype(bf16)

    def right(row):
        rows = pl.ds(row, R)
        here = pl.ds(pl.multiple_of(piece * (T // RP) + row, R), R)
        for p in range(2):
            for b in range(4):
                right_refs[piece][p, rows, lanes(b)] = grown[p, TB + b, here, :].astype(bf16)

    each_rows(W, below)
    for piece in range(RP):
        each_rows(T // RP, right)


def drain(grown):
    return pl.pallas_call(
        drain_kernel,
        in_specs=[VMEM],
        out_specs=[VMEM] * (5 + RP),
        out_shape=[jax.ShapeDtypeStruct((2, W, 2 * Q), bf16)] * 5
        + [jax.ShapeDtypeStruct((2, T // RP, W), bf16)] * RP,
        cost_estimate=cost(),
        compiler_params=params(4),
    )(grown)


def write_copy(tile, whole_ref, sem, p, b, first, count):
    rows = pl.ds(first, count)
    return pltpu.make_async_copy(
        tile.at[p, b, rows, :], whole_ref.at[p, rows, lanes(b)], sem.at[p, b]
    )


def side_kernel(*refs):
    right_refs, (far_ref, near1_ref, grown_in, grown, whole_ref, sem) = refs[:RP], refs[RP:]

    def done(p, b):
        if b < 2:
            return write_copy(grown, whole_ref, sem, p, b, W, T - W)
        return write_copy(grown, whole_ref, sem, p, b, 0, T)

    for part, first in ((far_ref, 4), (near1_ref, 2)):

        def below(row):
            rows = pl.ds(row, R)
            for p in range(2):
                for b in range(2):
                    grown[p, first + b, rows, :] += part[p, rows, lanes(b)].astype(f32)

        each_rows(W, below)
        if first == 4:
            for p in range(2):
                for b in range(4, TB):
                    done(p, b).start()

    def right(row):
        rows = pl.ds(row, R)
        here = pl.ds(pl.multiple_of(piece * (T // RP) + row, R), R)
        for p in range(2):
            for b in range(4):
                grown[p, b, here, :] += right_refs[piece][p, rows, lanes(b)].astype(f32)

    for piece in range(RP):
        each_rows(T // RP, right)
    for p in range(2):
        for b in range(4):
            done(p, b).start()
    for p in range(2):
        for b in range(TB):
            done(p, b).wait()


def add_side(right, far, near1, grown):
    return pl.pallas_call(
        side_kernel,
        in_specs=[VMEM] * (3 + RP),
        out_specs=[VMEM, ANY],
        out_shape=[TILES, jax.ShapeDtypeStruct((2, T, T), f32)],
        input_output_aliases={2 + RP: 0},
        scratch_shapes=[pltpu.SemaphoreType.DMA((2, TB))],
        cost_estimate=cost(),
        compiler_params=params(4),
    )(*right, far, near1, grown)


def last_kernel(near_ref, grown_in, whole_in, grown, whole_ref, sem):
    for half in range(2):
        for b in range(2):
            for p in range(2):
                for row in range(half * W // 2, (half + 1) * W // 2, 2 * R):
                    rows = pl.ds(row, 2 * R)
                    grown[p, b, rows, :] += near_ref[p, rows, lanes(b)].astype(f32)
                write_copy(grown, whole_ref, sem.at[half], p, b, half * W // 2, W // 2).start()
    for half in range(2):
        for b in range(2):
            for p in range(2):
                write_copy(grown, whole_ref, sem.at[half], p, b, half * W // 2, W // 2).wait()


def add_near(near, grown, whole):
    return pl.pallas_call(
        last_kernel,
        in_specs=[VMEM, VMEM, ANY],
        out_specs=[VMEM, ANY],
        out_shape=[TILES, jax.ShapeDtypeStruct((2, T, T), f32)],
        input_output_aliases={1: 0, 2: 1},
        scratch_shapes=[pltpu.SemaphoreType.DMA((2, 2, 2))],
        cost_estimate=cost(),
        compiler_params=params(4),
    )(near, grown, whole)[1]


def shards(slab, probe, intensities, offsets, live_count):
    left, left_t, pick = tables()
    left, left_t = jnp.asarray(left), jnp.asarray(left_t)
    near0, near1, far, right = pack(slab)
    near0 = shifted(near0, "tile", -1)
    near1 = shifted(near1, "tile", -1)
    far = shifted(far, "tile", -1)
    right = shifted(right, "scan", -1)
    measured = sort_intensities(intensities[0, 0], pick, probe, left, left_t)
    live = lax.dynamic_slice(live_count[:, 0], (lax.axis_index("scan"),), (1,))
    shifts = offsets[0, 0].T
    near0, measured, live, shifts = lax.optimization_barrier((near0, measured, live, shifts))
    corner0 = shifted(near0, "scan", -1)
    corner1 = shifted(near1, "scan", -1)
    grown = solve(
        live, shifts, slab, right, (near0, near1, far), (corner0, corner1), probe, measured,
        left, left_t,
    )
    near0, near1, far, corner0, corner1, *right = drain(grown)
    corner1 = shifted(corner1, "scan", 1)
    far = shifted(far, "tile", 1)
    corner0 = shifted(corner0, "scan", 1)
    near1 = (near1.astype(f32) + corner1.astype(f32)).astype(bf16)
    corner0, near1 = lax.optimization_barrier((corner0, near1))
    near0 = (near0.astype(f32) + corner0.astype(f32)).astype(bf16)
    near1 = shifted(near1, "tile", 1)
    right = [shifted(piece, "scan", 1) for piece in right]
    near0, far = lax.optimization_barrier((near0, far))
    near0 = shifted(near0, "tile", 1)
    grown, whole = add_side(right, far, near1, grown)
    return add_near(near0, grown, whole)


def solution(mesh):
    placed = (
        P(None, "tile", "scan"),
        P(),
        P("scan", "tile", None, None, None),
        P("scan", "tile", None, None),
        P(None, "tile"),
    )
    return jax.shard_map(
        shards, mesh=mesh, in_specs=placed, out_specs=P(None, "tile", "scan"), check_vma=False
    )
```

```python
import functools

import jax
import jax.numpy as jnp
import ml_dtypes
import numpy as np
from jax import lax
from jax.experimental import pallas as pl
from jax.experimental.pallas import tpu as pltpu
from jax.sharding import PartitionSpec as P

W = 512
Q = W // 4
T = 768
E = T + W
NB = E // Q
TB = T // Q
F = T - W
SOLVE_MIB = 24
RP = 2
PACK_MIB = 52
R = 16
f32, bf16 = jnp.float32, jnp.bfloat16


def shifted(value, axis, by):
    n = lax.axis_size(axis)
    return lax.ppermute(value, axis, [(i, i + by) for i in range(n) if 0 <= i + by < n])


def tables():
    k = np.arange(W, dtype=np.int64)
    phase = (k[:, None] * k[None, :] % W).astype(np.float64) * (2.0 * np.pi / W)
    factor = 1.0 / np.sqrt(W)
    re = (np.cos(phase) * factor).astype(np.float32)[:, :Q]
    im = (-np.sin(phase) * factor).astype(np.float32)[:, :Q]
    left = np.stack(
        [
            np.block([[re[j::4], -im[j::4]], [im[j::4], re[j::4]]])
            for j in range(4)
        ]
    ).astype(ml_dtypes.bfloat16)
    pick = np.zeros((W, W), np.float32)
    for j in range(4):
        pick[j * Q + np.arange(Q), 4 * np.arange(Q) + j] = 1.0
    return left, left.transpose(0, 2, 1).copy(), pick.astype(ml_dtypes.bfloat16)


def split4(re, im):
    t0r, t0i, t1r, t1i = re[0] + re[2], im[0] + im[2], re[0] - re[2], im[0] - im[2]
    t2r, t2i, t3r, t3i = re[1] + re[3], im[1] + im[3], re[1] - re[3], im[1] - im[3]
    return (
        (t0r + t2r, t1r + t3i, t0r - t2r, t1r - t3i),
        (t0i + t2i, t1i - t3r, t0i - t2i, t1i + t3r),
    )


def join4(re, im):
    s0r, s0i, s1r, s1i = re[0] + re[2], im[0] + im[2], re[0] - re[2], im[0] - im[2]
    s2r, s2i, s3r, s3i = re[1] + re[3], im[1] + im[3], re[1] - re[3], im[1] - im[3]
    return (
        (s0r + s2r, s1r - s3i, s0r - s2r, s1r + s3i),
        (s0i + s2i, s1i + s3r, s0i - s2i, s1i - s3r),
    )


def lanes(b):
    return pl.ds(b * Q, Q)


def each_rows(count, body):
    def step(i, carry):
        body(pl.multiple_of(i * R, R))
        return carry

    lax.fori_loop(0, count // R, step, 0)


VMEM = pl.BlockSpec(memory_space=pltpu.VMEM)
SMEM = pl.BlockSpec(memory_space=pltpu.SMEM)
ANY = pl.BlockSpec(memory_space=pl.ANY)
TILES = jax.ShapeDtypeStruct((2, NB, E, Q), f32)


def params(mib):
    return pltpu.CompilerParams(vmem_limit_bytes=mib * 2**20)


def cost():
    return pl.CostEstimate(flops=1024, bytes_accessed=1024, transcendentals=0)


def pack_kernel(slab_ref, *refs):
    outs, halves, (buf, sem, out_sem) = refs[: 3 + RP], refs[3 + RP : 6 + 2 * RP], refs[6 + 2 * RP :]
    pieces = 6
    step = T // pieces

    def copy(c):
        rows = pl.ds(c * step, step)
        return pltpu.make_async_copy(slab_ref.at[:, rows, :], buf.at[:, rows, :], sem.at[c])

    def copies_out(c):
        rows = pl.ds(c * step, step)
        made = [
            pltpu.make_async_copy(halves[k].at[:, rows, :], outs[k].at[:, rows, :], out_sem.at[c, k])
            for k in range(3)
            if (c + 1) * step <= W
        ]
        k, row = 3 + c * step // (T // RP), c * step % (T // RP)
        rows = pl.ds(row, step)
        return made + [
            pltpu.make_async_copy(halves[k].at[:, rows, :], outs[k].at[:, rows, :], out_sem.at[c, 3])
        ]

    for c in range(pieces):
        copy(c).start()
    for c in range(pieces):
        copy(c).wait()
        for p in range(2):
            for row in range(c * step, (c + 1) * step, 2 * R):
                here = pl.ds(row, 2 * R)
                part = buf[p, here, :].astype(bf16)
                if row < W:
                    halves[0][p, here, :] = part[:, : 2 * Q]
                    halves[1][p, here, :] = part[:, 2 * Q : W]
                    halves[2][p, here, :] = part[:, W:]
                halves[3 + row // (T // RP)][p, pl.ds(row % (T // RP), 2 * R), :] = part[:, :W]
        for one in copies_out(c):
            one.start()
    for c in range(pieces):
        for one in copies_out(c):
            one.wait()


def pack(slab):
    shapes = [(2, W, 2 * Q)] * 3 + [(2, T // RP, W)] * RP
    return pl.pallas_call(
        pack_kernel,
        in_specs=[ANY],
        out_specs=[ANY] * (3 + RP),
        out_shape=[jax.ShapeDtypeStruct(shape, bf16) for shape in shapes],
        scratch_shapes=[pltpu.VMEM(shape, bf16) for shape in shapes]
        + [
            pltpu.VMEM((2, T, T), f32),
            pltpu.SemaphoreType.DMA((6,)),
            pltpu.SemaphoreType.DMA((6, 4)),
        ],
        cost_estimate=cost(),
        compiler_params=params(PACK_MIB),
    )(slab)


def sort_kernel(pick_ref, pick_t_ref, in_ref, *refs):
    out_ref = refs[-1]
    rows = jnp.dot(pick_ref[...], in_ref[0], preferred_element_type=f32).astype(bf16)
    out_ref[0] = jnp.dot(rows, pick_t_ref[...], preferred_element_type=f32).astype(bf16)


def sort_intensities(measured, pick, *later):
    whole = pl.BlockSpec((W, W), lambda s: (0, 0))
    each = pl.BlockSpec((1, W, W), lambda s: (s, 0, 0))
    return pl.pallas_call(
        sort_kernel,
        grid=(measured.shape[0],),
        in_specs=[whole, whole, each] + [VMEM] * len(later),
        out_specs=each,
        out_shape=jax.ShapeDtypeStruct(measured.shape, bf16),
        cost_estimate=pl.CostEstimate(
            flops=24 * W**3, bytes_accessed=24 * W * W, transcendentals=0
        ),
        compiler_params=params(16),
    )(jnp.asarray(pick), jnp.asarray(pick.T.copy()), measured, *later)


def slots_kernel(
    live_ref,
    meta_ref,
    slab_ref,
    near0_ref,
    near1_ref,
    far_ref,
    corner0_ref,
    corner1_ref,
    probe_ref,
    meas_ref,
    ga_ref,
    gb_ref,
    *refs,
):
    right_refs, refs = refs[:RP], refs[RP:]
    grown, ext, half16, full32, mid, out, sem = refs

    def copy(p, b):
        return pltpu.make_async_copy(
            slab_ref.at[p, :, lanes(b)], ext.at[p, b, pl.ds(0, T), :], sem.at[p, b]
        )

    for p in range(2):
        for b in range(TB):
            copy(p, b).start()

    def clear(row):
        for p in range(2):
            for b in range(NB):
                grown[p, b, pl.ds(row, R), :] = jnp.zeros((R, Q), f32)

    def fill_right(row):
        rows = pl.ds(row, R)
        here = pl.ds(pl.multiple_of(piece * (T // RP) + row, R), R)
        for p in range(2):
            for b in range(4):
                ext[p, TB + b, here, :] = right_refs[piece][p, rows, lanes(b)].astype(f32)

    def fill_below(row):
        rows = pl.ds(row, R)
        there = pl.ds(pl.multiple_of(T + row, R), R)
        for p in range(2):
            for b in range(2):
                ext[p, b, there, :] = near0_ref[p, rows, lanes(b)].astype(f32)
                ext[p, 2 + b, there, :] = near1_ref[p, rows, lanes(b)].astype(f32)
                ext[p, 4 + b, there, :] = far_ref[p, rows, lanes(b)].astype(f32)
                ext[p, TB + b, there, :] = corner0_ref[p, rows, lanes(b)].astype(f32)
                ext[p, TB + 2 + b, there, :] = corner1_ref[p, rows, lanes(b)].astype(f32)

    each_rows(E, clear)
    for piece in range(RP):
        each_rows(T // RP, fill_right)
    each_rows(W, fill_below)
    for p in range(2):
        for b in range(TB):
            copy(p, b).wait()

    lane = lax.broadcasted_iota(jnp.int32, (R, Q), 1)

    def one_slot(slot, carry):
        row0 = meta_ref[0, slot]
        col0 = meta_ref[1, slot]
        block0 = col0 // Q
        by = col0 % Q
        inner = lane < Q - by
        outer = lane < by

        def cut(i, c):
            def rolled(q, p, b):
                rows = pl.ds(row0 + q * Q + i * R, R)
                return pltpu.roll(ext[p, block0 + b, rows, :], Q - by, 1)

            last = [[rolled(q, p, 0) for p in range(2)] for q in range(4)]
            for b in range(4):
                re, im = [], []
                for q in range(4):
                    here = pl.ds(pl.multiple_of(q * Q + i * R, R), R)
                    part = []
                    for p in range(2):
                        after = rolled(q, p, b + 1)
                        part.append(jnp.where(inner, last[q][p], after))
                        last[q][p] = after
                    pr, pi = probe_ref[0, here, lanes(b)], probe_ref[1, here, lanes(b)]
                    re.append(pr * part[0] - pi * part[1])
                    im.append(pr * part[1] + pi * part[0])
                re, im = split4(re, im)
                top = pl.ds(pl.multiple_of(i * R, R), R)
                low = pl.ds(pl.multiple_of(Q + i * R, R), R)
                for j in range(4):
                    half16[j, top, lanes(b)] = re[j].astype(bf16)
                    half16[j, low, lanes(b)] = im[j].astype(bf16)
            return c

        lax.fori_loop(0, Q // R, cut, 0, unroll=4)
        for j in range(4):
            full32[j] = jnp.dot(ga_ref[j], half16[j], preferred_element_type=f32)
            for i in range(Q // R):
                top, low = pl.ds(i * R, R), pl.ds(Q + i * R, R)
                re = [full32[j, top, lanes(q)] for q in range(4)]
                im = [full32[j, low, lanes(q)] for q in range(4)]
                re, im = split4(re, im)
                there = pl.ds(j * Q + i * R, R)
                for l in range(4):
                    mid[l, there, lanes(0)] = re[l].astype(bf16)
                    mid[l, there, lanes(1)] = im[l].astype(bf16)

        for l in range(4):
            far = jnp.dot(mid[l], gb_ref[l], preferred_element_type=f32)
            re, im = far[:, :Q], far[:, Q:]
            gap = re * re + im * im - meas_ref[slot, :, lanes(l)].astype(f32)
            misfit = jnp.concatenate([gap * re, gap * im], axis=1).astype(bf16)
            out[l] = jnp.dot(misfit, ga_ref[l], preferred_element_type=f32)

        for j in range(4):
            for i in range(Q // R):
                top, low = pl.ds(i * R, R), pl.ds(Q + i * R, R)
                here = pl.ds(j * Q + i * R, R)
                re = [out[l, here, lanes(0)] for l in range(4)]
                im = [out[l, here, lanes(1)] for l in range(4)]
                re, im = join4(re, im)
                for q in range(4):
                    half16[j, top, lanes(q)] = re[q].astype(bf16)
                    half16[j, low, lanes(q)] = im[q].astype(bf16)
            full32[j] = jnp.dot(gb_ref[j], half16[j], preferred_element_type=f32)

        def add(i, c):
            top = pl.ds(pl.multiple_of(i * R, R), R)
            low = pl.ds(pl.multiple_of(Q + i * R, R), R)
            last = [[None, None] for q in range(4)]
            for b in range(5):
                if b < 4:
                    re = [full32[j, top, lanes(b)] for j in range(4)]
                    im = [full32[j, low, lanes(b)] for j in range(4)]
                    re, im = join4(re, im)
                for q in range(4):
                    rows = pl.ds(row0 + q * Q + i * R, R)
                    here = pl.ds(pl.multiple_of(q * Q + i * R, R), R)
                    if b < 4:
                        pr, pi = probe_ref[0, here, lanes(b)], probe_ref[1, here, lanes(b)]
                        both = (pr * re[q] + pi * im[q], pr * im[q] - pi * re[q])
                        both = [pltpu.roll(v, by, 1) for v in both]
                    else:
                        both = [jnp.zeros((R, Q), f32)] * 2
                    for p in range(2):
                        before = last[q][p]
                        if before is None:
                            before = jnp.zeros((R, Q), f32)
                        grown[p, block0 + b, rows, :] += jnp.where(outer, before, both[p])
                        last[q][p] = both[p]
            return c

        lax.fori_loop(0, Q // R, add, 0, unroll=4)
        return carry

    lax.fori_loop(0, live_ref[0], one_slot, 0)


def solve(live, meta, slab, right, below, corner, probe, measured, left, left_t):
    return pl.pallas_call(
        slots_kernel,
        in_specs=[SMEM, SMEM, ANY] + [VMEM] * (9 + RP),
        out_specs=VMEM,
        out_shape=TILES,
        scratch_shapes=[
            pltpu.VMEM((2, NB, E, Q), f32),
            pltpu.VMEM((4, 2 * Q, W), bf16),
            pltpu.VMEM((4, 2 * Q, W), f32),
            pltpu.VMEM((4, W, 2 * Q), bf16),
            pltpu.VMEM((4, W, 2 * Q), f32),
            pltpu.SemaphoreType.DMA((2, TB)),
        ],
        cost_estimate=cost(),
        compiler_params=params(SOLVE_MIB),
    )(live, meta, slab, *below, *corner, probe, measured, left, left_t, *right)


def drain_kernel(grown, near0_ref, near1_ref, far_ref, corner0_ref, corner1_ref, *right_refs):
    def below(row):
        rows = pl.ds(row, R)
        here = pl.ds(pl.multiple_of(T + row, R), R)
        for p in range(2):
            for b in range(2):
                near0_ref[p, rows, lanes(b)] = grown[p, b, here, :].astype(bf16)
                near1_ref[p, rows, lanes(b)] = grown[p, 2 + b, here, :].astype(bf16)
                far_ref[p, rows, lanes(b)] = grown[p, 4 + b, here, :].astype(bf16)
                corner0_ref[p, rows, lanes(b)] = grown[p, TB + b, here, :].astype(bf16)
                corner1_ref[p, rows, lanes(b)] = grown[p, TB + 2 + b, here, :].astype(bf16)

    def right(row):
        rows = pl.ds(row, R)
        here = pl.ds(pl.multiple_of(piece * (T // RP) + row, R), R)
        for p in range(2):
            for b in range(4):
                right_refs[piece][p, rows, lanes(b)] = grown[p, TB + b, here, :].astype(bf16)

    each_rows(W, below)
    for piece in range(RP):
        each_rows(T // RP, right)


def drain(grown):
    return pl.pallas_call(
        drain_kernel,
        in_specs=[VMEM],
        out_specs=[VMEM] * (5 + RP),
        out_shape=[jax.ShapeDtypeStruct((2, W, 2 * Q), bf16)] * 5
        + [jax.ShapeDtypeStruct((2, T // RP, W), bf16)] * RP,
        cost_estimate=cost(),
        compiler_params=params(4),
    )(grown)


def write_copy(tile, whole_ref, sem, p, b, first, count):
    rows = pl.ds(first, count)
    return pltpu.make_async_copy(
        tile.at[p, b, rows, :], whole_ref.at[p, rows, lanes(b)], sem.at[p, b]
    )


def side_kernel(*refs):
    right_refs, (far_ref, near1_ref, grown_in, grown, whole_ref, sem) = refs[:RP], refs[RP:]

    def done(p, b):
        if b < 2:
            return write_copy(grown, whole_ref, sem, p, b, W, T - W)
        return write_copy(grown, whole_ref, sem, p, b, 0, T)

    for part, first in ((far_ref, 4), (near1_ref, 2)):

        def below(row):
            rows = pl.ds(row, R)
            for p in range(2):
                for b in range(2):
                    grown[p, first + b, rows, :] += part[p, rows, lanes(b)].astype(f32)

        each_rows(W, below)
        if first == 4:
            for p in range(2):
                for b in range(4, TB):
                    done(p, b).start()

    def right(row):
        rows = pl.ds(row, R)
        here = pl.ds(pl.multiple_of(piece * (T // RP) + row, R), R)
        for p in range(2):
            for b in range(4):
                grown[p, b, here, :] += right_refs[piece][p, rows, lanes(b)].astype(f32)

    for piece in range(RP):
        each_rows(T // RP, right)
    for p in range(2):
        for b in range(4):
            done(p, b).start()
    for p in range(2):
        for b in range(TB):
            done(p, b).wait()


def add_side(right, far, near1, grown):
    return pl.pallas_call(
        side_kernel,
        in_specs=[VMEM] * (3 + RP),
        out_specs=[VMEM, ANY],
        out_shape=[TILES, jax.ShapeDtypeStruct((2, T, T), f32)],
        input_output_aliases={2 + RP: 0},
        scratch_shapes=[pltpu.SemaphoreType.DMA((2, TB))],
        cost_estimate=cost(),
        compiler_params=params(4),
    )(*right, far, near1, grown)


def last_kernel(near_ref, grown_in, whole_in, grown, whole_ref, sem):
    for half in range(2):
        for b in range(2):
            for p in range(2):
                for row in range(half * W // 2, (half + 1) * W // 2, 2 * R):
                    rows = pl.ds(row, 2 * R)
                    grown[p, b, rows, :] += near_ref[p, rows, lanes(b)].astype(f32)
                write_copy(grown, whole_ref, sem.at[half], p, b, half * W // 2, W // 2).start()
    for half in range(2):
        for b in range(2):
            for p in range(2):
                write_copy(grown, whole_ref, sem.at[half], p, b, half * W // 2, W // 2).wait()


def add_near(near, grown, whole):
    return pl.pallas_call(
        last_kernel,
        in_specs=[VMEM, VMEM, ANY],
        out_specs=[VMEM, ANY],
        out_shape=[TILES, jax.ShapeDtypeStruct((2, T, T), f32)],
        input_output_aliases={1: 0, 2: 1},
        scratch_shapes=[pltpu.SemaphoreType.DMA((2, 2, 2))],
        cost_estimate=cost(),
        compiler_params=params(4),
    )(near, grown, whole)[1]


def shards(slab, probe, intensities, offsets, live_count):
    left, left_t, pick = tables()
    left, left_t = jnp.asarray(left), jnp.asarray(left_t)
    near0, near1, far, *right = pack(slab)
    near0 = shifted(near0, "tile", -1)
    near1 = shifted(near1, "tile", -1)
    far = shifted(far, "tile", -1)
    right = [shifted(piece, "scan", -1) for piece in right]
    measured = sort_intensities(intensities[0, 0], pick, probe, left, left_t)
    live = lax.dynamic_slice(live_count[:, 0], (lax.axis_index("scan"),), (1,))
    shifts = offsets[0, 0].T
    near0, measured, live, shifts = lax.optimization_barrier((near0, measured, live, shifts))
    corner0 = shifted(near0, "scan", -1)
    corner1 = shifted(near1, "scan", -1)
    grown = solve(
        live, shifts, slab, right, (near0, near1, far), (corner0, corner1), probe, measured,
        left, left_t,
    )
    near0, near1, far, corner0, corner1, *right = drain(grown)
    corner1 = shifted(corner1, "scan", 1)
    far = shifted(far, "tile", 1)
    corner0 = shifted(corner0, "scan", 1)
    near1 = (near1.astype(f32) + corner1.astype(f32)).astype(bf16)
    near1, *right = lax.optimization_barrier((near1, *right))
    corner0, near1 = lax.optimization_barrier((corner0, near1))
    near0 = (near0.astype(f32) + corner0.astype(f32)).astype(bf16)
    near1 = shifted(near1, "tile", 1)
    right = [shifted(piece, "scan", 1) for piece in right]
    near0, far = lax.optimization_barrier((near0, far))
    near0 = shifted(near0, "tile", 1)
    grown, whole = add_side(right, far, near1, grown)
    return add_near(near0, grown, whole)


def solution(mesh):
    placed = (
        P(None, "tile", "scan"),
        P(),
        P("scan", "tile", None, None, None),
        P("scan", "tile", None, None),
        P(None, "tile"),
    )
    return jax.shard_map(
        shards, mesh=mesh, in_specs=placed, out_specs=P(None, "tile", "scan"), check_vma=False
    )
```

```python
import functools

import jax
import jax.numpy as jnp
import ml_dtypes
import numpy as np
from jax import lax
from jax.experimental import pallas as pl
from jax.experimental.pallas import tpu as pltpu
from jax.sharding import PartitionSpec as P

W = 512
Q = W // 4
T = 768
E = T + W
NB = E // Q
TB = T // Q
F = T - W
SOLVE_MIB = 24
RP = 2
PACK_MIB = 52
R = 16
f32, bf16 = jnp.float32, jnp.bfloat16


def shifted(value, axis, by):
    n = lax.axis_size(axis)
    return lax.ppermute(value, axis, [(i, i + by) for i in range(n) if 0 <= i + by < n])


def tables():
    k = np.arange(W, dtype=np.int64)
    phase = (k[:, None] * k[None, :] % W).astype(np.float64) * (2.0 * np.pi / W)
    factor = 1.0 / np.sqrt(W)
    re = (np.cos(phase) * factor).astype(np.float32)[:, :Q]
    im = (-np.sin(phase) * factor).astype(np.float32)[:, :Q]
    left = np.stack(
        [
            np.block([[re[j::4], -im[j::4]], [im[j::4], re[j::4]]])
            for j in range(4)
        ]
    ).astype(ml_dtypes.bfloat16)
    pick = np.zeros((W, W), np.float32)
    for j in range(4):
        pick[j * Q + np.arange(Q), 4 * np.arange(Q) + j] = 1.0
    return left, left.transpose(0, 2, 1).copy(), pick.astype(ml_dtypes.bfloat16)


def split4(re, im):
    t0r, t0i, t1r, t1i = re[0] + re[2], im[0] + im[2], re[0] - re[2], im[0] - im[2]
    t2r, t2i, t3r, t3i = re[1] + re[3], im[1] + im[3], re[1] - re[3], im[1] - im[3]
    return (
        (t0r + t2r, t1r + t3i, t0r - t2r, t1r - t3i),
        (t0i + t2i, t1i - t3r, t0i - t2i, t1i + t3r),
    )


def join4(re, im):
    s0r, s0i, s1r, s1i = re[0] + re[2], im[0] + im[2], re[0] - re[2], im[0] - im[2]
    s2r, s2i, s3r, s3i = re[1] + re[3], im[1] + im[3], re[1] - re[3], im[1] - im[3]
    return (
        (s0r + s2r, s1r - s3i, s0r - s2r, s1r + s3i),
        (s0i + s2i, s1i + s3r, s0i - s2i, s1i - s3r),
    )


def lanes(b):
    return pl.ds(b * Q, Q)


def each_rows(count, body):
    def step(i, carry):
        body(pl.multiple_of(i * R, R))
        return carry

    lax.fori_loop(0, count // R, step, 0, unroll=4)


VMEM = pl.BlockSpec(memory_space=pltpu.VMEM)
SMEM = pl.BlockSpec(memory_space=pltpu.SMEM)
ANY = pl.BlockSpec(memory_space=pl.ANY)
TILES = jax.ShapeDtypeStruct((2, NB, E, Q), f32)


def params(mib):
    return pltpu.CompilerParams(vmem_limit_bytes=mib * 2**20)


def cost():
    return pl.CostEstimate(flops=1024, bytes_accessed=1024, transcendentals=0)


def pack_kernel(first_row, slab_ref, *refs):
    count = (len(refs) - 3) // 2
    outs, halves, (buf, sem, out_sem) = refs[:count], refs[count : 2 * count], refs[2 * count :]
    step = Q
    width = buf.shape[2]

    def copy(c):
        return pltpu.make_async_copy(
            slab_ref.at[:, pl.ds(first_row + c * step, step), pl.ds(0, width)],
            buf.at[:, pl.ds(c * step, step), :],
            sem.at[c],
        )

    def copy_out(c, k):
        rows = pl.ds(c * step, step)
        return pltpu.make_async_copy(halves[k].at[:, rows, :], outs[k].at[:, rows, :], out_sem.at[c, k])

    steps = range(buf.shape[1] // step)
    for c in steps:
        copy(c).start()
    for c in steps:
        copy(c).wait()
        for p in range(2):
            for row in range(c * step, (c + 1) * step, 2 * R):
                here = pl.ds(row, 2 * R)
                part = buf[p, here, :].astype(bf16)
                for k in range(count):
                    wide = width // count
                    halves[k][p, here, :] = part[:, k * wide : (k + 1) * wide]
        for k in range(count):
            copy_out(c, k).start()
    for c in steps:
        for k in range(count):
            copy_out(c, k).wait()


def pack(slab, first_row, rows, width, count):
    shapes = [(2, rows, width // count)] * count
    return pl.pallas_call(
        functools.partial(pack_kernel, first_row),
        in_specs=[ANY],
        out_specs=[ANY] * count,
        out_shape=[jax.ShapeDtypeStruct(shape, bf16) for shape in shapes],
        scratch_shapes=[pltpu.VMEM(shape, bf16) for shape in shapes]
        + [
            pltpu.VMEM((2, rows, width), f32),
            pltpu.SemaphoreType.DMA((rows // Q,)),
            pltpu.SemaphoreType.DMA((rows // Q, count)),
        ],
        cost_estimate=cost(),
        compiler_params=params(PACK_MIB),
    )(slab)


def sort_kernel(pick_ref, pick_t_ref, in_ref, *refs):
    out_ref = refs[-1]
    rows = jnp.dot(pick_ref[...], in_ref[0], preferred_element_type=f32).astype(bf16)
    out_ref[0] = jnp.dot(rows, pick_t_ref[...], preferred_element_type=f32).astype(bf16)


def sort_intensities(measured, pick, *later):
    whole = pl.BlockSpec((W, W), lambda s: (0, 0))
    each = pl.BlockSpec((1, W, W), lambda s: (s, 0, 0))
    return pl.pallas_call(
        sort_kernel,
        grid=(measured.shape[0],),
        in_specs=[whole, whole, each] + [VMEM] * len(later),
        out_specs=each,
        out_shape=jax.ShapeDtypeStruct(measured.shape, bf16),
        cost_estimate=pl.CostEstimate(
            flops=24 * W**3, bytes_accessed=24 * W * W, transcendentals=0
        ),
        compiler_params=params(16),
    )(jnp.asarray(pick), jnp.asarray(pick.T.copy()), measured, *later)


def slots_kernel(
    live_ref,
    meta_ref,
    slab_ref,
    near0_ref,
    near1_ref,
    far_ref,
    corner0_ref,
    corner1_ref,
    probe_ref,
    meas_ref,
    ga_ref,
    gb_ref,
    *refs,
):
    right_refs, refs = refs[:RP], refs[RP:]
    grown, ext, half16, full32, mid, out, sem = refs

    def copy(p, b):
        return pltpu.make_async_copy(
            slab_ref.at[p, :, lanes(b)], ext.at[p, b, pl.ds(0, T), :], sem.at[p, b]
        )

    for p in range(2):
        for b in range(TB):
            copy(p, b).start()

    def clear(row):
        for p in range(2):
            for b in range(NB):
                grown[p, b, pl.ds(row, R), :] = jnp.zeros((R, Q), f32)

    def fill_right(row):
        rows = pl.ds(row, R)
        here = pl.ds(pl.multiple_of(piece * (T // RP) + row, R), R)
        for p in range(2):
            for b in range(4):
                ext[p, TB + b, here, :] = right_refs[piece][p, rows, lanes(b)].astype(f32)

    def fill_below(row):
        rows = pl.ds(row, R)
        there = pl.ds(pl.multiple_of(T + row, R), R)
        for p in range(2):
            for b in range(2):
                ext[p, b, there, :] = near0_ref[p, rows, lanes(b)].astype(f32)
                ext[p, 2 + b, there, :] = near1_ref[p, rows, lanes(b)].astype(f32)
                ext[p, 4 + b, there, :] = far_ref[p, rows, lanes(b)].astype(f32)
                ext[p, TB + b, there, :] = corner0_ref[p, rows, lanes(b)].astype(f32)
                ext[p, TB + 2 + b, there, :] = corner1_ref[p, rows, lanes(b)].astype(f32)

    each_rows(E, clear)
    for piece in range(RP):
        each_rows(T // RP, fill_right)
    each_rows(W, fill_below)
    for p in range(2):
        for b in range(TB):
            copy(p, b).wait()

    lane = lax.broadcasted_iota(jnp.int32, (R, Q), 1)

    def one_slot(slot, carry):
        row0 = meta_ref[0, slot]
        col0 = meta_ref[1, slot]
        block0 = col0 // Q
        by = col0 % Q
        inner = lane < Q - by
        outer = lane < by

        def cut(i, c):
            def rolled(q, p, b):
                rows = pl.ds(row0 + q * Q + i * R, R)
                return pltpu.roll(ext[p, block0 + b, rows, :], Q - by, 1)

            last = [[rolled(q, p, 0) for p in range(2)] for q in range(4)]
            for b in range(4):
                re, im = [], []
                for q in range(4):
                    here = pl.ds(pl.multiple_of(q * Q + i * R, R), R)
                    part = []
                    for p in range(2):
                        after = rolled(q, p, b + 1)
                        part.append(jnp.where(inner, last[q][p], after))
                        last[q][p] = after
                    pr, pi = probe_ref[0, here, lanes(b)], probe_ref[1, here, lanes(b)]
                    re.append(pr * part[0] - pi * part[1])
                    im.append(pr * part[1] + pi * part[0])
                re, im = split4(re, im)
                top = pl.ds(pl.multiple_of(i * R, R), R)
                low = pl.ds(pl.multiple_of(Q + i * R, R), R)
                for j in range(4):
                    half16[j, top, lanes(b)] = re[j].astype(bf16)
                    half16[j, low, lanes(b)] = im[j].astype(bf16)
            return c

        lax.fori_loop(0, Q // R, cut, 0, unroll=4)
        for j in range(4):
            full32[j] = jnp.dot(ga_ref[j], half16[j], preferred_element_type=f32)
            for i in range(Q // R):
                top, low = pl.ds(i * R, R), pl.ds(Q + i * R, R)
                re = [full32[j, top, lanes(q)] for q in range(4)]
                im = [full32[j, low, lanes(q)] for q in range(4)]
                re, im = split4(re, im)
                there = pl.ds(j * Q + i * R, R)
                for l in range(4):
                    mid[l, there, lanes(0)] = re[l].astype(bf16)
                    mid[l, there, lanes(1)] = im[l].astype(bf16)

        def finish(l, far):
            re, im = far[:, :Q], far[:, Q:]
            gap = re * re + im * im - meas_ref[slot, :, lanes(l)].astype(f32)
            misfit = jnp.concatenate([gap * re, gap * im], axis=1).astype(bf16)
            out[l] = jnp.dot(misfit, ga_ref[l], preferred_element_type=f32)

        fars = []
        for l in range(4):
            fars.append(jnp.dot(mid[l], gb_ref[l], preferred_element_type=f32))
            if l:
                finish(l - 1, fars[l - 1])
        finish(3, fars[3])

        for j in range(4):
            for i in range(Q // R):
                top, low = pl.ds(i * R, R), pl.ds(Q + i * R, R)
                here = pl.ds(j * Q + i * R, R)
                re = [out[l, here, lanes(0)] for l in range(4)]
                im = [out[l, here, lanes(1)] for l in range(4)]
                re, im = join4(re, im)
                for q in range(4):
                    half16[j, top, lanes(q)] = re[q].astype(bf16)
                    half16[j, low, lanes(q)] = im[q].astype(bf16)
            full32[j] = jnp.dot(gb_ref[j], half16[j], preferred_element_type=f32)

        def add(i, c):
            top = pl.ds(pl.multiple_of(i * R, R), R)
            low = pl.ds(pl.multiple_of(Q + i * R, R), R)
            last = [[None, None] for q in range(4)]
            for b in range(5):
                if b < 4:
                    re = [full32[j, top, lanes(b)] for j in range(4)]
                    im = [full32[j, low, lanes(b)] for j in range(4)]
                    re, im = join4(re, im)
                for q in range(4):
                    rows = pl.ds(row0 + q * Q + i * R, R)
                    here = pl.ds(pl.multiple_of(q * Q + i * R, R), R)
                    if b < 4:
                        pr, pi = probe_ref[0, here, lanes(b)], probe_ref[1, here, lanes(b)]
                        both = (pr * re[q] + pi * im[q], pr * im[q] - pi * re[q])
                        both = [pltpu.roll(v, by, 1) for v in both]
                    else:
                        both = [jnp.zeros((R, Q), f32)] * 2
                    for p in range(2):
                        before = last[q][p]
                        if before is None:
                            before = jnp.zeros((R, Q), f32)
                        grown[p, block0 + b, rows, :] += jnp.where(outer, before, both[p])
                        last[q][p] = both[p]
            return c

        lax.fori_loop(0, Q // R, add, 0, unroll=4)
        return carry

    lax.fori_loop(0, live_ref[0], one_slot, 0)


def solve(live, meta, slab, right, below, corner, probe, measured, left, left_t):
    return pl.pallas_call(
        slots_kernel,
        in_specs=[SMEM, SMEM, ANY] + [VMEM] * (9 + RP),
        out_specs=VMEM,
        out_shape=TILES,
        scratch_shapes=[
            pltpu.VMEM((2, NB, E, Q), f32),
            pltpu.VMEM((4, 2 * Q, W), bf16),
            pltpu.VMEM((4, 2 * Q, W), f32),
            pltpu.VMEM((4, W, 2 * Q), bf16),
            pltpu.VMEM((4, W, 2 * Q), f32),
            pltpu.SemaphoreType.DMA((2, TB)),
        ],
        cost_estimate=cost(),
        compiler_params=params(SOLVE_MIB),
    )(live, meta, slab, *below, *corner, probe, measured, left, left_t, *right)


def drain_kernel(grown, near0_ref, near1_ref, far_ref, corner0_ref, corner1_ref, *right_refs):
    def below(row):
        rows = pl.ds(row, R)
        here = pl.ds(pl.multiple_of(T + row, R), R)
        for p in range(2):
            for b in range(2):
                near0_ref[p, rows, lanes(b)] = grown[p, b, here, :].astype(bf16)
                near1_ref[p, rows, lanes(b)] = grown[p, 2 + b, here, :].astype(bf16)
                far_ref[p, rows, lanes(b)] = grown[p, 4 + b, here, :].astype(bf16)
                corner0_ref[p, rows, lanes(b)] = grown[p, TB + b, here, :].astype(bf16)
                corner1_ref[p, rows, lanes(b)] = grown[p, TB + 2 + b, here, :].astype(bf16)

    def right(row):
        rows = pl.ds(row, R)
        here = pl.ds(pl.multiple_of(piece * (T // RP) + row, R), R)
        for p in range(2):
            for b in range(4):
                right_refs[piece][p, rows, lanes(b)] = grown[p, TB + b, here, :].astype(bf16)

    each_rows(W, below)
    for piece in range(RP):
        each_rows(T // RP, right)


def drain(grown):
    return pl.pallas_call(
        drain_kernel,
        in_specs=[VMEM],
        out_specs=[VMEM] * (5 + RP),
        out_shape=[jax.ShapeDtypeStruct((2, W, 2 * Q), bf16)] * 5
        + [jax.ShapeDtypeStruct((2, T // RP, W), bf16)] * RP,
        cost_estimate=cost(),
        compiler_params=params(4),
    )(grown)


def write_copy(tile, whole_ref, sem, p, b, first, count):
    rows = pl.ds(first, count)
    return pltpu.make_async_copy(
        tile.at[p, b, rows, :], whole_ref.at[p, rows, lanes(b)], sem.at[p, b]
    )


def side_kernel(*refs):
    right_refs, (far_ref, near1_ref, grown_in, grown, whole_ref, sem) = refs[:RP], refs[RP:]

    def done(p, b):
        if b < 2:
            return write_copy(grown, whole_ref, sem, p, b, W, T - W)
        return write_copy(grown, whole_ref, sem, p, b, 0, T)

    for part, first in ((far_ref, 4), (near1_ref, 2)):

        def below(row):
            rows = pl.ds(row, R)
            for p in range(2):
                for b in range(2):
                    grown[p, first + b, rows, :] += part[p, rows, lanes(b)].astype(f32)

        each_rows(W, below)
        if first == 4:
            for p in range(2):
                for b in range(4, TB):
                    done(p, b).start()

    def right(row):
        rows = pl.ds(row, R)
        here = pl.ds(pl.multiple_of(piece * (T // RP) + row, R), R)
        for p in range(2):
            for b in range(4):
                grown[p, b, here, :] += right_refs[piece][p, rows, lanes(b)].astype(f32)

    for piece in range(RP):
        each_rows(T // RP, right)
    for p in range(2):
        for b in range(4):
            done(p, b).start()
    for p in range(2):
        for b in range(TB):
            done(p, b).wait()


def add_side(right, far, near1, grown):
    return pl.pallas_call(
        side_kernel,
        in_specs=[VMEM] * (3 + RP),
        out_specs=[VMEM, ANY],
        out_shape=[TILES, jax.ShapeDtypeStruct((2, T, T), f32)],
        input_output_aliases={2 + RP: 0},
        scratch_shapes=[pltpu.SemaphoreType.DMA((2, TB))],
        cost_estimate=cost(),
        compiler_params=params(4),
    )(*right, far, near1, grown)


def last_kernel(near_ref, grown_in, whole_in, grown, whole_ref, sem):
    for half in range(2):
        for b in range(2):
            for p in range(2):
                for row in range(half * W // 2, (half + 1) * W // 2, 2 * R):
                    rows = pl.ds(row, 2 * R)
                    grown[p, b, rows, :] += near_ref[p, rows, lanes(b)].astype(f32)
                write_copy(grown, whole_ref, sem.at[half], p, b, half * W // 2, W // 2).start()
    for half in range(2):
        for b in range(2):
            for p in range(2):
                write_copy(grown, whole_ref, sem.at[half], p, b, half * W // 2, W // 2).wait()


def add_near(near, grown, whole):
    return pl.pallas_call(
        last_kernel,
        in_specs=[VMEM, VMEM, ANY],
        out_specs=[VMEM, ANY],
        out_shape=[TILES, jax.ShapeDtypeStruct((2, T, T), f32)],
        input_output_aliases={1: 0, 2: 1},
        scratch_shapes=[pltpu.SemaphoreType.DMA((2, 2, 2))],
        cost_estimate=cost(),
        compiler_params=params(4),
    )(near, grown, whole)[1]


def shards(slab, probe, intensities, offsets, live_count):
    left, left_t, pick = tables()
    left, left_t = jnp.asarray(left), jnp.asarray(left_t)
    near0, near1, far = pack(slab, 0, W, T, 3)
    right = [pack(slab, piece * (T // RP), T // RP, W, 1)[0] for piece in range(RP)]
    far, right[1] = lax.optimization_barrier((far, right[1]))
    near0 = shifted(near0, "tile", -1)
    near1 = shifted(near1, "tile", -1)
    far = shifted(far, "tile", -1)
    right = [shifted(piece, "scan", -1) for piece in right]
    measured = sort_intensities(intensities[0, 0], pick, probe, left, left_t)
    live = lax.dynamic_slice(live_count[:, 0], (lax.axis_index("scan"),), (1,))
    shifts = offsets[0, 0].T
    near0, live, shifts = lax.optimization_barrier((near0, live, shifts))
    near1, measured = lax.optimization_barrier((near1, measured))
    corner0 = shifted(near0, "scan", -1)
    corner1 = shifted(near1, "scan", -1)
    grown = solve(
        live, shifts, slab, right, (near0, near1, far), (corner0, corner1), probe, measured,
        left, left_t,
    )
    near0, near1, far, corner0, corner1, *right = drain(grown)
    corner1 = shifted(corner1, "scan", 1)
    far = shifted(far, "tile", 1)
    corner0 = shifted(corner0, "scan", 1)
    near1 = (near1.astype(f32) + corner1.astype(f32)).astype(bf16)
    corner0, near1 = lax.optimization_barrier((corner0, near1))
    near0 = (near0.astype(f32) + corner0.astype(f32)).astype(bf16)
    near1 = shifted(near1, "tile", 1)
    right = [shifted(piece, "scan", 1) for piece in right]
    near0, far = lax.optimization_barrier((near0, far))
    near0 = shifted(near0, "tile", 1)
    grown, whole = add_side(right, far, near1, grown)
    return add_near(near0, grown, whole)


def solution(mesh):
    placed = (
        P(None, "tile", "scan"),
        P(),
        P("scan", "tile", None, None, None),
        P("scan", "tile", None, None),
        P(None, "tile"),
    )
    return jax.shard_map(
        shards, mesh=mesh, in_specs=placed, out_specs=P(None, "tile", "scan"), check_vma=False
    )
```

```python
import functools

import jax
import jax.numpy as jnp
import ml_dtypes
import numpy as np
from jax import lax
from jax.experimental import pallas as pl
from jax.experimental.pallas import tpu as pltpu
from jax.sharding import PartitionSpec as P

W = 512
Q = W // 4
T = 768
E = T + W
NB = E // Q
TB = T // Q
F = T - W
SOLVE_MIB = 24
RP = 2
PACK_MIB = 52
R = 16
f32, bf16 = jnp.float32, jnp.bfloat16


def shifted(value, axis, by):
    n = lax.axis_size(axis)
    return lax.ppermute(value, axis, [(i, i + by) for i in range(n) if 0 <= i + by < n])


def tables():
    k = np.arange(W, dtype=np.int64)
    phase = (k[:, None] * k[None, :] % W).astype(np.float64) * (2.0 * np.pi / W)
    factor = 1.0 / np.sqrt(W)
    re = (np.cos(phase) * factor).astype(np.float32)[:, :Q]
    im = (-np.sin(phase) * factor).astype(np.float32)[:, :Q]
    left = np.stack(
        [
            np.block([[re[j::4], -im[j::4]], [im[j::4], re[j::4]]])
            for j in range(4)
        ]
    ).astype(ml_dtypes.bfloat16)
    pick = np.zeros((W, W), np.float32)
    for j in range(4):
        pick[j * Q + np.arange(Q), 4 * np.arange(Q) + j] = 1.0
    return left, left.transpose(0, 2, 1).copy(), pick.astype(ml_dtypes.bfloat16)


def split4(re, im):
    t0r, t0i, t1r, t1i = re[0] + re[2], im[0] + im[2], re[0] - re[2], im[0] - im[2]
    t2r, t2i, t3r, t3i = re[1] + re[3], im[1] + im[3], re[1] - re[3], im[1] - im[3]
    return (
        (t0r + t2r, t1r + t3i, t0r - t2r, t1r - t3i),
        (t0i + t2i, t1i - t3r, t0i - t2i, t1i + t3r),
    )


def join4(re, im):
    s0r, s0i, s1r, s1i = re[0] + re[2], im[0] + im[2], re[0] - re[2], im[0] - im[2]
    s2r, s2i, s3r, s3i = re[1] + re[3], im[1] + im[3], re[1] - re[3], im[1] - im[3]
    return (
        (s0r + s2r, s1r - s3i, s0r - s2r, s1r + s3i),
        (s0i + s2i, s1i + s3r, s0i - s2i, s1i - s3r),
    )


def lanes(b):
    return pl.ds(b * Q, Q)


def each_rows(count, body):
    def step(i, carry):
        body(pl.multiple_of(i * R, R))
        return carry

    lax.fori_loop(0, count // R, step, 0, unroll=4)


VMEM = pl.BlockSpec(memory_space=pltpu.VMEM)
SMEM = pl.BlockSpec(memory_space=pltpu.SMEM)
ANY = pl.BlockSpec(memory_space=pl.ANY)
TILES = jax.ShapeDtypeStruct((2, NB, E, Q), f32)


def params(mib):
    return pltpu.CompilerParams(vmem_limit_bytes=mib * 2**20)


def cost():
    return pl.CostEstimate(flops=1024, bytes_accessed=1024, transcendentals=0)


def pack_kernel(slab_ref, *refs):
    outs, halves, (buf, sem, out_sem) = refs[: 3 + RP], refs[3 + RP : 6 + 2 * RP], refs[6 + 2 * RP :]
    pieces = 6
    step = T // pieces

    def copy(c):
        rows = pl.ds(c * step, step)
        return pltpu.make_async_copy(slab_ref.at[:, rows, :], buf.at[:, rows, :], sem.at[c])

    def copies_out(c):
        rows = pl.ds(c * step, step)
        made = [
            pltpu.make_async_copy(halves[k].at[:, rows, :], outs[k].at[:, rows, :], out_sem.at[c, k])
            for k in range(3)
            if (c + 1) * step <= W
        ]
        k, row = 3 + c * step // (T // RP), c * step % (T // RP)
        rows = pl.ds(row, step)
        return made + [
            pltpu.make_async_copy(halves[k].at[:, rows, :], outs[k].at[:, rows, :], out_sem.at[c, 3])
        ]

    for c in range(pieces):
        copy(c).start()
    for c in range(pieces):
        copy(c).wait()
        for p in range(2):
            for row in range(c * step, (c + 1) * step, 2 * R):
                here = pl.ds(row, 2 * R)
                part = buf[p, here, :].astype(bf16)
                if row < W:
                    halves[0][p, here, :] = part[:, : 2 * Q]
                    halves[1][p, here, :] = part[:, 2 * Q : W]
                    halves[2][p, here, :] = part[:, W:]
                halves[3 + row // (T // RP)][p, pl.ds(row % (T // RP), 2 * R), :] = part[:, :W]
        for one in copies_out(c):
            one.start()
    for c in range(pieces):
        for one in copies_out(c):
            one.wait()


def pack(slab):
    shapes = [(2, W, 2 * Q)] * 3 + [(2, T // RP, W)] * RP
    return pl.pallas_call(
        pack_kernel,
        in_specs=[ANY],
        out_specs=[ANY] * (3 + RP),
        out_shape=[jax.ShapeDtypeStruct(shape, bf16) for shape in shapes],
        scratch_shapes=[pltpu.VMEM(shape, bf16) for shape in shapes]
        + [
            pltpu.VMEM((2, T, T), f32),
            pltpu.SemaphoreType.DMA((6,)),
            pltpu.SemaphoreType.DMA((6, 4)),
        ],
        cost_estimate=cost(),
        compiler_params=params(PACK_MIB),
    )(slab)


def sort_kernel(pick_ref, pick_t_ref, in_ref, *refs):
    out_ref = refs[-1]
    rows = jnp.dot(pick_ref[...], in_ref[0], preferred_element_type=f32).astype(bf16)
    out_ref[0] = jnp.dot(rows, pick_t_ref[...], preferred_element_type=f32).astype(bf16)


def sort_intensities(measured, pick, *later):
    whole = pl.BlockSpec((W, W), lambda s: (0, 0))
    each = pl.BlockSpec((1, W, W), lambda s: (s, 0, 0))
    return pl.pallas_call(
        sort_kernel,
        grid=(measured.shape[0],),
        in_specs=[whole, whole, each] + [VMEM] * len(later),
        out_specs=each,
        out_shape=jax.ShapeDtypeStruct(measured.shape, bf16),
        cost_estimate=pl.CostEstimate(
            flops=24 * W**3, bytes_accessed=24 * W * W, transcendentals=0
        ),
        compiler_params=params(16),
    )(jnp.asarray(pick), jnp.asarray(pick.T.copy()), measured, *later)


def slots_kernel(
    live_ref,
    meta_ref,
    slab_ref,
    near0_ref,
    near1_ref,
    far_ref,
    corner0_ref,
    corner1_ref,
    probe_ref,
    meas_ref,
    ga_ref,
    gb_ref,
    *refs,
):
    right_refs, refs = refs[:RP], refs[RP:]
    grown, ext, half16, full32, mid, out, sem = refs

    def copy(p, b):
        return pltpu.make_async_copy(
            slab_ref.at[p, :, lanes(b)], ext.at[p, b, pl.ds(0, T), :], sem.at[p, b]
        )

    for p in range(2):
        for b in range(TB):
            copy(p, b).start()

    def clear(row):
        for p in range(2):
            for b in range(NB):
                grown[p, b, pl.ds(row, R), :] = jnp.zeros((R, Q), f32)

    def fill_right(row):
        rows = pl.ds(row, R)
        here = pl.ds(pl.multiple_of(piece * (T // RP) + row, R), R)
        for p in range(2):
            for b in range(4):
                ext[p, TB + b, here, :] = right_refs[piece][p, rows, lanes(b)].astype(f32)

    def fill_below(row):
        rows = pl.ds(row, R)
        there = pl.ds(pl.multiple_of(T + row, R), R)
        for p in range(2):
            for b in range(2):
                ext[p, b, there, :] = near0_ref[p, rows, lanes(b)].astype(f32)
                ext[p, 2 + b, there, :] = near1_ref[p, rows, lanes(b)].astype(f32)
                ext[p, 4 + b, there, :] = far_ref[p, rows, lanes(b)].astype(f32)
                ext[p, TB + b, there, :] = corner0_ref[p, rows, lanes(b)].astype(f32)
                ext[p, TB + 2 + b, there, :] = corner1_ref[p, rows, lanes(b)].astype(f32)

    each_rows(E, clear)
    for piece in range(RP):
        each_rows(T // RP, fill_right)
    each_rows(W, fill_below)
    for p in range(2):
        for b in range(TB):
            copy(p, b).wait()

    lane = lax.broadcasted_iota(jnp.int32, (R, Q), 1)

    def one_slot(slot, carry):
        row0 = meta_ref[0, slot]
        col0 = meta_ref[1, slot]
        block0 = col0 // Q
        by = col0 % Q
        inner = lane < Q - by
        outer = lane < by

        def cut(i, c):
            def rolled(q, p, b):
                rows = pl.ds(row0 + q * Q + i * R, R)
                return pltpu.roll(ext[p, block0 + b, rows, :], Q - by, 1)

            last = [[rolled(q, p, 0) for p in range(2)] for q in range(4)]
            for b in range(4):
                re, im = [], []
                for q in range(4):
                    here = pl.ds(pl.multiple_of(q * Q + i * R, R), R)
                    part = []
                    for p in range(2):
                        after = rolled(q, p, b + 1)
                        part.append(jnp.where(inner, last[q][p], after))
                        last[q][p] = after
                    pr, pi = probe_ref[0, here, lanes(b)], probe_ref[1, here, lanes(b)]
                    re.append(pr * part[0] - pi * part[1])
                    im.append(pr * part[1] + pi * part[0])
                re, im = split4(re, im)
                top = pl.ds(pl.multiple_of(i * R, R), R)
                low = pl.ds(pl.multiple_of(Q + i * R, R), R)
                for j in range(4):
                    half16[j, top, lanes(b)] = re[j].astype(bf16)
                    half16[j, low, lanes(b)] = im[j].astype(bf16)
            return c

        lax.fori_loop(0, Q // R, cut, 0, unroll=4)
        for j in range(4):
            full32[j] = jnp.dot(ga_ref[j], half16[j], preferred_element_type=f32)
            for i in range(Q // R):
                top, low = pl.ds(i * R, R), pl.ds(Q + i * R, R)
                re = [full32[j, top, lanes(q)] for q in range(4)]
                im = [full32[j, low, lanes(q)] for q in range(4)]
                re, im = split4(re, im)
                there = pl.ds(j * Q + i * R, R)
                for l in range(4):
                    mid[l, there, lanes(0)] = re[l].astype(bf16)
                    mid[l, there, lanes(1)] = im[l].astype(bf16)

        def finish(l, far):
            re, im = far[:, :Q], far[:, Q:]
            gap = re * re + im * im - meas_ref[slot, :, lanes(l)].astype(f32)
            misfit = jnp.concatenate([gap * re, gap * im], axis=1).astype(bf16)
            out[l] = jnp.dot(misfit, ga_ref[l], preferred_element_type=f32)

        fars = []
        for l in range(4):
            fars.append(jnp.dot(mid[l], gb_ref[l], preferred_element_type=f32))
            if l:
                finish(l - 1, fars[l - 1])
        finish(3, fars[3])

        for j in range(4):
            for i in range(Q // R):
                top, low = pl.ds(i * R, R), pl.ds(Q + i * R, R)
                here = pl.ds(j * Q + i * R, R)
                re = [out[l, here, lanes(0)] for l in range(4)]
                im = [out[l, here, lanes(1)] for l in range(4)]
                re, im = join4(re, im)
                for q in range(4):
                    half16[j, top, lanes(q)] = re[q].astype(bf16)
                    half16[j, low, lanes(q)] = im[q].astype(bf16)
            full32[j] = jnp.dot(gb_ref[j], half16[j], preferred_element_type=f32)

        def add(i, c):
            top = pl.ds(pl.multiple_of(i * R, R), R)
            low = pl.ds(pl.multiple_of(Q + i * R, R), R)
            last = [[None, None] for q in range(4)]
            for b in range(5):
                if b < 4:
                    re = [full32[j, top, lanes(b)] for j in range(4)]
                    im = [full32[j, low, lanes(b)] for j in range(4)]
                    re, im = join4(re, im)
                for q in range(4):
                    rows = pl.ds(row0 + q * Q + i * R, R)
                    here = pl.ds(pl.multiple_of(q * Q + i * R, R), R)
                    if b < 4:
                        pr, pi = probe_ref[0, here, lanes(b)], probe_ref[1, here, lanes(b)]
                        both = (pr * re[q] + pi * im[q], pr * im[q] - pi * re[q])
                        both = [pltpu.roll(v, by, 1) for v in both]
                    else:
                        both = [jnp.zeros((R, Q), f32)] * 2
                    for p in range(2):
                        before = last[q][p]
                        if before is None:
                            before = jnp.zeros((R, Q), f32)
                        grown[p, block0 + b, rows, :] += jnp.where(outer, before, both[p])
                        last[q][p] = both[p]
            return c

        lax.fori_loop(0, Q // R, add, 0, unroll=4)
        return carry

    lax.fori_loop(0, live_ref[0], one_slot, 0)


def solve(live, meta, slab, right, below, corner, probe, measured, left, left_t):
    return pl.pallas_call(
        slots_kernel,
        in_specs=[SMEM, SMEM, ANY] + [VMEM] * (9 + RP),
        out_specs=VMEM,
        out_shape=TILES,
        scratch_shapes=[
            pltpu.VMEM((2, NB, E, Q), f32),
            pltpu.VMEM((4, 2 * Q, W), bf16),
            pltpu.VMEM((4, 2 * Q, W), f32),
            pltpu.VMEM((4, W, 2 * Q), bf16),
            pltpu.VMEM((4, W, 2 * Q), f32),
            pltpu.SemaphoreType.DMA((2, TB)),
        ],
        cost_estimate=cost(),
        compiler_params=params(SOLVE_MIB),
    )(live, meta, slab, *below, *corner, probe, measured, left, left_t, *right)


def drain_kernel(grown, near0_ref, near1_ref, far_ref, corner0_ref, corner1_ref, *right_refs):
    def below(row):
        rows = pl.ds(row, R)
        here = pl.ds(pl.multiple_of(T + row, R), R)
        for p in range(2):
            for b in range(2):
                near0_ref[p, rows, lanes(b)] = grown[p, b, here, :].astype(bf16)
                near1_ref[p, rows, lanes(b)] = grown[p, 2 + b, here, :].astype(bf16)
                far_ref[p, rows, lanes(b)] = grown[p, 4 + b, here, :].astype(bf16)
                corner0_ref[p, rows, lanes(b)] = grown[p, TB + b, here, :].astype(bf16)
                corner1_ref[p, rows, lanes(b)] = grown[p, TB + 2 + b, here, :].astype(bf16)

    def right(row):
        rows = pl.ds(row, R)
        here = pl.ds(pl.multiple_of(piece * (T // RP) + row, R), R)
        for p in range(2):
            for b in range(4):
                right_refs[piece][p, rows, lanes(b)] = grown[p, TB + b, here, :].astype(bf16)

    each_rows(W, below)
    for piece in range(RP):
        each_rows(T // RP, right)


def drain(grown):
    return pl.pallas_call(
        drain_kernel,
        in_specs=[VMEM],
        out_specs=[VMEM] * (5 + RP),
        out_shape=[jax.ShapeDtypeStruct((2, W, 2 * Q), bf16)] * 5
        + [jax.ShapeDtypeStruct((2, T // RP, W), bf16)] * RP,
        cost_estimate=cost(),
        compiler_params=params(4),
    )(grown)


def write_copy(tile, whole_ref, sem, p, b, first, count):
    rows = pl.ds(first, count)
    return pltpu.make_async_copy(
        tile.at[p, b, rows, :], whole_ref.at[p, rows, lanes(b)], sem.at[p, b]
    )


def side_kernel(*refs):
    right_refs, (far_ref, near1_ref, grown_in, grown, whole_ref, sem) = refs[:RP], refs[RP:]

    def done(p, b):
        if b < 2:
            return write_copy(grown, whole_ref, sem, p, b, W, T - W)
        return write_copy(grown, whole_ref, sem, p, b, 0, T)

    for part, first in ((far_ref, 4), (near1_ref, 2)):

        def below(row):
            rows = pl.ds(row, R)
            for p in range(2):
                for b in range(2):
                    grown[p, first + b, rows, :] += part[p, rows, lanes(b)].astype(f32)

        each_rows(W, below)
        if first == 4:
            for p in range(2):
                for b in range(4, TB):
                    done(p, b).start()

    def right(row):
        rows = pl.ds(row, R)
        here = pl.ds(pl.multiple_of(piece * (T // RP) + row, R), R)
        for p in range(2):
            for b in range(4):
                grown[p, b, here, :] += right_refs[piece][p, rows, lanes(b)].astype(f32)

    for piece in range(RP):
        each_rows(T // RP, right)
    for p in range(2):
        for b in range(4):
            done(p, b).start()
    for p in range(2):
        for b in range(TB):
            done(p, b).wait()


def add_side(right, far, near1, grown):
    return pl.pallas_call(
        side_kernel,
        in_specs=[VMEM] * (3 + RP),
        out_specs=[VMEM, ANY],
        out_shape=[TILES, jax.ShapeDtypeStruct((2, T, T), f32)],
        input_output_aliases={2 + RP: 0},
        scratch_shapes=[pltpu.SemaphoreType.DMA((2, TB))],
        cost_estimate=cost(),
        compiler_params=params(4),
    )(*right, far, near1, grown)


def last_kernel(near_ref, grown_in, whole_in, grown, whole_ref, sem):
    for half in range(2):
        for b in range(2):
            for p in range(2):
                for row in range(half * W // 2, (half + 1) * W // 2, 2 * R):
                    rows = pl.ds(row, 2 * R)
                    grown[p, b, rows, :] += near_ref[p, rows, lanes(b)].astype(f32)
                write_copy(grown, whole_ref, sem.at[half], p, b, half * W // 2, W // 2).start()
    for half in range(2):
        for b in range(2):
            for p in range(2):
                write_copy(grown, whole_ref, sem.at[half], p, b, half * W // 2, W // 2).wait()


def add_near(near, grown, whole):
    return pl.pallas_call(
        last_kernel,
        in_specs=[VMEM, VMEM, ANY],
        out_specs=[VMEM, ANY],
        out_shape=[TILES, jax.ShapeDtypeStruct((2, T, T), f32)],
        input_output_aliases={1: 0, 2: 1},
        scratch_shapes=[pltpu.SemaphoreType.DMA((2, 2, 2))],
        cost_estimate=cost(),
        compiler_params=params(4),
    )(near, grown, whole)[1]


def shards(slab, probe, intensities, offsets, live_count):
    left, left_t, pick = tables()
    left, left_t = jnp.asarray(left), jnp.asarray(left_t)
    near0, near1, far, *right = pack(slab)
    near0 = shifted(near0, "tile", -1)
    near1 = shifted(near1, "tile", -1)
    far = shifted(far, "tile", -1)
    right = [shifted(piece, "scan", -1) for piece in right]
    live = lax.dynamic_slice(live_count[:, 0], (lax.axis_index("scan"),), (1,))
    shifts = offsets[0, 0].T
    near0, live, shifts, intensities = lax.optimization_barrier(
        (near0, live, shifts, intensities)
    )
    measured = sort_intensities(intensities[0, 0], pick, probe, left, left_t)
    near1, measured = lax.optimization_barrier((near1, measured))
    corner0 = shifted(near0, "scan", -1)
    corner1 = shifted(near1, "scan", -1)
    grown = solve(
        live, shifts, slab, right, (near0, near1, far), (corner0, corner1), probe, measured,
        left, left_t,
    )
    near0, near1, far, corner0, corner1, *right = drain(grown)
    corner1 = shifted(corner1, "scan", 1)
    far = shifted(far, "tile", 1)
    corner0 = shifted(corner0, "scan", 1)
    near1 = (near1.astype(f32) + corner1.astype(f32)).astype(bf16)
    corner0, near1 = lax.optimization_barrier((corner0, near1))
    near0 = (near0.astype(f32) + corner0.astype(f32)).astype(bf16)
    near1 = shifted(near1, "tile", 1)
    right = [shifted(piece, "scan", 1) for piece in right]
    near0, far = lax.optimization_barrier((near0, far))
    near0 = shifted(near0, "tile", 1)
    grown, whole = add_side(right, far, near1, grown)
    return add_near(near0, grown, whole)


def solution(mesh):
    placed = (
        P(None, "tile", "scan"),
        P(),
        P("scan", "tile", None, None, None),
        P("scan", "tile", None, None),
        P(None, "tile"),
    )
    return jax.shard_map(
        shards, mesh=mesh, in_specs=placed, out_specs=P(None, "tile", "scan"), check_vma=False
    )
```

```python
import functools

import jax
import jax.numpy as jnp
import ml_dtypes
import numpy as np
from jax import lax
from jax.experimental import pallas as pl
from jax.experimental.pallas import tpu as pltpu
from jax.sharding import PartitionSpec as P

W = 512
Q = W // 4
T = 768
E = T + W
NB = E // Q
TB = T // Q
F = T - W
SOLVE_MIB = 24
RP = 2
PACK_MIB = 52
R = 16
f32, bf16 = jnp.float32, jnp.bfloat16


def shifted(value, axis, by):
    n = lax.axis_size(axis)
    return lax.ppermute(value, axis, [(i, i + by) for i in range(n) if 0 <= i + by < n])


def tables():
    k = np.arange(W, dtype=np.int64)
    phase = (k[:, None] * k[None, :] % W).astype(np.float64) * (2.0 * np.pi / W)
    factor = 1.0 / np.sqrt(W)
    re = (np.cos(phase) * factor).astype(np.float32)[:, :Q]
    im = (-np.sin(phase) * factor).astype(np.float32)[:, :Q]
    left = np.stack(
        [
            np.block([[re[j::4], -im[j::4]], [im[j::4], re[j::4]]])
            for j in range(4)
        ]
    ).astype(ml_dtypes.bfloat16)
    pick = np.zeros((W, W), np.float32)
    for j in range(4):
        pick[j * Q + np.arange(Q), 4 * np.arange(Q) + j] = 1.0
    return left, left.transpose(0, 2, 1).copy(), pick.astype(ml_dtypes.bfloat16)


def split4(re, im):
    t0r, t0i, t1r, t1i = re[0] + re[2], im[0] + im[2], re[0] - re[2], im[0] - im[2]
    t2r, t2i, t3r, t3i = re[1] + re[3], im[1] + im[3], re[1] - re[3], im[1] - im[3]
    return (
        (t0r + t2r, t1r + t3i, t0r - t2r, t1r - t3i),
        (t0i + t2i, t1i - t3r, t0i - t2i, t1i + t3r),
    )


def join4(re, im):
    s0r, s0i, s1r, s1i = re[0] + re[2], im[0] + im[2], re[0] - re[2], im[0] - im[2]
    s2r, s2i, s3r, s3i = re[1] + re[3], im[1] + im[3], re[1] - re[3], im[1] - im[3]
    return (
        (s0r + s2r, s1r - s3i, s0r - s2r, s1r + s3i),
        (s0i + s2i, s1i + s3r, s0i - s2i, s1i - s3r),
    )


def lanes(b):
    return pl.ds(b * Q, Q)


def each_rows(count, body):
    def step(i, carry):
        body(pl.multiple_of(i * R, R))
        return carry

    lax.fori_loop(0, count // R, step, 0, unroll=4)


VMEM = pl.BlockSpec(memory_space=pltpu.VMEM)
SMEM = pl.BlockSpec(memory_space=pltpu.SMEM)
ANY = pl.BlockSpec(memory_space=pl.ANY)
TILES = jax.ShapeDtypeStruct((2, NB, E, Q), f32)


def params(mib):
    return pltpu.CompilerParams(vmem_limit_bytes=mib * 2**20)


def cost():
    return pl.CostEstimate(flops=1024, bytes_accessed=1024, transcendentals=0)


def pack_kernel(slab_ref, *refs):
    outs, halves, (buf, sem, out_sem) = refs[: 3 + RP], refs[3 + RP : 6 + 2 * RP], refs[6 + 2 * RP :]
    pieces = 6
    step = T // pieces

    def copy(c):
        rows = pl.ds(c * step, step)
        return pltpu.make_async_copy(slab_ref.at[:, rows, :], buf.at[:, rows, :], sem.at[c])

    def copies_out(c):
        rows = pl.ds(c * step, step)
        made = [
            pltpu.make_async_copy(halves[k].at[:, rows, :], outs[k].at[:, rows, :], out_sem.at[c, k])
            for k in range(3)
            if (c + 1) * step <= W
        ]
        k, row = 3 + c * step // (T // RP), c * step % (T // RP)
        rows = pl.ds(row, step)
        return made + [
            pltpu.make_async_copy(halves[k].at[:, rows, :], outs[k].at[:, rows, :], out_sem.at[c, 3])
        ]

    for c in range(pieces):
        copy(c).start()
    for c in range(pieces):
        copy(c).wait()
        for p in range(2):
            for row in range(c * step, (c + 1) * step, 2 * R):
                here = pl.ds(row, 2 * R)
                part = buf[p, here, :].astype(bf16)
                if row < W:
                    halves[0][p, here, :] = part[:, : 2 * Q]
                    halves[1][p, here, :] = part[:, 2 * Q : W]
                    halves[2][p, here, :] = part[:, W:]
                halves[3 + row // (T // RP)][p, pl.ds(row % (T // RP), 2 * R), :] = part[:, :W]
        for one in copies_out(c):
            one.start()
    for c in range(pieces):
        for one in copies_out(c):
            one.wait()


def pack(slab):
    shapes = [(2, W, 2 * Q)] * 3 + [(2, T // RP, W)] * RP
    return pl.pallas_call(
        pack_kernel,
        in_specs=[ANY],
        out_specs=[ANY] * (3 + RP),
        out_shape=[jax.ShapeDtypeStruct(shape, bf16) for shape in shapes],
        scratch_shapes=[pltpu.VMEM(shape, bf16) for shape in shapes]
        + [
            pltpu.VMEM((2, T, T), f32),
            pltpu.SemaphoreType.DMA((6,)),
            pltpu.SemaphoreType.DMA((6, 4)),
        ],
        cost_estimate=cost(),
        compiler_params=params(PACK_MIB),
    )(slab)


def sort_kernel(pick_ref, pick_t_ref, in_ref, *refs):
    out_ref = refs[-1]
    rows = jnp.dot(pick_ref[...], in_ref[0], preferred_element_type=f32).astype(bf16)
    out_ref[0] = jnp.dot(rows, pick_t_ref[...], preferred_element_type=f32).astype(bf16)


def sort_intensities(measured, pick, *later):
    whole = pl.BlockSpec((W, W), lambda s: (0, 0))
    each = pl.BlockSpec((1, W, W), lambda s: (s, 0, 0))
    return pl.pallas_call(
        sort_kernel,
        grid=(measured.shape[0],),
        in_specs=[whole, whole, each] + [VMEM] * len(later),
        out_specs=each,
        out_shape=jax.ShapeDtypeStruct(measured.shape, bf16),
        cost_estimate=pl.CostEstimate(
            flops=24 * W**3, bytes_accessed=24 * W * W, transcendentals=0
        ),
        compiler_params=params(16),
    )(jnp.asarray(pick), jnp.asarray(pick.T.copy()), measured, *later)


def slots_kernel(
    live_ref,
    meta_ref,
    slab_ref,
    near0_ref,
    near1_ref,
    far_ref,
    corner0_ref,
    corner1_ref,
    probe_ref,
    meas_ref,
    ga_ref,
    gb_ref,
    *refs,
):
    right_refs, refs = refs[:RP], refs[RP:]
    grown, ext, half16, full32, mid, out, sem = refs

    def copy(p, b):
        return pltpu.make_async_copy(
            slab_ref.at[p, :, lanes(b)], ext.at[p, b, pl.ds(0, T), :], sem.at[p, b]
        )

    for p in range(2):
        for b in range(TB):
            copy(p, b).start()

    def clear(row):
        for p in range(2):
            for b in range(NB):
                grown[p, b, pl.ds(row, R), :] = jnp.zeros((R, Q), f32)

    def fill_right(row):
        rows = pl.ds(row, R)
        here = pl.ds(pl.multiple_of(piece * (T // RP) + row, R), R)
        for p in range(2):
            for b in range(4):
                ext[p, TB + b, here, :] = right_refs[piece][p, rows, lanes(b)].astype(f32)

    def fill_below(row):
        rows = pl.ds(row, R)
        there = pl.ds(pl.multiple_of(T + row, R), R)
        for p in range(2):
            for b in range(2):
                ext[p, b, there, :] = near0_ref[p, rows, lanes(b)].astype(f32)
                ext[p, 2 + b, there, :] = near1_ref[p, rows, lanes(b)].astype(f32)
                ext[p, 4 + b, there, :] = far_ref[p, rows, lanes(b)].astype(f32)
                ext[p, TB + b, there, :] = corner0_ref[p, rows, lanes(b)].astype(f32)
                ext[p, TB + 2 + b, there, :] = corner1_ref[p, rows, lanes(b)].astype(f32)

    each_rows(E, clear)
    for piece in range(RP):
        each_rows(T // RP, fill_right)
    each_rows(W, fill_below)
    for p in range(2):
        for b in range(TB):
            copy(p, b).wait()

    lane = lax.broadcasted_iota(jnp.int32, (R, Q), 1)

    def one_slot(slot, carry):
        row0 = meta_ref[0, slot]
        col0 = meta_ref[1, slot]
        block0 = col0 // Q
        by = col0 % Q
        inner = lane < Q - by
        outer = lane < by

        def cut(i, c):
            def rolled(q, p, b):
                rows = pl.ds(row0 + q * Q + i * R, R)
                return pltpu.roll(ext[p, block0 + b, rows, :], Q - by, 1)

            last = [[rolled(q, p, 0) for p in range(2)] for q in range(4)]
            for b in range(4):
                re, im = [], []
                for q in range(4):
                    here = pl.ds(pl.multiple_of(q * Q + i * R, R), R)
                    part = []
                    for p in range(2):
                        after = rolled(q, p, b + 1)
                        part.append(jnp.where(inner, last[q][p], after))
                        last[q][p] = after
                    pr, pi = probe_ref[0, here, lanes(b)], probe_ref[1, here, lanes(b)]
                    re.append(pr * part[0] - pi * part[1])
                    im.append(pr * part[1] + pi * part[0])
                re, im = split4(re, im)
                top = pl.ds(pl.multiple_of(i * R, R), R)
                low = pl.ds(pl.multiple_of(Q + i * R, R), R)
                for j in range(4):
                    half16[j, top, lanes(b)] = re[j].astype(bf16)
                    half16[j, low, lanes(b)] = im[j].astype(bf16)
            return c

        lax.fori_loop(0, Q // R, cut, 0, unroll=4)
        for j in range(4):
            full32[j] = jnp.dot(ga_ref[j], half16[j], preferred_element_type=f32)
            for i in range(Q // R):
                top, low = pl.ds(i * R, R), pl.ds(Q + i * R, R)
                re = [full32[j, top, lanes(q)] for q in range(4)]
                im = [full32[j, low, lanes(q)] for q in range(4)]
                re, im = split4(re, im)
                there = pl.ds(j * Q + i * R, R)
                for l in range(4):
                    mid[l, there, lanes(0)] = re[l].astype(bf16)
                    mid[l, there, lanes(1)] = im[l].astype(bf16)

        def finish(l, far):
            re, im = far[:, :Q], far[:, Q:]
            gap = re * re + im * im - meas_ref[slot, :, lanes(l)].astype(f32)
            misfit = jnp.concatenate([gap * re, gap * im], axis=1).astype(bf16)
            out[l] = jnp.dot(misfit, ga_ref[l], preferred_element_type=f32)

        fars = []
        for l in range(4):
            fars.append(jnp.dot(mid[l], gb_ref[l], preferred_element_type=f32))
            if l:
                finish(l - 1, fars[l - 1])
        finish(3, fars[3])

        for j in range(4):
            for i in range(Q // R):
                top, low = pl.ds(i * R, R), pl.ds(Q + i * R, R)
                here = pl.ds(j * Q + i * R, R)
                re = [out[l, here, lanes(0)] for l in range(4)]
                im = [out[l, here, lanes(1)] for l in range(4)]
                re, im = join4(re, im)
                for q in range(4):
                    half16[j, top, lanes(q)] = re[q].astype(bf16)
                    half16[j, low, lanes(q)] = im[q].astype(bf16)
            full32[j] = jnp.dot(gb_ref[j], half16[j], preferred_element_type=f32)

        def add(i, c):
            top = pl.ds(pl.multiple_of(i * R, R), R)
            low = pl.ds(pl.multiple_of(Q + i * R, R), R)
            last = [[None, None] for q in range(4)]
            for b in range(5):
                if b < 4:
                    re = [full32[j, top, lanes(b)] for j in range(4)]
                    im = [full32[j, low, lanes(b)] for j in range(4)]
                    re, im = join4(re, im)
                for q in range(4):
                    rows = pl.ds(row0 + q * Q + i * R, R)
                    here = pl.ds(pl.multiple_of(q * Q + i * R, R), R)
                    if b < 4:
                        pr, pi = probe_ref[0, here, lanes(b)], probe_ref[1, here, lanes(b)]
                        both = (pr * re[q] + pi * im[q], pr * im[q] - pi * re[q])
                        both = [pltpu.roll(v, by, 1) for v in both]
                    else:
                        both = [jnp.zeros((R, Q), f32)] * 2
                    for p in range(2):
                        before = last[q][p]
                        if before is None:
                            before = jnp.zeros((R, Q), f32)
                        grown[p, block0 + b, rows, :] += jnp.where(outer, before, both[p])
                        last[q][p] = both[p]
            return c

        lax.fori_loop(0, Q // R, add, 0, unroll=4)
        return carry

    lax.fori_loop(0, live_ref[0], one_slot, 0)


def solve(live, meta, slab, right, below, corner, probe, measured, left, left_t):
    return pl.pallas_call(
        slots_kernel,
        in_specs=[SMEM, SMEM, ANY] + [VMEM] * (9 + RP),
        out_specs=VMEM,
        out_shape=TILES,
        scratch_shapes=[
            pltpu.VMEM((2, NB, E, Q), f32),
            pltpu.VMEM((4, 2 * Q, W), bf16),
            pltpu.VMEM((4, 2 * Q, W), f32),
            pltpu.VMEM((4, W, 2 * Q), bf16),
            pltpu.VMEM((4, W, 2 * Q), f32),
            pltpu.SemaphoreType.DMA((2, TB)),
        ],
        cost_estimate=cost(),
        compiler_params=params(SOLVE_MIB),
    )(live, meta, slab, *below, *corner, probe, measured, left, left_t, *right)


def drain_kernel(grown, near0_ref, near1_ref, far_ref, corner0_ref, corner1_ref, *right_refs):
    def below(row):
        rows = pl.ds(row, R)
        here = pl.ds(pl.multiple_of(T + row, R), R)
        for p in range(2):
            for b in range(2):
                near0_ref[p, rows, lanes(b)] = grown[p, b, here, :].astype(bf16)
                near1_ref[p, rows, lanes(b)] = grown[p, 2 + b, here, :].astype(bf16)
                far_ref[p, rows, lanes(b)] = grown[p, 4 + b, here, :].astype(bf16)
                corner0_ref[p, rows, lanes(b)] = grown[p, TB + b, here, :].astype(bf16)
                corner1_ref[p, rows, lanes(b)] = grown[p, TB + 2 + b, here, :].astype(bf16)

    def right(row):
        rows = pl.ds(row, R)
        here = pl.ds(pl.multiple_of(piece * (T // RP) + row, R), R)
        for p in range(2):
            for b in range(4):
                right_refs[piece][p, rows, lanes(b)] = grown[p, TB + b, here, :].astype(bf16)

    each_rows(W, below)
    for piece in range(RP):
        each_rows(T // RP, right)


def drain(grown):
    return pl.pallas_call(
        drain_kernel,
        in_specs=[VMEM],
        out_specs=[VMEM] * (5 + RP),
        out_shape=[jax.ShapeDtypeStruct((2, W, 2 * Q), bf16)] * 5
        + [jax.ShapeDtypeStruct((2, T // RP, W), bf16)] * RP,
        cost_estimate=cost(),
        compiler_params=params(4),
    )(grown)


def write_copy(tile, whole_ref, sem, p, b, first, count):
    rows = pl.ds(first, count)
    return pltpu.make_async_copy(
        tile.at[p, b, rows, :], whole_ref.at[p, rows, lanes(b)], sem.at[p, b]
    )


def side_kernel(*refs):
    right_refs, (far_ref, near1_ref, grown_in, grown, whole_ref, sem) = refs[:RP], refs[RP:]

    def done(p, b):
        if b < 2:
            return write_copy(grown, whole_ref, sem, p, b, W, T - W)
        return write_copy(grown, whole_ref, sem, p, b, 0, T)

    for part, first in ((far_ref, 4), (near1_ref, 2)):

        def below(row):
            rows = pl.ds(row, R)
            for p in range(2):
                for b in range(2):
                    grown[p, first + b, rows, :] += part[p, rows, lanes(b)].astype(f32)

        each_rows(W, below)
        if first == 4:
            for p in range(2):
                for b in range(4, TB):
                    done(p, b).start()

    def right(row):
        rows = pl.ds(row, R)
        here = pl.ds(pl.multiple_of(piece * (T // RP) + row, R), R)
        for p in range(2):
            for b in range(4):
                grown[p, b, here, :] += right_refs[piece][p, rows, lanes(b)].astype(f32)

    for piece in range(RP):
        each_rows(T // RP, right)
    for p in range(2):
        for b in range(4):
            done(p, b).start()
    for p in range(2):
        for b in range(TB):
            done(p, b).wait()


def add_side(right, far, near1, grown):
    return pl.pallas_call(
        side_kernel,
        in_specs=[VMEM] * (3 + RP),
        out_specs=[VMEM, ANY],
        out_shape=[TILES, jax.ShapeDtypeStruct((2, T, T), f32)],
        input_output_aliases={2 + RP: 0},
        scratch_shapes=[pltpu.SemaphoreType.DMA((2, TB))],
        cost_estimate=cost(),
        compiler_params=params(4),
    )(*right, far, near1, grown)


def last_kernel(near_ref, grown_in, whole_in, grown, whole_ref, sem):
    for half in range(2):
        for b in range(2):
            for p in range(2):
                for row in range(half * W // 2, (half + 1) * W // 2, 2 * R):
                    rows = pl.ds(row, 2 * R)
                    grown[p, b, rows, :] += near_ref[p, rows, lanes(b)].astype(f32)
                write_copy(grown, whole_ref, sem.at[half], p, b, half * W // 2, W // 2).start()
    for half in range(2):
        for b in range(2):
            for p in range(2):
                write_copy(grown, whole_ref, sem.at[half], p, b, half * W // 2, W // 2).wait()


def add_near(near, grown, whole):
    return pl.pallas_call(
        last_kernel,
        in_specs=[VMEM, VMEM, ANY],
        out_specs=[VMEM, ANY],
        out_shape=[TILES, jax.ShapeDtypeStruct((2, T, T), f32)],
        input_output_aliases={1: 0, 2: 1},
        scratch_shapes=[pltpu.SemaphoreType.DMA((2, 2, 2))],
        cost_estimate=cost(),
        compiler_params=params(4),
    )(near, grown, whole)[1]


def shards(slab, probe, intensities, offsets, live_count):
    left, left_t, pick = tables()
    left, left_t = jnp.asarray(left), jnp.asarray(left_t)
    near0, near1, far, *right = pack(slab)
    near0 = shifted(near0, "tile", -1)
    near1 = shifted(near1, "tile", -1)
    far = shifted(far, "tile", -1)
    right = [shifted(piece, "scan", -1) for piece in right]
    live = lax.dynamic_slice(live_count[:, 0], (lax.axis_index("scan"),), (1,))
    shifts = offsets[0, 0].T
    near0, live, shifts, intensities = lax.optimization_barrier(
        (near0, live, shifts, intensities)
    )
    measured = sort_intensities(intensities[0, 0], pick, probe, left, left_t)
    near1, measured = lax.optimization_barrier((near1, measured))
    corner0 = shifted(near0, "scan", -1)
    corner1 = shifted(near1, "scan", -1)
    grown = solve(
        live, shifts, slab, right, (near0, near1, far), (corner0, corner1), probe, measured,
        left, left_t,
    )
    near0, near1, far, corner0, corner1, *right = drain(grown)
    corner1 = shifted(corner1, "scan", 1)
    far = shifted(far, "tile", 1)
    corner0 = shifted(corner0, "scan", 1)
    near1 = (near1.astype(f32) + corner1.astype(f32)).astype(bf16)
    near1, right[1] = lax.optimization_barrier((near1, right[1]))
    near0 = (near0.astype(f32) + corner0.astype(f32)).astype(bf16)
    near1 = shifted(near1, "tile", 1)
    right = [shifted(piece, "scan", 1) for piece in right]
    near0, far = lax.optimization_barrier((near0, far))
    near0 = shifted(near0, "tile", 1)
    grown, whole = add_side(right, far, near1, grown)
    return add_near(near0, grown, whole)


def solution(mesh):
    placed = (
        P(None, "tile", "scan"),
        P(),
        P("scan", "tile", None, None, None),
        P("scan", "tile", None, None),
        P(None, "tile"),
    )
    return jax.shard_map(
        shards, mesh=mesh, in_specs=placed, out_specs=P(None, "tile", "scan"), check_vma=False
    )
```

```python
import functools

import jax
import jax.numpy as jnp
import ml_dtypes
import numpy as np
from jax import lax
from jax.experimental import pallas as pl
from jax.experimental.pallas import tpu as pltpu
from jax.sharding import PartitionSpec as P

W = 512
Q = W // 4
T = 768
E = T + W
NB = E // Q
TB = T // Q
F = T - W
SOLVE_MIB = 24
RP = 2
PACK_MIB = 52
R = 16
f32, bf16 = jnp.float32, jnp.bfloat16


def shifted(value, axis, by):
    n = lax.axis_size(axis)
    return lax.ppermute(value, axis, [(i, i + by) for i in range(n) if 0 <= i + by < n])


def tables():
    k = np.arange(W, dtype=np.int64)
    phase = (k[:, None] * k[None, :] % W).astype(np.float64) * (2.0 * np.pi / W)
    factor = 1.0 / np.sqrt(W)
    re = (np.cos(phase) * factor).astype(np.float32)[:, :Q]
    im = (-np.sin(phase) * factor).astype(np.float32)[:, :Q]
    left = np.stack(
        [
            np.block([[re[j::4], -im[j::4]], [im[j::4], re[j::4]]])
            for j in range(4)
        ]
    ).astype(ml_dtypes.bfloat16)
    pick = np.zeros((W, W), np.float32)
    for j in range(4):
        pick[j * Q + np.arange(Q), 4 * np.arange(Q) + j] = 1.0
    return left, left.transpose(0, 2, 1).copy(), pick.astype(ml_dtypes.bfloat16)


def split4(re, im):
    t0r, t0i, t1r, t1i = re[0] + re[2], im[0] + im[2], re[0] - re[2], im[0] - im[2]
    t2r, t2i, t3r, t3i = re[1] + re[3], im[1] + im[3], re[1] - re[3], im[1] - im[3]
    return (
        (t0r + t2r, t1r + t3i, t0r - t2r, t1r - t3i),
        (t0i + t2i, t1i - t3r, t0i - t2i, t1i + t3r),
    )


def join4(re, im):
    s0r, s0i, s1r, s1i = re[0] + re[2], im[0] + im[2], re[0] - re[2], im[0] - im[2]
    s2r, s2i, s3r, s3i = re[1] + re[3], im[1] + im[3], re[1] - re[3], im[1] - im[3]
    return (
        (s0r + s2r, s1r - s3i, s0r - s2r, s1r + s3i),
        (s0i + s2i, s1i + s3r, s0i - s2i, s1i - s3r),
    )


def lanes(b):
    return pl.ds(b * Q, Q)


def each_rows(count, body):
    def step(i, carry):
        body(pl.multiple_of(i * R, R))
        return carry

    lax.fori_loop(0, count // R, step, 0, unroll=4)


VMEM = pl.BlockSpec(memory_space=pltpu.VMEM)
SMEM = pl.BlockSpec(memory_space=pltpu.SMEM)
ANY = pl.BlockSpec(memory_space=pl.ANY)
TILES = jax.ShapeDtypeStruct((2, NB, E, Q), f32)


def params(mib):
    return pltpu.CompilerParams(vmem_limit_bytes=mib * 2**20)


def cost():
    return pl.CostEstimate(flops=1024, bytes_accessed=1024, transcendentals=0)


def pack_kernel(slab_ref, *refs):
    outs, halves, (buf, sem, out_sem) = refs[: 3 + RP], refs[3 + RP : 6 + 2 * RP], refs[6 + 2 * RP :]
    pieces = 6
    step = T // pieces

    def copy(c):
        rows = pl.ds(c * step, step)
        return pltpu.make_async_copy(slab_ref.at[:, rows, :], buf.at[:, rows, :], sem.at[c])

    def copies_out(c):
        rows = pl.ds(c * step, step)
        made = [
            pltpu.make_async_copy(halves[k].at[:, rows, :], outs[k].at[:, rows, :], out_sem.at[c, k])
            for k in range(3)
            if (c + 1) * step <= W
        ]
        k, row = 3 + c * step // (T // RP), c * step % (T // RP)
        rows = pl.ds(row, step)
        return made + [
            pltpu.make_async_copy(halves[k].at[:, rows, :], outs[k].at[:, rows, :], out_sem.at[c, 3])
        ]

    for c in range(pieces):
        copy(c).start()
    for c in range(pieces):
        copy(c).wait()
        for p in range(2):
            for row in range(c * step, (c + 1) * step, 2 * R):
                here = pl.ds(row, 2 * R)
                part = buf[p, here, :].astype(bf16)
                if row < W:
                    halves[0][p, here, :] = part[:, : 2 * Q]
                    halves[1][p, here, :] = part[:, 2 * Q : W]
                    halves[2][p, here, :] = part[:, W:]
                halves[3 + row // (T // RP)][p, pl.ds(row % (T // RP), 2 * R), :] = part[:, :W]
        for one in copies_out(c):
            one.start()
    for c in range(pieces):
        for one in copies_out(c):
            one.wait()


def pack(slab):
    shapes = [(2, W, 2 * Q)] * 3 + [(2, T // RP, W)] * RP
    return pl.pallas_call(
        pack_kernel,
        in_specs=[ANY],
        out_specs=[ANY] * (3 + RP),
        out_shape=[jax.ShapeDtypeStruct(shape, bf16) for shape in shapes],
        scratch_shapes=[pltpu.VMEM(shape, bf16) for shape in shapes]
        + [
            pltpu.VMEM((2, T, T), f32),
            pltpu.SemaphoreType.DMA((6,)),
            pltpu.SemaphoreType.DMA((6, 4)),
        ],
        cost_estimate=cost(),
        compiler_params=params(PACK_MIB),
    )(slab)


def sort_kernel(pick_ref, pick_t_ref, in_ref, *refs):
    out_ref = refs[-1]
    rows = jnp.dot(pick_ref[...], in_ref[0], preferred_element_type=f32).astype(bf16)
    out_ref[0] = jnp.dot(rows, pick_t_ref[...], preferred_element_type=f32).astype(bf16)


def sort_intensities(measured, pick, *later):
    whole = pl.BlockSpec((W, W), lambda s: (0, 0))
    each = pl.BlockSpec((1, W, W), lambda s: (s, 0, 0))
    return pl.pallas_call(
        sort_kernel,
        grid=(measured.shape[0],),
        in_specs=[whole, whole, each] + [VMEM] * len(later),
        out_specs=each,
        out_shape=jax.ShapeDtypeStruct(measured.shape, bf16),
        cost_estimate=pl.CostEstimate(
            flops=24 * W**3, bytes_accessed=24 * W * W, transcendentals=0
        ),
        compiler_params=params(16),
    )(jnp.asarray(pick), jnp.asarray(pick.T.copy()), measured, *later)


def slots_kernel(
    live_ref,
    meta_ref,
    slab_ref,
    near0_ref,
    near1_ref,
    far_ref,
    corner0_ref,
    corner1_ref,
    probe_ref,
    meas_ref,
    ga_ref,
    gb_ref,
    *refs,
):
    right_refs, refs = refs[:RP], refs[RP:]
    grown, ext, half16, full32, mid, out, sem = refs

    def copy(p, b):
        return pltpu.make_async_copy(
            slab_ref.at[p, :, lanes(b)], ext.at[p, b, pl.ds(0, T), :], sem.at[p, b]
        )

    for p in range(2):
        for b in range(TB):
            copy(p, b).start()

    def clear(row):
        for p in range(2):
            for b in range(NB):
                grown[p, b, pl.ds(row, R), :] = jnp.zeros((R, Q), f32)

    def fill_right(row):
        rows = pl.ds(row, R)
        here = pl.ds(pl.multiple_of(piece * (T // RP) + row, R), R)
        for p in range(2):
            for b in range(4):
                ext[p, TB + b, here, :] = right_refs[piece][p, rows, lanes(b)].astype(f32)

    def fill_below(row):
        rows = pl.ds(row, R)
        there = pl.ds(pl.multiple_of(T + row, R), R)
        for p in range(2):
            for b in range(2):
                ext[p, b, there, :] = near0_ref[p, rows, lanes(b)].astype(f32)
                ext[p, 2 + b, there, :] = near1_ref[p, rows, lanes(b)].astype(f32)
                ext[p, 4 + b, there, :] = far_ref[p, rows, lanes(b)].astype(f32)
                ext[p, TB + b, there, :] = corner0_ref[p, rows, lanes(b)].astype(f32)
                ext[p, TB + 2 + b, there, :] = corner1_ref[p, rows, lanes(b)].astype(f32)

    each_rows(E, clear)
    for piece in range(RP):
        each_rows(T // RP, fill_right)
    each_rows(W, fill_below)
    for p in range(2):
        for b in range(TB):
            copy(p, b).wait()

    lane = lax.broadcasted_iota(jnp.int32, (R, Q), 1)

    def one_slot(slot, carry):
        row0 = meta_ref[0, slot]
        col0 = meta_ref[1, slot]
        block0 = col0 // Q
        by = col0 % Q
        inner = lane < Q - by
        outer = lane < by

        def cut(i, c):
            def rolled(q, p, b):
                rows = pl.ds(row0 + q * Q + i * R, R)
                return pltpu.roll(ext[p, block0 + b, rows, :], Q - by, 1)

            last = [[rolled(q, p, 0) for p in range(2)] for q in range(4)]
            for b in range(4):
                re, im = [], []
                for q in range(4):
                    here = pl.ds(pl.multiple_of(q * Q + i * R, R), R)
                    part = []
                    for p in range(2):
                        after = rolled(q, p, b + 1)
                        part.append(jnp.where(inner, last[q][p], after))
                        last[q][p] = after
                    pr, pi = probe_ref[0, here, lanes(b)], probe_ref[1, here, lanes(b)]
                    re.append(pr * part[0] - pi * part[1])
                    im.append(pr * part[1] + pi * part[0])
                re, im = split4(re, im)
                top = pl.ds(pl.multiple_of(i * R, R), R)
                low = pl.ds(pl.multiple_of(Q + i * R, R), R)
                for j in range(4):
                    half16[j, top, lanes(b)] = re[j].astype(bf16)
                    half16[j, low, lanes(b)] = im[j].astype(bf16)
            return c

        lax.fori_loop(0, Q // R, cut, 0, unroll=4)
        for j in range(4):
            full32[j] = jnp.dot(ga_ref[j], half16[j], preferred_element_type=f32)
            for i in range(Q // R):
                top, low = pl.ds(i * R, R), pl.ds(Q + i * R, R)
                re = [full32[j, top, lanes(q)] for q in range(4)]
                im = [full32[j, low, lanes(q)] for q in range(4)]
                re, im = split4(re, im)
                there = pl.ds(j * Q + i * R, R)
                for l in range(4):
                    mid[l, there, lanes(0)] = re[l].astype(bf16)
                    mid[l, there, lanes(1)] = im[l].astype(bf16)

        def finish(l, far):
            re, im = far[:, :Q], far[:, Q:]
            gap = re * re + im * im - meas_ref[slot, :, lanes(l)].astype(f32)
            misfit = jnp.concatenate([gap * re, gap * im], axis=1).astype(bf16)
            out[l] = jnp.dot(misfit, ga_ref[l], preferred_element_type=f32)

        fars = []
        for l in range(4):
            fars.append(jnp.dot(mid[l], gb_ref[l], preferred_element_type=f32))
            if l:
                finish(l - 1, fars[l - 1])
        finish(3, fars[3])

        for j in range(4):
            for i in range(Q // R):
                top, low = pl.ds(i * R, R), pl.ds(Q + i * R, R)
                here = pl.ds(j * Q + i * R, R)
                re = [out[l, here, lanes(0)] for l in range(4)]
                im = [out[l, here, lanes(1)] for l in range(4)]
                re, im = join4(re, im)
                for q in range(4):
                    half16[j, top, lanes(q)] = re[q].astype(bf16)
                    half16[j, low, lanes(q)] = im[q].astype(bf16)
            full32[j] = jnp.dot(gb_ref[j], half16[j], preferred_element_type=f32)

        def add(i, c):
            top = pl.ds(pl.multiple_of(i * R, R), R)
            low = pl.ds(pl.multiple_of(Q + i * R, R), R)
            last = [[None, None] for q in range(4)]
            for b in range(5):
                if b < 4:
                    re = [full32[j, top, lanes(b)] for j in range(4)]
                    im = [full32[j, low, lanes(b)] for j in range(4)]
                    re, im = join4(re, im)
                for q in range(4):
                    rows = pl.ds(row0 + q * Q + i * R, R)
                    here = pl.ds(pl.multiple_of(q * Q + i * R, R), R)
                    if b < 4:
                        pr, pi = probe_ref[0, here, lanes(b)], probe_ref[1, here, lanes(b)]
                        both = (pr * re[q] + pi * im[q], pr * im[q] - pi * re[q])
                        both = [pltpu.roll(v, by, 1) for v in both]
                    else:
                        both = [jnp.zeros((R, Q), f32)] * 2
                    for p in range(2):
                        before = last[q][p]
                        if before is None:
                            before = jnp.zeros((R, Q), f32)
                        grown[p, block0 + b, rows, :] += jnp.where(outer, before, both[p])
                        last[q][p] = both[p]
            return c

        lax.fori_loop(0, Q // R, add, 0, unroll=4)
        return carry

    lax.fori_loop(0, live_ref[0], one_slot, 0)


def solve(live, meta, slab, right, below, corner, probe, measured, left, left_t):
    return pl.pallas_call(
        slots_kernel,
        in_specs=[SMEM, SMEM, ANY] + [VMEM] * (9 + RP),
        out_specs=VMEM,
        out_shape=TILES,
        scratch_shapes=[
            pltpu.VMEM((2, NB, E, Q), f32),
            pltpu.VMEM((4, 2 * Q, W), bf16),
            pltpu.VMEM((4, 2 * Q, W), f32),
            pltpu.VMEM((4, W, 2 * Q), bf16),
            pltpu.VMEM((4, W, 2 * Q), f32),
            pltpu.SemaphoreType.DMA((2, TB)),
        ],
        cost_estimate=cost(),
        compiler_params=params(SOLVE_MIB),
    )(live, meta, slab, *below, *corner, probe, measured, left, left_t, *right)


def drain_kernel(grown, near0_ref, near1_ref, far_ref, corner0_ref, corner1_ref, *right_refs):
    def below(row):
        rows = pl.ds(row, R)
        here = pl.ds(pl.multiple_of(T + row, R), R)
        for p in range(2):
            for b in range(2):
                near0_ref[p, rows, lanes(b)] = grown[p, b, here, :].astype(bf16)
                near1_ref[p, rows, lanes(b)] = grown[p, 2 + b, here, :].astype(bf16)
                far_ref[p, rows, lanes(b)] = grown[p, 4 + b, here, :].astype(bf16)
                corner0_ref[p, rows, lanes(b)] = grown[p, TB + b, here, :].astype(bf16)
                corner1_ref[p, rows, lanes(b)] = grown[p, TB + 2 + b, here, :].astype(bf16)

    def right(row):
        rows = pl.ds(row, R)
        here = pl.ds(pl.multiple_of(piece * (T // RP) + row, R), R)
        for p in range(2):
            for b in range(4):
                right_refs[piece][p, rows, lanes(b)] = grown[p, TB + b, here, :].astype(bf16)

    each_rows(W, below)
    for piece in range(RP):
        each_rows(T // RP, right)


def drain(grown):
    return pl.pallas_call(
        drain_kernel,
        in_specs=[VMEM],
        out_specs=[VMEM] * (5 + RP),
        out_shape=[jax.ShapeDtypeStruct((2, W, 2 * Q), bf16)] * 5
        + [jax.ShapeDtypeStruct((2, T // RP, W), bf16)] * RP,
        cost_estimate=cost(),
        compiler_params=params(4),
    )(grown)


def write_copy(tile, whole_ref, sem, p, b, first, count):
    rows = pl.ds(first, count)
    return pltpu.make_async_copy(
        tile.at[p, b, rows, :], whole_ref.at[p, rows, lanes(b)], sem.at[p, b]
    )


def side_kernel(*refs):
    right_refs, (far_ref, near1_ref, grown_in, grown, whole_ref, sem) = refs[:RP], refs[RP:]

    def done(p, b):
        if b < 2:
            return write_copy(grown, whole_ref, sem, p, b, W, T - W)
        return write_copy(grown, whole_ref, sem, p, b, 0, T)

    for part, first in ((far_ref, 4), (near1_ref, 2)):

        def below(row):
            rows = pl.ds(row, R)
            for p in range(2):
                for b in range(2):
                    grown[p, first + b, rows, :] += part[p, rows, lanes(b)].astype(f32)

        each_rows(W, below)
        if first == 4:
            for p in range(2):
                for b in range(4, TB):
                    done(p, b).start()

    def right(row):
        rows = pl.ds(row, R)
        here = pl.ds(pl.multiple_of(piece * (T // RP) + row, R), R)
        for p in range(2):
            for b in range(4):
                grown[p, b, here, :] += right_refs[piece][p, rows, lanes(b)].astype(f32)

    for piece in range(RP):
        each_rows(T // RP, right)
    for p in range(2):
        for b in range(4):
            done(p, b).start()
    for p in range(2):
        for b in range(TB):
            done(p, b).wait()


def add_side(right, far, near1, grown):
    return pl.pallas_call(
        side_kernel,
        in_specs=[VMEM] * (3 + RP),
        out_specs=[VMEM, ANY],
        out_shape=[TILES, jax.ShapeDtypeStruct((2, T, T), f32)],
        input_output_aliases={2 + RP: 0},
        scratch_shapes=[pltpu.SemaphoreType.DMA((2, TB))],
        cost_estimate=cost(),
        compiler_params=params(4),
    )(*right, far, near1, grown)


def last_kernel(near_ref, grown_in, whole_in, grown, whole_ref, sem):
    for half in range(2):
        for b in range(2):
            for p in range(2):
                for row in range(half * W // 2, (half + 1) * W // 2, 2 * R):
                    rows = pl.ds(row, 2 * R)
                    grown[p, b, rows, :] += near_ref[p, rows, lanes(b)].astype(f32)
                write_copy(grown, whole_ref, sem.at[half], p, b, half * W // 2, W // 2).start()
    for half in range(2):
        for b in range(2):
            for p in range(2):
                write_copy(grown, whole_ref, sem.at[half], p, b, half * W // 2, W // 2).wait()


def add_near(near, grown, whole):
    return pl.pallas_call(
        last_kernel,
        in_specs=[VMEM, VMEM, ANY],
        out_specs=[VMEM, ANY],
        out_shape=[TILES, jax.ShapeDtypeStruct((2, T, T), f32)],
        input_output_aliases={1: 0, 2: 1},
        scratch_shapes=[pltpu.SemaphoreType.DMA((2, 2, 2))],
        cost_estimate=cost(),
        compiler_params=params(4),
    )(near, grown, whole)[1]


def shards(slab, probe, intensities, offsets, live_count):
    left, left_t, pick = tables()
    left, left_t = jnp.asarray(left), jnp.asarray(left_t)
    near0, near1, far, *right = pack(slab)
    near0 = shifted(near0, "tile", -1)
    near1 = shifted(near1, "tile", -1)
    far = shifted(far, "tile", -1)
    right = [shifted(piece, "scan", -1) for piece in right]
    live = lax.dynamic_slice(live_count[:, 0], (lax.axis_index("scan"),), (1,))
    shifts = offsets[0, 0].T
    near0, live, shifts, intensities = lax.optimization_barrier(
        (near0, live, shifts, intensities)
    )
    measured = sort_intensities(intensities[0, 0], pick, probe, left, left_t)
    near1, measured = lax.optimization_barrier((near1, measured))
    corner0 = shifted(near0, "scan", -1)
    corner1 = shifted(near1, "scan", -1)
    grown = solve(
        live, shifts, slab, right, (near0, near1, far), (corner0, corner1), probe, measured,
        left, left_t,
    )
    near0, near1, far, corner0, corner1, *right = drain(grown)
    corner1 = shifted(corner1, "scan", 1)
    far = shifted(far, "tile", 1)
    corner0 = shifted(corner0, "scan", 1)
    near1 = (near1.astype(f32) + corner1.astype(f32)).astype(bf16)
    near1, right[1] = lax.optimization_barrier((near1, right[1]))
    near1 = shifted(near1, "tile", 1)
    right = [shifted(piece, "scan", 1) for piece in right]
    far, near0 = lax.optimization_barrier((far, near0))
    near0 = (near0.astype(f32) + corner0.astype(f32)).astype(bf16)
    near0 = shifted(near0, "tile", 1)
    grown, whole = add_side(right, far, near1, grown)
    return add_near(near0, grown, whole)


def solution(mesh):
    placed = (
        P(None, "tile", "scan"),
        P(),
        P("scan", "tile", None, None, None),
        P("scan", "tile", None, None),
        P(None, "tile"),
    )
    return jax.shard_map(
        shards, mesh=mesh, in_specs=placed, out_specs=P(None, "tile", "scan"), check_vma=False
    )
```
